32 devices in a mesh: dp: 16 (over z, x, core), seq: 2 (over y).
Axes of the slice: x: 2, y: 2, z: 4, core: 2. Of those that a mesh axis runs over, the one named last changes fastest.
Arguments:
- image_tokens: bfloat16 [16, 1024, 384], P('dp', 'seq'), may hold values from -6 to 6
- kept_index: int32 [16, 704], P('dp'), may hold values from 0 to 1023, as said below
- kept_count: int32 [16], P('dp'), may hold values from 616 to 704, as said below
- sample_valid: int32 [16], P('dp'), may hold values 0 or 1
- timestep: int32 [16], P('dp'), may hold values from 0 to 999
- class_label: int32 [16], P('dp'), may hold values from 0 to 999
- class_table: bfloat16 [1000, 384], replicated, may hold values from -6 to 6
- ada_weight: bfloat16 [384, 2304], replicated, may hold values from -0.3125 to 0.3125
- ada_bias: bfloat16 [2304], replicated, may hold values from -3 to 3
- qkv_weight: bfloat16 [384, 1152], replicated, may hold values from -0.3125 to 0.3125
- qv_bias: bfloat16 [2, 384], replicated, may hold values from -3 to 3
- rel_bias: bfloat16 [2, 6, 63], replicated, may hold values from -4 to 4
- out_weight: bfloat16 [384, 384], replicated, may hold values from -0.875 to 0.875
- out_bias: bfloat16 [384], replicated, may hold values from -2 to 2
- fc1_weight: bfloat16 [384, 1536], replicated, may hold values from -0.3125 to 0.3125
- fc1_bias: bfloat16 [1536], replicated, may hold values from -3 to 3
- fc2_weight: bfloat16 [1536, 384], replicated, may hold values from -0.15625 to 0.15625
- fc2_bias: bfloat16 [384], replicated, may hold values from -2 to 2
- grad_full: bfloat16 [16, 1024, 384], P('dp', 'seq'), may hold values from -6 to 6
- grad_masked: bfloat16 [16, 704, 384], P('dp', 'seq'), may hold values from -6 to 6
Outputs:
- out_full: bfloat16 [16, 1024, 384], P('dp', 'seq')
- out_masked: bfloat16 [16, 704, 384], P('dp', 'seq')
- grad_input: float32 [16, 1024, 384], P('dp', 'seq')
- grad_class_table: float32 [1000, 384], replicated
- grad_ada_weight: float32 [384, 2304], replicated
- grad_ada_bias: float32 [2304], replicated
- grad_qkv_weight: float32 [384, 1152], replicated
- grad_qv_bias: float32 [2, 384], replicated
- grad_rel_bias: float32 [2, 6, 63], replicated
- grad_out_weight: float32 [384, 384], replicated
- grad_out_bias: float32 [384], replicated
- grad_fc1_weight: float32 [384, 1536], replicated
- grad_fc1_bias: float32 [1536], replicated
- grad_fc2_weight: float32 [1536, 384], replicated
- grad_fc2_bias: float32 [384], replicated
The draws below stay inside these ranges and needn't reach their ends.
Inputs may be any that keep to these rules, and one draw needn't show every extreme that they name: `kept_index`: the first kept_count[s] slots of sample s hold distinct positions in rising order; later slots hold 0. `kept_count`: some sample has 704 kept tokens in every draw.
All inputs are finite; a program needn't handle non-finite values. No bound on the sum of `sample_valid` on one device may be relied on, other than what follows from the above.
Results may differ from the reference program's by a relative error of at most 0.015.
The reference program's roundings to bfloat16 on the way count: a program that leaves them out, or rounds other values in their place, can miss the bound.
Values may be sent and summed in bfloat16 or wider, within the bound.
No kernel may reach another device: no remote copies, remote signals or barrier semaphores. Data moves between devices by JAX's collectives and lax.ppermute only.
A program may use at most 192 MiB of HBM per device.

```python
import math
import jax
import jax.numpy as jnp
from jax import lax

D = 384
HEADS = 6
HDIM = 64
FF = 1536
NCLASS = 1000
GRID = 32
SEQ_LEN = 1024
SAMPLES = 16
KEEP = 704


def permute_one(single):
    return jax.random.permutation(single, SEQ_LEN)


def kept_layout(key):
    sample_keys = jax.random.split(key, SAMPLES)
    orders = jax.vmap(permute_one)(sample_keys)
    spare = jax.random.randint(jax.random.fold_in(key, 5), (SAMPLES,), 0, KEEP // 8 + 1)
    numbers = jnp.arange(SAMPLES, dtype=jnp.int32)
    counts = KEEP - spare
    counts = jnp.where(numbers == 0, KEEP, counts)
    counts = jnp.where(numbers == 1, KEEP - KEEP // 8, counts)
    slot_numbers = jnp.arange(KEEP, dtype=jnp.int32)
    live = slot_numbers[None, :] < counts[:, None]
    chosen = jnp.where(live, orders[:, :KEEP].astype(jnp.int32), SEQ_LEN + slot_numbers[None, :])
    chosen = jnp.sort(chosen, axis=1)
    return (jnp.where(live, chosen, 0).astype(jnp.int32), counts.astype(jnp.int32))


def draw_kept_index(key, part):
    positions, counts = kept_layout(key)
    return positions


def draw_kept_count(key, part):
    positions, counts = kept_layout(key)
    return counts


def set_ends(values, key, smallest, high):
    place = [jax.random.randint(jax.random.fold_in(key, axis), (), 0, length) for axis, length in enumerate(values.shape)]
    widest = values.shape.index(max(values.shape))
    neighbour = place[:widest] + [(place[widest] + 1) % values.shape[widest]] + place[widest + 1:]
    return values.at[tuple(place)].set(smallest).at[tuple(neighbour)].set(high)


def shard_levels(rng, dims, pieces, smallest, top_value):
    def one(axis_at, parts):
        heights = jax.random.uniform(jax.random.fold_in(jax.random.fold_in(rng, 6), axis_at), (parts,), jnp.float32, smallest / len(pieces), top_value / len(pieces))
        return jnp.repeat(jnp.exp(heights), dims[axis_at] // parts).reshape((-1,) + (1,) * (len(dims) - axis_at - 1))

    gain = one(*pieces[0])
    for cut in pieces[1:]:
        gain = gain * one(*cut)
    return gain


def scatter_about(stream_key, extent, width, reach, shards=(), kind=jnp.bfloat16):
    factor_of = shard_levels(stream_key, extent, shards, -0.22, 0.18) if shards else 1.0
    entries = jax.random.normal(stream_key, extent, jnp.float32) * width * factor_of
    return jnp.minimum(jnp.maximum(entries, -reach), reach).astype(kind)


def setup_inputs(seed: int = 0) -> dict:
    key_of = jax.random.split(jax.random.key(seed), 21)
    return {
        "image_tokens": scatter_about(key_of[0], (SAMPLES, SEQ_LEN, D), 1.0, 6.0, ((0, 16), (1, 2))),
        "kept_index": draw_kept_index(jax.random.fold_in(key_of[20], 71), 0),
        "kept_count": draw_kept_count(jax.random.fold_in(key_of[20], 71), 0),
        "sample_valid": set_ends((jax.random.randint(key_of[3], (SAMPLES,), 0, 4) < 3).astype(jnp.int32), jax.random.fold_in(key_of[3], 1), 0, 1),
        "timestep": set_ends(jax.random.randint(key_of[4], (SAMPLES,), 0, 1000), jax.random.fold_in(key_of[4], 1), 0, 999).astype(jnp.int32),
        "class_label": set_ends(jax.random.randint(key_of[5], (SAMPLES,), 0, NCLASS), jax.random.fold_in(key_of[5], 1), 0, NCLASS - 1).astype(jnp.int32),
        "class_table": scatter_about(key_of[6], (NCLASS, D), 1.0, 6.0),
        "ada_weight": scatter_about(key_of[7], (D, 6 * D), D ** -0.5, 0.3125),
        "ada_bias": scatter_about(key_of[8], (6 * D,), 0.5, 3.0),
        "qkv_weight": scatter_about(key_of[9], (D, 3 * D), D ** -0.5, 0.3125),
        "qv_bias": scatter_about(key_of[10], (2, D), 0.5, 3.0),
        "rel_bias": scatter_about(key_of[11], (2, HEADS, 2 * GRID - 1), 1.0, 4.0),
        "out_weight": scatter_about(key_of[12], (D, D), (D // 8) ** -0.5, 0.875),
        "out_bias": scatter_about(key_of[13], (D,), 0.3, 2.0),
        "fc1_weight": scatter_about(key_of[14], (D, FF), D ** -0.5, 0.3125),
        "fc1_bias": scatter_about(key_of[15], (FF,), 0.5, 3.0),
        "fc2_weight": scatter_about(key_of[16], (FF, D), FF ** -0.5, 0.15625),
        "fc2_bias": scatter_about(key_of[17], (D,), 0.3, 2.0),
        "grad_full": scatter_about(key_of[18], (SAMPLES, SEQ_LEN, D), 1.0, 6.0, ((0, 16), (1, 2))),
        "grad_masked": scatter_about(key_of[19], (SAMPLES, KEEP, D), 1.0, 6.0, ((0, 16), (1, 2))),
    }


@jax.custom_vjp
def low(v):
    return lax.optimization_barrier(v.astype(jnp.bfloat16)).astype(jnp.float32)

@jax.custom_vjp
def low_back(v):
    return v

def low_keep(v):
    return (low(v), None)

def low_pass(kept, grad):
    return (grad,)

def back_keep(v):
    return (v, None)

def back_low(kept, grad):
    return (low(grad),)
low.defvjp(low_keep, low_pass)
low_back.defvjp(back_keep, back_low)

def matmul(left, right):
    return jnp.dot(left, right, precision=lax.Precision.HIGHEST, preferred_element_type=jnp.float32)

def layer_norm(value):
    average = lax.optimization_barrier(jnp.mean(value, axis=-1, keepdims=True))
    centred = value - average
    variance = lax.optimization_barrier(jnp.mean(centred * centred, axis=-1, keepdims=True))
    return centred * lax.rsqrt(variance + 1e-06)

def time_features(moments):
    half_width = D // 2
    frequency = jnp.exp(-math.log(10000.0) * jnp.arange(half_width, dtype=jnp.float32) / half_width)
    angles = moments.astype(jnp.float32)[:, None] * frequency[None, :]
    return jnp.concatenate([jnp.cos(angles), jnp.sin(angles)], axis=-1)

def relative_tables(rel):
    first = jnp.arange(GRID, dtype=jnp.int32)
    offsets = first[None, :] - first[:, None] + GRID - 1
    return rel[:, :, offsets]

def block_forward(tokens, where, key_live, modulation, params):
    shift_one, scale_one, gate_one, shift_two, scale_two, gate_two = [modulation[number] for number in range(6)]
    length = tokens.shape[0]
    normed = layer_norm(tokens)
    lowered = low(normed * (1.0 + scale_one) + shift_one)
    projected = matmul(lowered, params['qkv'])
    query = low_back(low(projected[:, :D] + params['qv'][0]))
    keys = low_back(low(projected[:, D:2 * D]))
    values = low_back(low(projected[:, 2 * D:] + params['qv'][1]))
    query_heads = query.reshape(length, HEADS, HDIM)
    key_heads = keys.reshape(length, HEADS, HDIM)
    value_heads = values.reshape(length, HEADS, HDIM)
    tables = relative_tables(params['rel'])
    rows = where // GRID
    cols = where % GRID
    bias = tables[0][:, rows[:, None], rows[None, :]] + tables[1][:, cols[:, None], cols[None, :]]
    raw = jnp.einsum('qhd,khd->hqk', query_heads, key_heads, precision=lax.Precision.HIGHEST)
    scores = low_back(raw * (1.0 / math.sqrt(HDIM)) + bias)
    scores = jnp.where(key_live[None, None, :], scores, -1e+30)
    attention = jax.nn.softmax(scores, axis=-1)
    mixed = jnp.einsum('hqk,khd->qhd', low(attention), value_heads, precision=lax.Precision.HIGHEST)
    merged = low_back(low(mixed.reshape(length, D)))
    attended = low_back(matmul(merged, params['out']) + params['out_bias'])
    middle = tokens + gate_one * attended
    second = low(layer_norm(middle) * (1.0 + scale_two) + shift_two)
    hidden_pre = low_back(matmul(second, params['fc1']) + params['fc1_bias'])
    hidden = low(jax.nn.gelu(hidden_pre))
    branch = low_back(matmul(hidden, params['fc2']) + params['fc2_bias'])
    return middle + gate_two * branch

def reference(image_tokens, kept_index, kept_count, sample_valid, timestep, class_label, class_table, ada_weight, ada_bias, qkv_weight, qv_bias, rel_bias, out_weight, out_bias, fc1_weight, fc1_bias, fc2_weight, fc2_bias, grad_full, grad_masked):
    params = {'table': class_table.astype(jnp.float32), 'ada': ada_weight.astype(jnp.float32), 'ada_bias': ada_bias.astype(jnp.float32), 'qkv': qkv_weight.astype(jnp.float32), 'qv': qv_bias.astype(jnp.float32), 'rel': rel_bias.astype(jnp.float32), 'out': out_weight.astype(jnp.float32), 'out_bias': out_bias.astype(jnp.float32), 'fc1': fc1_weight.astype(jnp.float32), 'fc1_bias': fc1_bias.astype(jnp.float32), 'fc2': fc2_weight.astype(jnp.float32), 'fc2_bias': fc2_bias.astype(jnp.float32)}
    positions = jnp.arange(SEQ_LEN, dtype=jnp.int32)
    slot_numbers = jnp.arange(KEEP, dtype=jnp.int32)

    def one_sample(totals, inputs):
        tokens, picked, kept, valid, moment, label, cot_full, cot_masked = inputs
        live = slot_numbers < kept

        def forward(weights, rows_in):
            conditioned = weights['table'][label] + time_features(moment[None])[0]
            activated = low(jax.nn.silu(conditioned))
            modulation = (matmul(activated[None, :], weights['ada'])[0] + weights['ada_bias']).reshape(6, D)
            full = block_forward(rows_in, positions, positions >= 0, modulation, weights)
            masked = block_forward(rows_in[picked], picked, live, modulation, weights)
            return (full, masked)
        (full, masked), pull = jax.vjp(forward, params, tokens.astype(jnp.float32))
        mask_full = valid.astype(jnp.float32)
        mask_slots = mask_full * live.astype(jnp.float32)
        grads, grad_rows = pull((cot_full.astype(jnp.float32) * mask_full, cot_masked.astype(jnp.float32) * mask_slots[:, None]))
        totals = jax.tree.map(jnp.add, totals, grads)
        return (totals, ((full * mask_full).astype(jnp.bfloat16), (masked * mask_slots[:, None]).astype(jnp.bfloat16), grad_rows))
    start = jax.tree.map(jnp.zeros_like, params)
    totals, stacked = lax.scan(one_sample, start, (image_tokens, kept_index, kept_count, sample_valid, timestep, class_label, grad_full, grad_masked))
    out_full, out_masked, grad_input = stacked
    return (out_full, out_masked, grad_input, totals['table'], totals['ada'], totals['ada_bias'], totals['qkv'], totals['qv'], totals['rel'], totals['out'], totals['out_bias'], totals['fc1'], totals['fc1_bias'], totals['fc2'], totals['fc2_bias'])
```

```python
import functools
import math

import jax
import jax.numpy as jnp
from jax import lax
from jax.experimental import pallas as pl
from jax.experimental.pallas import tpu as pltpu
from jax.sharding import PartitionSpec as P

D = 384
HEADS = 6
HDIM = 64
GRID = 32
FF = 1536
CHUNK = 512

AXES = ("dp", "seq")
F32 = jnp.float32
BF16 = jnp.bfloat16
MIB = 1024 * 1024
GELU_A = math.sqrt(2.0 / math.pi)
GELU_B = 0.044715

highest = lax.Precision.HIGHEST
big_negative = -1e30
vmem = pl.BlockSpec(memory_space=pltpu.VMEM)
smem = pl.BlockSpec(memory_space=pltpu.SMEM)


def round_up(value, step):
    return -(-value // step) * step


def blocks_of(first, count, most):
    pieces = -(-count // most)
    size = round_up(-(-count // pieces), 16)
    found = []
    at = 0
    while at < count:
        found.append((first + at, min(size, count - at)))
        at += size
    return found


def mm(left, right):
    return lax.dot_general(left, right, (((1,), (0,)), ((), ())), preferred_element_type=F32)


def mm_t(left, right):
    return lax.dot_general(left, right, (((1,), (1,)), ((), ())), preferred_element_type=F32)


def norm_parts(value):
    average = jnp.mean(value, axis=-1, keepdims=True)
    centred = value - average
    variance = jnp.mean(centred * centred, axis=-1, keepdims=True)
    inverse = lax.rsqrt(variance + 1e-06)
    return (centred * inverse, inverse)


def norm_back(normed, inverse, grad):
    first = jnp.mean(grad, axis=-1, keepdims=True)
    second = jnp.mean(grad * normed, axis=-1, keepdims=True)
    return inverse * (grad - first - normed * second)


def place_onehot(position):
    lane = lax.broadcasted_iota(jnp.int32, (position.shape[0], 2 * GRID), 1)
    wanted = jnp.where(lane < GRID, position // GRID, position % GRID + GRID)
    return (lane == wanted).astype(F32).astype(BF16)


def prep_kernel(
    start_ref, tok_ref, kept_ref, picked_ref, where_ref, mod_ref, weight_ref, qv_ref, table_ref,
    qaug_ref, kaug_ref, vaug_ref, a_ref, slot_ref, mask_ref, qs_ref,
):
    total = tok_ref.shape[0]
    own = qaug_ref.shape[1] - picked_ref.shape[0]
    slots = picked_ref.shape[0]
    shift, scale = mod_ref[0:1, :], mod_ref[1:2, :]
    normed, unused = norm_parts(tok_ref[...].astype(F32))
    lowered = (normed * (1.0 + scale) + shift).astype(BF16)
    a_ref[...] = lowered
    query = (mm(lowered, weight_ref[:, :D]) + qv_ref[0:1, :]).astype(BF16)
    scaled = (query.astype(F32) * (1.0 / math.sqrt(HDIM))).astype(BF16)
    qs_ref[...] = scaled
    keys = mm(lowered, weight_ref[:, D : 2 * D]).astype(BF16)
    values = (mm(lowered, weight_ref[:, 2 * D :]) + qv_ref[1:2, :]).astype(BF16)
    key_place = place_onehot(lax.broadcasted_iota(jnp.int32, (total, 1), 0))
    lane = lax.broadcasted_iota(jnp.int32, (total, HDIM), 1)
    ones = (lane == 0).astype(F32).astype(BF16)
    for head in range(HEADS):
        cols = slice(head * HDIM, (head + 1) * HDIM)
        kaug_ref[head] = jnp.concatenate([keys[:, cols], key_place], axis=1)
        vaug_ref[head] = jnp.concatenate([values[:, cols], ones], axis=1)
    chosen = (picked_ref[...] == lax.broadcasted_iota(jnp.int32, (slots, total), 1)).astype(F32)
    chosen = chosen.astype(BF16)
    slot_ref[:, :D] = mm(chosen, tok_ref[...]).astype(BF16)
    slot_ref[:, D:] = mm(chosen, lowered).astype(BF16)
    slot_query = mm(chosen, scaled).astype(BF16)
    own_query = qs_ref[pl.ds(pl.multiple_of(start_ref[0], 16), own), :]
    offsets = mm(place_onehot(where_ref[...]), table_ref[...]).astype(BF16)
    for head in range(HEADS):
        cols = slice(head * HDIM, (head + 1) * HDIM)
        qaug_ref[head, :own] = jnp.concatenate([own_query[:, cols], offsets[:own, cols]], axis=1)
        qaug_ref[head, own:] = jnp.concatenate([slot_query[:, cols], offsets[own:, cols]], axis=1)
    held = kept_ref.shape[0]
    hit = kept_ref[...] == lax.broadcasted_iota(jnp.int32, (held, total), 1)
    count = jnp.sum(hit.astype(F32), axis=0, keepdims=True)
    mask_ref[...] = jnp.broadcast_to(jnp.where(count > 0.0, 0.0, big_negative), mask_ref.shape)


def attend_kernel(own, qaug_ref, kaug_ref, vaug_ref, mask_ref, o_ref, lse_ref):
    rows = qaug_ref.shape[1]
    spans = [(at, size, False) for at, size in blocks_of(0, own, 256)]
    spans += [(at, size, True) for at, size in blocks_of(own, rows - own, 256)]

    def pair(group, carry):
        for at, size, masked in spans:
            outs, logs = [], []
            for side in range(2):
                head = 2 * group + side
                scores = mm_t(qaug_ref[head, at : at + size, :], kaug_ref[head])
                if masked:
                    scores = scores + mask_ref[0:1, :]
                top = jnp.max(scores, axis=-1, keepdims=True)
                spread = jnp.exp(scores - top).astype(BF16)
                mixed = mm(spread, vaug_ref[head])
                total = mixed[:, HDIM : HDIM + 1]
                outs.append(mixed[:, :HDIM] * (1.0 / total))
                logs.append(jnp.broadcast_to(top + jnp.log(total), (size, HDIM)))
            o_ref[group, at : at + size, :] = jnp.concatenate(outs, axis=1)
            lse_ref[group, at : at + size, :] = jnp.concatenate(logs, axis=1)
        return carry

    lax.fori_loop(0, HEADS // 2, pair, 0)


def feed_kernel(
    own, o_ref, tok_ref, slot_ref, cot_full_ref, cot_slot_ref, wgt_ref, mod_ref,
    wout_ref, bout_ref, w1_ref, b1_ref, w2_ref, b2_ref, extra_ref,
    out_full_ref, out_slot_ref, dm_ref, do_ref, small_ref, pay_ref, g1_ref, g2_ref, go_ref, gb1_ref,
):
    rows = o_ref.shape[1]
    slots = rows - own
    g1_ref[...] = jnp.zeros(g1_ref.shape, F32)
    g2_ref[...] = jnp.zeros(g2_ref.shape, F32)
    go_ref[...] = jnp.zeros(go_ref.shape, F32)
    gb1_ref[...] = jnp.zeros(gb1_ref.shape, F32)
    small_ref[...] = jnp.zeros(small_ref.shape, F32)
    gate1, shift2, scale2, gate2 = [mod_ref[n : n + 1, :] for n in range(2, 6)]

    def part(x_ref, cot_ref, out_ref, base, size):
        def step(index, carry):
            at = pl.multiple_of(index * size, 16)
            here = pl.ds(at, size)
            there = pl.ds(pl.multiple_of(base + index * size, 16), size)
            weight = wgt_ref[there, :]
            merged = jnp.concatenate([o_ref[n, there, :] for n in range(HEADS // 2)], axis=1)
            merged = merged.astype(BF16)
            attended = mm(merged, wout_ref[...]) + bout_ref[...]
            middle = x_ref[here, :D].astype(F32) + gate1 * attended
            normed, inverse = norm_parts(middle)
            second = (normed * (1.0 + scale2) + shift2).astype(BF16)
            second_t = second.T
            cot = cot_ref[here, :].astype(F32) * weight
            dz_f = gate2 * cot
            dz = dz_f.astype(BF16)
            branch = jnp.broadcast_to(b2_ref[...], (size, D))
            back = jnp.zeros((size, D), F32)
            for c in range(FF // CHUNK):
                cols = slice(c * CHUNK, (c + 1) * CHUNK)
                u = mm(second, w1_ref[:, cols]) + b1_ref[:, cols]
                square = u * u
                t = jnp.tanh(GELU_A * u * (1.0 + GELU_B * square))
                cdf = 0.5 * (1.0 + t)
                hidden = (u * cdf).astype(BF16)
                slope = cdf + (0.5 * GELU_A) * u * (1.0 - t * t) * (1.0 + (3.0 * GELU_B) * square)
                branch = branch + mm(hidden, w2_ref[cols, :])
                du_f = slope * mm_t(dz, w2_ref[cols, :])
                du = du_f.astype(BF16)
                back = back + mm_t(du, w1_ref[:, cols])
                g2_ref[cols, :] += mm(hidden.T, dz)
                g1_ref[:, cols] += mm(second_t, du)
                gb1_ref[:, cols] += jnp.sum(du.astype(F32), axis=0, keepdims=True)
            out_ref[here, :] = ((middle + gate2 * branch) * weight).astype(BF16)
            dmid = cot + norm_back(normed, inverse, back * (1.0 + scale2))
            dm_ref[there, :] = dmid
            datt = (gate1 * dmid).astype(BF16)
            do_ref[there, :] = mm_t(datt, wout_ref[...]).astype(BF16)
            go_ref[...] += mm(merged.T, datt)
            sums = [
                dmid * attended, back, back * normed, cot * branch,
                dz.astype(F32), datt.astype(F32),
            ]
            for n, value in enumerate(sums):
                small_ref[n : n + 1, :] += jnp.sum(value, axis=0, keepdims=True)
            return carry

        count = x_ref.shape[0] // size
        lax.fori_loop(0, count, step, 0)

    part(tok_ref, cot_full_ref, out_full_ref, 0, blocks_of(0, own, 256)[0][1])
    part(slot_ref, cot_slot_ref, out_slot_ref, own, blocks_of(0, slots, 256)[0][1])
    for n in range(4):
        pay_ref[n * D : (n + 1) * D, :] = g1_ref[:, n * D : (n + 1) * D].astype(BF16)
    pay_ref[FF : 2 * FF, :] = g2_ref[...].astype(BF16)
    pay_ref[2 * FF : 2 * FF + D, :] = go_ref[...].astype(BF16)
    base = 2 * FF + D
    heads = [gb1_ref[:, n * D : (n + 1) * D] for n in range(4)]
    heads += [small_ref[4:5, :], small_ref[5:6, :], jnp.zeros((10, D), F32)]
    pay_ref[base : base + 16, :] = jnp.concatenate(heads, axis=0).astype(BF16)
    pay_ref[base + 16 :, :] = extra_ref[...]


def attend_back_kernel(
    own, qaug_ref, kaug_ref, vaug_ref, mask_ref, o_ref, lse_ref, do_ref, where_ref,
    dq_ref, dk_ref, dv_ref, tab_ref, dkt_ref, dvt_ref,
):
    rows = qaug_ref.shape[1]
    spans = [(at, size, False) for at, size in blocks_of(0, own, 256)]
    spans += [(at, size, True) for at, size in blocks_of(own, rows - own, 256)]

    def pair(group, carry):
        dkt_ref[...] = jnp.zeros(dkt_ref.shape, F32)
        dvt_ref[...] = jnp.zeros(dvt_ref.shape, F32)
        tab_ref[group] = jnp.zeros(tab_ref.shape[1:], F32)
        for at, size, masked in spans:
            place_t = place_onehot(where_ref[at : at + size, :]).T
            dqs, tabs = [], []
            for side in range(2):
                head = 2 * group + side
                lanes = slice(side * HDIM, (side + 1) * HDIM)
                query = qaug_ref[head, at : at + size, :]
                keys = kaug_ref[head]
                scores = mm_t(query, keys)
                if masked:
                    scores = scores + mask_ref[0:1, :]
                weights = jnp.exp(scores - lse_ref[group, at : at + size, side * HDIM : side * HDIM + 1])
                grad_out = do_ref[group, at : at + size, lanes]
                delta = jnp.sum(
                    grad_out.astype(F32) * o_ref[group, at : at + size, lanes], axis=-1, keepdims=True
                )
                dp = mm_t(grad_out, vaug_ref[head, :, :HDIM])
                ds = (weights * (dp - delta)).astype(BF16)
                found = mm(ds, keys)
                dqs.append(found[:, :HDIM] * (1.0 / math.sqrt(HDIM)))
                tabs.append(found[:, HDIM:].astype(BF16))
                dkt_ref[lanes, :] += mm(query[:, :HDIM].T, ds)
                dvt_ref[lanes, :] += mm(grad_out.T, weights.astype(BF16))
            dq_ref[group, at : at + size, :] = jnp.concatenate(dqs, axis=1).astype(BF16)
            tab_ref[group] += mm(place_t, jnp.concatenate(tabs, axis=1))
        dk_ref[group] = dkt_ref[...].astype(BF16).T
        dv_ref[group] = dvt_ref[...].astype(BF16).T
        return carry

    lax.fori_loop(0, HEADS // 2, pair, 0)


def prep_back_kernel(
    own, start_ref, tok_ref, a_ref, slot_ref, picked_ref, mod_ref, weight_ref,
    dq_ref, dk_ref, dv_ref, dm_ref,
    pay_ref, small_ref, dx_ref, dx_own_ref, dxs_ref,
):
    total = tok_ref.shape[0]
    rows = dq_ref.shape[1]
    slots = rows - own
    scale = mod_ref[1:2, :]
    start = pl.multiple_of(start_ref[0], 16)
    here = pl.ds(start, own)

    def joined(ref, span):
        return jnp.concatenate([ref[n, span, :] for n in range(HEADS // 2)], axis=1)

    every = slice(0, total)
    dk, dv = joined(dk_ref, every), joined(dv_ref, every)
    dq_own, dq_slot = joined(dq_ref, slice(0, own)), joined(dq_ref, slice(own, rows))
    lowered_t = a_ref[...].T
    gq = mm(a_ref[here, :].T, dq_own) + mm(slot_ref[:, D:].T, dq_slot)
    pay_ref[0:D, :] = gq.astype(BF16)
    pay_ref[D : 2 * D, :] = mm(lowered_t, dk).astype(BF16)
    pay_ref[2 * D : 3 * D, :] = mm(lowered_t, dv).astype(BF16)
    column = lambda value: jnp.sum(value.astype(F32), axis=0, keepdims=True)
    normed, inverse = norm_parts(tok_ref[...].astype(F32))
    da = mm_t(dk, weight_ref[:, D : 2 * D]) + mm_t(dv, weight_ref[:, 2 * D :])
    shift_sum, scale_sum = column(da), column(da * normed)
    dxs_ref[...] = norm_back(normed, inverse, da * (1.0 + scale))
    own_normed, own_inverse = norm_parts(tok_ref[here, :].astype(F32))
    da = mm_t(dq_own, weight_ref[:, :D])
    shift_sum, scale_sum = shift_sum + column(da), scale_sum + column(da * own_normed)
    dxs_ref[here, :] += dm_ref[:own, :] + norm_back(own_normed, own_inverse, da * (1.0 + scale))
    slot_normed, slot_inverse = norm_parts(slot_ref[:, :D].astype(F32))
    da = mm_t(dq_slot, weight_ref[:, :D])
    shift_sum, scale_sum = shift_sum + column(da), scale_sum + column(da * slot_normed)
    spread = dm_ref[own:, :] + norm_back(slot_normed, slot_inverse, da * (1.0 + scale))
    chosen = (picked_ref[...] == lax.broadcasted_iota(jnp.int32, (slots, total), 1)).astype(F32)
    dxs_ref[...] += mm(chosen.astype(BF16).T, spread.astype(BF16))
    dx_ref[...] = dxs_ref[...].astype(BF16)
    dx_own_ref[...] = dxs_ref[here, :]
    parts = [shift_sum, scale_sum, column(dq_own) + column(dq_slot), column(dv)]
    small_ref[...] = jnp.concatenate(parts + [jnp.zeros((4, D), F32)], axis=0)


def call(kernel, outs, scratch, args, specs=None, flops=0, limit=48):
    return pl.pallas_call(
        kernel,
        out_shape=[jax.ShapeDtypeStruct(shape, dtype) for shape, dtype in outs],
        in_specs=specs if specs is not None else [vmem] * len(args),
        out_specs=[vmem] * len(outs),
        scratch_shapes=[pltpu.VMEM(shape, dtype) for shape, dtype in scratch],
        compiler_params=pltpu.CompilerParams(vmem_limit_bytes=limit * MIB),
        cost_estimate=pl.CostEstimate(flops=flops, bytes_accessed=4 * MIB, transcendentals=0),
    )(*args)


def reduce_all(value, dp, seq):
    rows = value.shape[0]
    place = lax.axis_index("dp")
    side = place % 2
    swap = [(n, n ^ 1) for n in range(dp)]
    groups = [
        [(2 * pair + core) * seq + at for pair in range(dp // 2) for at in range(seq)]
        for core in range(2)
    ]
    peers = dp // 2 * seq
    halves = value.reshape(2, rows // 2, D)
    keep = lax.dynamic_index_in_dim(halves, side, 0, keepdims=False)
    send = lax.dynamic_index_in_dim(halves, 1 - side, 0, keepdims=False)
    got = lax.ppermute(send, "dp", swap)
    mine = (keep.astype(F32) + got.astype(F32)).astype(BF16)
    pieces = lax.all_to_all(
        mine.reshape(peers, rows // 2 // peers, D), AXES, 0, 0, axis_index_groups=groups
    )
    chunk = jnp.sum(pieces.astype(F32), axis=0).astype(BF16)
    wide = jnp.broadcast_to(chunk[None], (peers,) + chunk.shape)
    half = lax.all_to_all(wide, AXES, 0, 0, axis_index_groups=groups).reshape(rows // 2, D)
    other = lax.ppermute(half, "dp", swap)
    first = jnp.where(side == 0, half, other)
    second = jnp.where(side == 0, other, half)
    return jnp.concatenate([first, second], axis=0)


def gather_tokens(tokens, seq):
    rows = tokens.shape[0]
    me = lax.axis_index("seq")
    whole = jnp.zeros((seq, rows, D), tokens.dtype)
    whole = lax.dynamic_update_index_in_dim(whole, tokens, me, 0)
    for step in range(1, seq):
        came = lax.ppermute(tokens, "seq", [(n, (n + step) % seq) for n in range(seq)])
        whole = lax.dynamic_update_index_in_dim(whole, came, (me - step) % seq, 0)
    return whole.reshape(seq * rows, D)


def scatter_rows(partial, own, seq):
    rows = own.shape[0]
    me = lax.axis_index("seq")
    blocks = partial.reshape(seq, rows, D)
    for step in range(1, seq):
        block = lax.dynamic_index_in_dim(blocks, (me + step) % seq, 0, keepdims=False)
        own = own + lax.ppermute(block, "seq", [(n, (n + step) % seq) for n in range(seq)]).astype(F32)
    return own


def time_features(moments):
    half_width = D // 2
    frequency = jnp.exp(-math.log(10000.0) * jnp.arange(half_width, dtype=F32) / half_width)
    angles = moments.astype(F32)[:, None] * frequency[None, :]
    return jnp.concatenate([jnp.cos(angles), jnp.sin(angles)], axis=-1)


def offset_hot():
    first = jnp.arange(GRID, dtype=jnp.int32)
    offsets = first[None, :] - first[:, None] + GRID - 1
    return (offsets[..., None] == jnp.arange(2 * GRID - 1, dtype=jnp.int32)).astype(F32)


def bias_table(rel_bias):
    both = jnp.einsum("cho,ijo->cihj", rel_bias.astype(F32), offset_hot(), precision=highest)
    empty = jnp.zeros_like(both[0])
    top = jnp.concatenate([both[0], empty], axis=-1)
    low = jnp.concatenate([empty, both[1]], axis=-1)
    return jnp.concatenate([top, low], axis=0).reshape(2 * GRID, HEADS * 2 * GRID).astype(BF16)


def body(
    dp, seq, image_tokens, kept_index, kept_count, sample_valid, timestep, class_label, class_table,
    ada_weight, ada_bias, qkv_weight, qv_bias, rel_bias, out_weight, out_bias, fc1_weight,
    fc1_bias, fc2_weight, fc2_bias, grad_full, grad_masked,
):
    samples, own, width = image_tokens.shape
    held = kept_index.shape[1]
    slots = grad_masked.shape[1]
    padded = round_up(slots, 16)
    rows = own + padded
    total = own * seq
    everyone = dp * samples
    classes = class_table.shape[0]
    dp_place, seq_place = lax.axis_index("dp"), lax.axis_index("seq")
    start = (seq_place * own).astype(jnp.int32).reshape(1)

    conditioned = jnp.take(class_table, class_label, axis=0).astype(F32) + time_features(timestep)
    gate = jax.nn.sigmoid(conditioned)
    activated = (conditioned * gate).astype(BF16)
    slope = gate * (1.0 + conditioned * (1.0 - gate))
    modulation = jnp.dot(activated, ada_weight, preferred_element_type=F32) + ada_bias.astype(F32)
    modulation = jnp.pad(modulation.reshape(samples, 6, D), ((0, 0), (0, 2), (0, 0)))
    table = bias_table(rel_bias)
    valid = sample_valid.astype(F32)

    digits = jnp.stack([class_label // GRID, class_label % GRID], axis=1).astype(F32)
    digits = jnp.pad(digits, ((0, 0), (0, D - 2)))
    info = jnp.stack([activated.astype(F32), slope, digits], axis=0)
    info = info * (seq_place == 0).astype(F32)
    extra_rows = round_up(2 * FF + D + 16 + 3 * everyone, dp * seq * 16) - (2 * FF + D + 16)
    spread = (jnp.arange(everyone)[:, None] == dp_place * samples + jnp.arange(samples)[None, :])
    info = jnp.einsum("es,nsd->end", spread.astype(F32), info, precision=highest)
    info = info.transpose(1, 0, 2).reshape(3 * everyone, D).astype(BF16)
    info = jnp.pad(info, ((0, extra_rows - 3 * everyone), (0, 0)))

    slot_numbers = jnp.arange(held, dtype=jnp.int32)
    live_all = slot_numbers[None, :] < kept_count[:, None]
    slot_start = seq_place * slots
    outs = []
    for s in range(samples):
        tokens = image_tokens[s]
        whole = gather_tokens(tokens, seq)
        kept = jnp.where(live_all[s], kept_index[s], -1)[:, None]
        picked = lax.dynamic_slice_in_dim(kept_index[s], slot_start, slots, 0)
        live = lax.dynamic_slice_in_dim(live_all[s], slot_start, slots, 0)
        picked = jnp.pad(picked, (0, padded - slots))[:, None]
        where = jnp.concatenate([start + jnp.arange(own, dtype=jnp.int32), picked[:, 0]])[:, None]
        weight = valid[s] * jnp.concatenate(
            [jnp.ones((own,), F32), jnp.pad(live.astype(F32), (0, padded - slots))]
        )
        cot_slot = jnp.pad(grad_masked[s], ((0, padded - slots), (0, 0)))
        qaug, kaug, vaug, lowered, slot, mask = call(
            prep_kernel,
            [
                ((HEADS, rows, 128), BF16), ((HEADS, total, 128), BF16), ((HEADS, total, 128), BF16),
                ((total, D), BF16), ((padded, 2 * D), BF16), ((8, total), F32),
            ],
            [((total, D), BF16)],
            [start, whole, kept, picked, where, modulation[s], qkv_weight, qv_bias.astype(F32), table],
            specs=[smem] + [vmem] * 8,
        )
        mixed, lse = call(
            functools.partial(attend_kernel, own),
            [((HEADS // 2, rows, 128), F32), ((HEADS // 2, rows, 128), F32)],
            [],
            [qaug, kaug, vaug, mask],
        )
        out_full, out_slot, dmid, dout, small, payload = call(
            functools.partial(feed_kernel, own),
            [
                ((own, D), BF16), ((padded, D), BF16), ((rows, D), F32), ((rows, D), BF16),
                ((8, D), F32), ((2 * FF + D + 16 + extra_rows, D), BF16),
            ],
            [((D, FF), F32), ((FF, D), F32), ((D, D), F32), ((1, FF), F32)],
            [
                mixed, tokens, slot, grad_full[s], cot_slot, weight[:, None], modulation[s],
                out_weight, out_bias.astype(F32)[None], fc1_weight, fc1_bias.astype(F32)[None],
                fc2_weight, fc2_bias.astype(F32)[None], info if s == 0 else jnp.zeros_like(info),
            ],
        )
        dout = dout.reshape(rows, HEADS // 2, 128).transpose(1, 0, 2)
        dq, dk, dv, tab = call(
            functools.partial(attend_back_kernel, own),
            [
                ((HEADS // 2, rows, 128), BF16), ((HEADS // 2, total, 128), BF16),
                ((HEADS // 2, total, 128), BF16), ((HEADS // 2, 2 * GRID, 128), F32),
            ],
            [((128, total), F32), ((128, total), F32)],
            [qaug, kaug, vaug, mask, mixed, lse, dout, where],
        )
        pay_qkv, small_one, dx, dx_own = call(
            functools.partial(prep_back_kernel, own),
            [((3 * D, D), BF16), ((8, D), F32), ((total, D), BF16), ((own, D), F32)],
            [((total, D), F32)],
            [start, whole, lowered, slot, picked, modulation[s], qkv_weight, dq, dk, dv, dmid],
            specs=[smem] + [vmem] * 10,
        )
        grad_input = scatter_rows(dx, dx_own, seq)
        dmod = jnp.concatenate([small_one[0:2], small[0:4]], axis=0)
        outs.append((out_full, out_slot[:slots], grad_input, payload, pay_qkv, small_one[2:4], tab, dmod))

    def sum_of(number):
        if samples == 1:
            return outs[0][number]
        return functools.reduce(jnp.add, [o[number].astype(F32) for o in outs]).astype(outs[0][number].dtype)

    offsets = offset_hot()
    tab = sum_of(6).reshape(HEADS // 2, 2, GRID, 2, 2, GRID)
    tab = jnp.stack([tab[:, 0, :, :, 0, :], tab[:, 1, :, :, 1, :]]).transpose(0, 1, 3, 2, 4)
    tab = tab.reshape(2, HEADS, GRID, GRID)
    grad_rel = jnp.einsum("chij,ijo->cho", tab, offsets, precision=highest)
    grad_rel = jnp.pad(grad_rel, ((0, 0), (0, 0), (0, 1))).reshape(2, D)
    dmods = jnp.stack([o[7] for o in outs], axis=1)
    dmods = jnp.einsum("es,nsd->end", spread.astype(F32), dmods, precision=highest)
    tail = jnp.concatenate([sum_of(5), grad_rel, dmods.reshape(6 * everyone, D)], axis=0)
    tail_rows = round_up(3 * D + tail.shape[0], dp * seq * 8) - 3 * D
    tail = jnp.pad(tail, ((0, tail_rows - tail.shape[0]), (0, 0))).astype(BF16)

    layer = reduce_all(sum_of(3), dp, seq)
    last = reduce_all(jnp.concatenate([sum_of(4), tail], axis=0), dp, seq)

    base = 2 * FF + D
    grad_fc1 = layer[:FF].reshape(4, D, D).transpose(1, 0, 2).reshape(D, FF).astype(F32)
    grad_fc2 = layer[FF : 2 * FF].astype(F32)
    grad_out = layer[2 * FF : base].astype(F32)
    grad_fc1_bias = layer[base : base + 4].reshape(FF).astype(F32)
    grad_fc2_bias = layer[base + 4].astype(F32)
    grad_out_bias = layer[base + 5].astype(F32)
    info = layer[base + 16 : base + 16 + 3 * everyone].reshape(3, everyone, D)
    act_all, slope_all = info[0], info[1].astype(F32)
    label_all = (info[2, :, 0].astype(F32) * GRID + info[2, :, 1].astype(F32)).astype(jnp.int32)

    grad_qkv = last[: 3 * D].reshape(3, D, D).transpose(1, 0, 2).reshape(D, 3 * D).astype(F32)
    grad_qv = last[3 * D : 3 * D + 2].astype(F32)
    grad_rel = last[3 * D + 2 : 3 * D + 4].reshape(2, HEADS, 64)[:, :, :63].astype(F32)
    dmod_all = last[3 * D + 4 : 3 * D + 4 + 6 * everyone].reshape(everyone, 6 * D)
    grad_ada = lax.dot_general(act_all, dmod_all, (((0,), (0,)), ((), ())), preferred_element_type=F32)
    grad_ada_bias = jnp.sum(dmod_all.astype(F32), axis=0)
    grad_act = lax.dot_general(dmod_all, ada_weight, (((1,), (1,)), ((), ())), preferred_element_type=F32)
    grad_cond = slope_all * grad_act
    label_hot = (label_all[:, None] == jnp.arange(classes, dtype=jnp.int32)).astype(F32)
    grad_table = jnp.dot(label_hot.T, grad_cond, precision=highest)

    out_full, out_masked, grad_input = [jnp.stack([o[n] for o in outs]) for n in range(3)]
    return (
        out_full, out_masked, grad_input, grad_table, grad_ada, grad_ada_bias, grad_qkv, grad_qv,
        grad_rel, grad_out, grad_out_bias, grad_fc1, grad_fc1_bias, grad_fc2, grad_fc2_bias,
    )


def solution(mesh):
    split = P("dp", "seq", None)
    placed = (split, P("dp", None)) + (P("dp"),) * 4 + (P(),) * 12 + (split, split)
    return jax.shard_map(
        functools.partial(body, mesh.shape["dp"], mesh.shape["seq"]),
        mesh=mesh,
        in_specs=placed,
        out_specs=(split,) * 3 + (P(),) * 12,
        check_vma=False,
    )
```

```python
import functools
import math

import jax
import jax.numpy as jnp
from jax import lax
from jax.experimental import pallas as pl
from jax.experimental.pallas import tpu as pltpu
from jax.sharding import PartitionSpec as P

D = 384
HEADS = 6
HDIM = 64
GRID = 32
FF = 1536
CHUNK = 512

AXES = ("dp", "seq")
F32 = jnp.float32
BF16 = jnp.bfloat16
MIB = 1024 * 1024
GELU_A = math.sqrt(2.0 / math.pi)
GELU_B = 0.044715

highest = lax.Precision.HIGHEST
big_negative = -1e30
vmem = pl.BlockSpec(memory_space=pltpu.VMEM)
smem = pl.BlockSpec(memory_space=pltpu.SMEM)
hbm = pl.BlockSpec(memory_space=pltpu.HBM)


def round_up(value, step):
    return -(-value // step) * step


def blocks_of(first, count, most):
    pieces = -(-count // most)
    size = round_up(-(-count // pieces), 16)
    found = []
    at = 0
    while at < count:
        found.append((first + at, min(size, count - at)))
        at += size
    return found


def mm(left, right):
    return lax.dot_general(left, right, (((1,), (0,)), ((), ())), preferred_element_type=F32)


def mm_t(left, right):
    return lax.dot_general(left, right, (((1,), (1,)), ((), ())), preferred_element_type=F32)


def norm_parts(value):
    average = jnp.mean(value, axis=-1, keepdims=True)
    centred = value - average
    variance = jnp.mean(centred * centred, axis=-1, keepdims=True)
    inverse = lax.rsqrt(variance + 1e-06)
    return (centred * inverse, inverse)


def norm_back(normed, inverse, grad):
    first = jnp.mean(grad, axis=-1, keepdims=True)
    second = jnp.mean(grad * normed, axis=-1, keepdims=True)
    return inverse * (grad - first - normed * second)


def place_onehot(position, turned=False):
    lane = lax.broadcasted_iota(jnp.int32, (position.shape[0], 2 * GRID), 1)
    if turned:
        lane = jnp.where(lane < GRID, GRID - 1 - lane, 3 * GRID - 1 - lane)
    wanted = jnp.where(lane < GRID, position // GRID, position % GRID + GRID)
    return (lane == wanted).astype(F32).astype(BF16)


class Copies:
    def __init__(self, sems):
        self.sems, self.made = sems, []

    def start(self, source, target):
        copy = pltpu.make_async_copy(source, target, self.sems.at[len(self.made)])
        copy.start()
        self.made.append(copy)

    def wait(self):
        for copy in self.made:
            copy.wait()


def halves_writer(side_ref, keep_ref, send_ref):
    half = keep_ref.shape[0]

    def put(at, value):
        count = value.shape[0]
        for which in range(2):
            first, last = max(at, which * half), min(at + count, (which + 1) * half)
            if first >= last:
                continue
            piece = value[first - at : last - at].astype(BF16)
            span = slice(first - which * half, last - which * half)

            @pl.when(side_ref[0] == which)
            def keep():
                keep_ref[span, :] = piece

            @pl.when(side_ref[0] != which)
            def send():
                send_ref[span, :] = piece

    return put


def prep_kernel(
    own, seq, starts_ref, *refs,
):
    token_refs, refs = refs[:seq], refs[seq:]
    kept_ref, picked_ref, where_ref, mod_ref, weight_ref, qv_ref, table_ref = refs[:7]
    qaug_ref, kaug_ref, vaug_ref, x_ref, mask_ref, a_out, tok_out, slot_out = refs[7:15]
    qs_ref, a_ref, tok_ref, slot_ref, sems = refs[15:]
    copies = Copies(sems)
    total = own * seq
    slots = picked_ref.shape[0]
    for n in range(seq):
        tok_ref[pl.ds(pl.multiple_of(starts_ref[n], 16), own), :] = token_refs[n][...]
    copies.start(tok_ref, tok_out)
    shift, scale = mod_ref[0:1, :], mod_ref[1:2, :]
    normed, unused = norm_parts(tok_ref[...].astype(F32))
    lowered = (normed * (1.0 + scale) + shift).astype(BF16)
    a_ref[...] = lowered
    copies.start(a_ref, a_out)
    query = (mm(lowered, weight_ref[:, :D]) + qv_ref[0:1, :]).astype(BF16)
    scaled = (query.astype(F32) * (1.0 / math.sqrt(HDIM))).astype(BF16)
    qs_ref[...] = scaled
    keys = mm(lowered, weight_ref[:, D : 2 * D]).astype(BF16)
    values = (mm(lowered, weight_ref[:, 2 * D :]) + qv_ref[1:2, :]).astype(BF16)
    key_place = place_onehot(lax.broadcasted_iota(jnp.int32, (total, 1), 0))
    lane = lax.broadcasted_iota(jnp.int32, (total, HDIM), 1)
    ones = (lane == 0).astype(F32).astype(BF16)
    for head in range(HEADS):
        cols = slice(head * HDIM, (head + 1) * HDIM)
        kaug_ref[head] = jnp.concatenate([keys[:, cols], key_place], axis=1)
        vaug_ref[head] = jnp.concatenate([values[:, cols], ones], axis=1)
    chosen = (picked_ref[...] == lax.broadcasted_iota(jnp.int32, (slots, total), 1)).astype(F32)
    chosen = chosen.astype(BF16)
    x_ref[:own, :] = token_refs[0][...]
    x_ref[own:, :] = mm(chosen, tok_ref[...]).astype(BF16)
    slot_ref[...] = mm(chosen, lowered).astype(BF16)
    copies.start(slot_ref, slot_out)
    slot_query = mm(chosen, scaled).astype(BF16)
    own_query = qs_ref[pl.ds(pl.multiple_of(starts_ref[0], 16), own), :]
    offsets = mm(place_onehot(where_ref[...]), table_ref[...]).astype(BF16)
    for head in range(HEADS):
        cols = slice(head * HDIM, (head + 1) * HDIM)
        qaug_ref[head, :own] = jnp.concatenate([own_query[:, cols], offsets[:own, cols]], axis=1)
        qaug_ref[head, own:] = jnp.concatenate([slot_query[:, cols], offsets[own:, cols]], axis=1)
    held = kept_ref.shape[0]
    hit = kept_ref[...] == lax.broadcasted_iota(jnp.int32, (held, total), 1)
    count = jnp.sum(hit.astype(F32), axis=0, keepdims=True)
    mask_ref[...] = jnp.broadcast_to(jnp.where(count > 0.0, 0.0, big_negative), mask_ref.shape)
    copies.wait()


def attend_kernel(
    own, qaug_ref, kaug_ref, vaug_ref, mask_ref, o_ref, lse_ref, qaug_out, kaug_out, vaug_out, sems
):
    rows = qaug_ref.shape[1]
    copies = Copies(sems)
    copies.start(qaug_ref, qaug_out)
    copies.start(kaug_ref, kaug_out)
    copies.start(vaug_ref, vaug_out)
    spans = [(at, size, False) for at, size in blocks_of(0, own, 256)]
    spans += [(at, size, True) for at, size in blocks_of(own, rows - own, 256)]

    def pair(group, carry):
        for at, size, masked in spans:
            outs, logs = [], []
            for side in range(2):
                head = 2 * group + side
                scores = mm_t(qaug_ref[head, at : at + size, :], kaug_ref[head])
                if masked:
                    scores = scores + mask_ref[0:1, :]
                top = jnp.max(scores, axis=-1, keepdims=True)
                spread = jnp.exp(scores - top).astype(BF16)
                mixed = mm(spread, vaug_ref[head])
                total = mixed[:, HDIM : HDIM + 1]
                outs.append(mixed[:, :HDIM] * (1.0 / total))
                logs.append(jnp.broadcast_to(top + jnp.log(total), (size, HDIM)))
            o_ref[group, at : at + size, :] = jnp.concatenate(outs, axis=1)
            lse_ref[group, at : at + size, :] = jnp.concatenate(logs, axis=1)
        return carry

    lax.fori_loop(0, HEADS // 2, pair, 0)
    copies.wait()


def feed_kernel(
    size, own, side_ref, o_ref, lse_ref, x_ref, cot_ref, wgt_ref, mod_ref,
    wout_ref, bout_ref, w1_ref, b1_ref, w2_ref, b2_ref, extra_ref,
    do_ref, small_ref, keep_ref, send_ref, y_full_out, y_slot_out, dm_out, o_out, lse_out, x_out, do_out,
    y_ref, dm_ref, g1_ref, g2_ref, go_ref, gb1_ref, sems,
):
    rows = o_ref.shape[1]
    copies = Copies(sems)
    copies.start(o_ref, o_out)
    copies.start(lse_ref, lse_out)
    copies.start(x_ref, x_out)
    g1_ref[...] = jnp.zeros(g1_ref.shape, F32)
    g2_ref[...] = jnp.zeros(g2_ref.shape, F32)
    go_ref[...] = jnp.zeros(go_ref.shape, F32)
    gb1_ref[...] = jnp.zeros(gb1_ref.shape, F32)
    small_ref[...] = jnp.zeros(small_ref.shape, F32)
    gate1, shift2, scale2, gate2 = [mod_ref[n : n + 1, :] for n in range(2, 6)]

    def step(index, carry):
        here = pl.ds(pl.multiple_of(index * size, 16), size)
        weight = wgt_ref[here, :]
        merged = jnp.concatenate([o_ref[n, here, :] for n in range(HEADS // 2)], axis=1)
        merged = merged.astype(BF16)
        attended = mm(merged, wout_ref[...]) + bout_ref[...]
        middle = x_ref[here, :].astype(F32) + gate1 * attended
        normed, inverse = norm_parts(middle)
        second = (normed * (1.0 + scale2) + shift2).astype(BF16)
        second_t = second.T
        cot = cot_ref[here, :].astype(F32) * weight
        dz = (gate2 * cot).astype(BF16)
        branch = jnp.broadcast_to(b2_ref[...], (size, D))
        back = jnp.zeros((size, D), F32)
        for c in range(FF // CHUNK):
            cols = slice(c * CHUNK, (c + 1) * CHUNK)
            u = mm(second, w1_ref[:, cols]) + b1_ref[:, cols]
            square = u * u
            t = jnp.tanh(GELU_A * u * (1.0 + GELU_B * square))
            cdf = 0.5 * (1.0 + t)
            hidden = (u * cdf).astype(BF16)
            slope = cdf + (0.5 * GELU_A) * u * (1.0 - t * t) * (1.0 + (3.0 * GELU_B) * square)
            branch = branch + mm(hidden, w2_ref[cols, :])
            du = (slope * mm_t(dz, w2_ref[cols, :])).astype(BF16)
            back = back + mm_t(du, w1_ref[:, cols])
            g2_ref[cols, :] += mm(hidden.T, dz)
            g1_ref[:, cols] += mm(second_t, du)
            gb1_ref[:, cols] += jnp.sum(du.astype(F32), axis=0, keepdims=True)
        y_ref[here, :] = ((middle + gate2 * branch) * weight).astype(BF16)
        dmid = cot + norm_back(normed, inverse, back * (1.0 + scale2))
        dm_ref[here, :] = dmid
        datt = (gate1 * dmid).astype(BF16)
        dout = mm_t(datt, wout_ref[...]).astype(BF16)
        for n in range(HEADS // 2):
            do_ref[n, here, :] = dout[:, n * 128 : (n + 1) * 128]
        go_ref[...] += mm(merged.T, datt)
        sums = [
            dmid * attended, back, back * normed, cot * branch, dz.astype(F32), datt.astype(F32),
        ]
        for n, value in enumerate(sums):
            small_ref[n : n + 1, :] += jnp.sum(value, axis=0, keepdims=True)
        return carry

    lax.fori_loop(0, rows // size, step, 0)
    copies.start(dm_ref, dm_out)
    copies.start(do_ref, do_out)
    copies.start(y_ref.at[pl.ds(0, own)], y_full_out)
    copies.start(y_ref.at[pl.ds(own, rows - own)], y_slot_out)
    put = halves_writer(side_ref, keep_ref, send_ref)
    for n in range(4):
        put(n * D, g1_ref[:, n * D : (n + 1) * D])
    put(FF, g2_ref[...])
    put(2 * FF, go_ref[...])
    base = 2 * FF + D
    heads = [gb1_ref[:, n * D : (n + 1) * D] for n in range(4)]
    heads += [small_ref[4:5, :], small_ref[5:6, :], jnp.zeros((10, D), F32)]
    put(base, jnp.concatenate(heads, axis=0))
    put(base + 16, extra_ref[...])
    copies.wait()


def attend_back(own, q_ref, k_ref, v_ref, mask_ref, o_ref, lse_ref, do_ref, where_ref, outs, sums):
    dq_ref, dk_ref, dv_ref, tab_ref = outs
    dkt_ref, dvt_ref = sums
    rows = q_ref.shape[1]
    spans = [(at, size, False) for at, size in blocks_of(0, own, 256)]
    spans += [(at, size, True) for at, size in blocks_of(own, rows - own, 256)]
    dkt_ref[...] = jnp.zeros(dkt_ref.shape, F32)
    dvt_ref[...] = jnp.zeros(dvt_ref.shape, F32)
    tab_ref[...] = jnp.zeros(tab_ref.shape, F32)
    for at, size, masked in spans:
        place_t = place_onehot(where_ref[at : at + size, :], turned=True).T
        dqs, tabs = [], []
        for side in range(2):
            lanes = slice(side * HDIM, (side + 1) * HDIM)
            query = q_ref[side, at : at + size, :]
            keys = k_ref[side]
            scores = mm_t(query, keys)
            if masked:
                scores = scores + mask_ref[0:1, :]
            weights = jnp.exp(scores - lse_ref[at : at + size, side * HDIM : side * HDIM + 1])
            grad_out = do_ref[at : at + size, lanes]
            delta = jnp.sum(grad_out.astype(F32) * o_ref[at : at + size, lanes], axis=-1, keepdims=True)
            dp = mm_t(grad_out, v_ref[side, :, :HDIM])
            ds = (weights * (dp - delta)).astype(BF16)
            found = mm(ds, keys)
            dqs.append(found[:, :HDIM] * (1.0 / math.sqrt(HDIM)))
            tabs.append(found[:, HDIM:].astype(BF16))
            dkt_ref[lanes, :] += mm(query[:, :HDIM].T, ds)
            dvt_ref[lanes, :] += mm(grad_out.T, weights.astype(BF16))
        dq_ref[at : at + size, :] = jnp.concatenate(dqs, axis=1).astype(BF16)
        tab_ref[...] += mm(place_t, jnp.concatenate(tabs, axis=1))
    dk_ref[...] = dkt_ref[...].astype(BF16).T
    dv_ref[...] = dvt_ref[...].astype(BF16).T


def first_back_kernel(
    own, mask_ref, where_ref, *refs,
):
    sources, refs = refs[:6], refs[6:]
    tab_ref, dq_out, dk_out, dv_out, refs = *refs[:4], refs[4:]
    local, refs = refs[:6], refs[6:]
    dq_ref, dk_ref, dv_ref, dkt_ref, dvt_ref, sems = refs
    copies = Copies(sems)
    for source, target in zip(sources, local):
        copies.start(source.at[pl.ds(0, target.shape[0])], target)
    copies.wait()
    q_ref, k_ref, v_ref, o_ref, lse_ref, do_ref = local
    outs = dq_ref.at[0], dk_ref.at[0], dv_ref.at[0], tab_ref.at[0]
    attend_back(
        own, q_ref, k_ref, v_ref, mask_ref, o_ref.at[0], lse_ref.at[0], do_ref.at[0], where_ref, outs,
        (dkt_ref, dvt_ref),
    )
    copies = Copies(sems)
    copies.start(dq_ref, dq_out)
    copies.start(dk_ref, dk_out)
    copies.start(dv_ref, dv_out)
    copies.wait()


def rest_back_kernel(
    own, everyone, scalar_ref, q_ref, k_ref, v_ref, o_ref, lse_ref, do_ref, mask_ref, where_ref, picked_ref, mod_ref,
    prior_ref, tab0_ref, *refs,
):
    sources, refs = refs[:9], refs[9:]
    keep_ref, send_ref, dx_ref, dx_own_ref, refs = *refs[:4], refs[4:]
    local, refs = refs[:9], refs[9:]
    dq_ref, dk_ref, dv_ref, tab_ref, dxs_ref, dkt_ref, dvt_ref, sems = refs
    tok_ref, a_ref, x_ref, slot_ref, weight_ref, dm_ref, dq0_ref, dk0_ref, dv0_ref = local
    step = pl.program_id(0)
    last = pl.num_programs(0) - 1

    def copies():
        return [
            pltpu.make_async_copy(source, target, sems.at[n])
            for n, (source, target) in enumerate(zip(sources, local))
        ]

    @pl.when(step == 0)
    def fetch():
        for copy in copies():
            copy.start()

    @pl.when(step < last)
    def attention():
        outs = dq_ref.at[step], dk_ref.at[step], dv_ref.at[step], tab_ref.at[step]
        attend_back(
            own, q_ref, k_ref, v_ref, mask_ref, o_ref.at[0], lse_ref.at[0], do_ref.at[0], where_ref, outs,
            (dkt_ref, dvt_ref),
        )

    @pl.when(step == last)
    def projections():
        for copy in copies():
            copy.wait()
        groups = dq_ref.shape[0]
        total = tok_ref.shape[0]
        rows = x_ref.shape[0]
        slots = rows - own
        scale = mod_ref[1:2, :]
        here = pl.ds(pl.multiple_of(scalar_ref[1], 16), own)

        def joined(first, rest, span):
            return jnp.concatenate([first[0, span, :]] + [rest[n, span, :] for n in range(groups)], axis=1)

        every = slice(0, total)
        dk, dv = joined(dk0_ref, dk_ref, every), joined(dv0_ref, dv_ref, every)
        dq_own = joined(dq0_ref, dq_ref, slice(0, own))
        dq_slot = joined(dq0_ref, dq_ref, slice(own, rows))
        lowered_t = a_ref[...].T
        put = halves_writer(scalar_ref, keep_ref, send_ref)
        put(0, mm(a_ref[here, :].T, dq_own) + mm(slot_ref[...].T, dq_slot))
        put(D, mm(lowered_t, dk))
        put(2 * D, mm(lowered_t, dv))
        column = lambda value: jnp.sum(value.astype(F32), axis=0, keepdims=True)
        normed, inverse = norm_parts(tok_ref[...].astype(F32))
        da = mm_t(dk, weight_ref[:, D : 2 * D]) + mm_t(dv, weight_ref[:, 2 * D :])
        shift_sum, scale_sum = column(da), column(da * normed)
        dxs_ref[...] = norm_back(normed, inverse, da * (1.0 + scale))
        own_normed, own_inverse = norm_parts(x_ref[:own, :].astype(F32))
        da = mm_t(dq_own, weight_ref[:, :D])
        shift_sum, scale_sum = shift_sum + column(da), scale_sum + column(da * own_normed)
        dxs_ref[here, :] += dm_ref[:own, :] + norm_back(own_normed, own_inverse, da * (1.0 + scale))
        slot_normed, slot_inverse = norm_parts(x_ref[own:, :].astype(F32))
        da = mm_t(dq_slot, weight_ref[:, :D])
        shift_sum, scale_sum = shift_sum + column(da), scale_sum + column(da * slot_normed)
        spread = dm_ref[own:, :] + norm_back(slot_normed, slot_inverse, da * (1.0 + scale))
        chosen = (picked_ref[...] == lax.broadcasted_iota(jnp.int32, (slots, total), 1)).astype(F32)
        dxs_ref[...] += mm(chosen.astype(BF16).T, spread.astype(BF16))
        dx_own_ref[...] = dxs_ref[here, :]
        for n in range(dx_ref.shape[0]):
            dx_ref[n] = dxs_ref[pl.ds(pl.multiple_of(scalar_ref[3 + n], 16), own), :].astype(BF16)
        rel = table_sums([tab0_ref[0]] + [tab_ref[n] for n in range(groups)])
        smalls = jnp.concatenate(
            [
                shift_sum, scale_sum, prior_ref[0:4, :], column(dq_own) + column(dq_slot), column(dv),
                *rel, jnp.zeros((6, D), F32),
            ],
            axis=0,
        ).astype(BF16)
        tail = 2 * keep_ref.shape[0] - 3 * D
        row = lax.broadcasted_iota(jnp.int32, (tail, 16), 0)
        lane = lax.broadcasted_iota(jnp.int32, (tail, 16), 1)
        wanted = jnp.where(row % everyone == scalar_ref[2], row // everyone, -1)
        wanted = jnp.where(row < 6 * everyone, wanted, row - 6 * everyone + 6)
        put(3 * D, mm((lane == wanted).astype(F32).astype(BF16), smalls))


def table_sums(tabs):
    found = ([], [])
    for tab in tabs:
        for side in range(2):
            for part in range(2):
                at = 2 * side * GRID + part * GRID
                square = tab[part * GRID : (part + 1) * GRID, at : at + GRID]
                wide = jnp.concatenate([square, jnp.zeros((GRID, 128 - GRID), F32)], axis=1)
                turned = pltpu.roll(wide, 0, 1, stride=1, stride_axis=0)
                found[part].append(jnp.sum(turned, axis=0, keepdims=True)[:, : 2 * GRID])
    return [jnp.concatenate(parts, axis=1) for parts in found]


def call(kernel, outs, scratch, args, scalars=0, far=0, away=0, copies=0, micros=1, limit=32):
    scratches = [pltpu.VMEM(shape, dtype) for shape, dtype in scratch]
    if copies:
        scratches.append(pltpu.SemaphoreType.DMA((copies,)))
    return pl.pallas_call(
        kernel,
        out_shape=[jax.ShapeDtypeStruct(shape, dtype) for shape, dtype in outs[: len(outs) - away]]
        + [pltpu.HBM(shape, dtype) for shape, dtype in outs[len(outs) - away :]],
        in_specs=[smem] * scalars + [vmem] * (len(args) - scalars - far) + [hbm] * far,
        out_specs=[vmem] * (len(outs) - away) + [hbm] * away,
        scratch_shapes=scratches,
        compiler_params=pltpu.CompilerParams(vmem_limit_bytes=limit * MIB),
        cost_estimate=pl.CostEstimate(flops=micros * 10**9, bytes_accessed=MIB, transcendentals=0),
    )(*args)


def in_hbm(value):
    return pltpu.with_memory_space_constraint(value, pltpu.HBM)


def rest_back_call(own, everyone, arrays, scalars, mod, prior, firsts, tail_half):
    qaug, kaug, vaug, mixed, lse, dout, mask, where, picked, *sources = arrays
    tab0, dq0, dk0, dv0 = firsts
    sources = [*sources, dq0, dk0, dv0]
    rows, total = qaug.shape[1], kaug.shape[1]
    groups = HEADS // 2 - 1
    group = lambda n: jnp.minimum(n, groups - 1) + 1
    heads = lambda count: pl.BlockSpec((2, count, 128), lambda n: (group(n), 0, 0))
    pairs = pl.BlockSpec((1, rows, 128), lambda n: (group(n), 0, 0))
    whole = lambda value: pl.BlockSpec(value.shape, lambda n: (0,) * value.ndim)
    others = total // own - 1
    outs = [((tail_half, D), BF16), ((tail_half, D), BF16), ((others, own, D), BF16), ((own, D), F32)]
    scratch = [(value.shape, value.dtype) for value in sources]
    scratch += [
        ((groups, rows, 128), BF16), ((groups, total, 128), BF16), ((groups, total, 128), BF16),
        ((groups, 2 * GRID, 128), F32), ((total, D), F32), ((128, total), F32), ((128, total), F32),
    ]
    small = [mask, where, picked, mod, prior, tab0]
    return pl.pallas_call(
        functools.partial(rest_back_kernel, own, everyone),
        grid=(groups + 1,),
        out_shape=[jax.ShapeDtypeStruct(shape, dtype) for shape, dtype in outs[:2]]
        + [pltpu.HBM(shape, dtype) for shape, dtype in outs[2:]],
        in_specs=[smem, heads(rows), heads(total), heads(total), pairs, pairs, pairs]
        + [whole(value) for value in small]
        + [hbm] * len(sources),
        out_specs=[pl.BlockSpec(shape, lambda n, r=len(shape): (0,) * r) for shape, unused in outs],
        scratch_shapes=[pltpu.VMEM(shape, dtype) for shape, dtype in scratch]
        + [pltpu.SemaphoreType.DMA((len(sources),))],
        compiler_params=pltpu.CompilerParams(
            vmem_limit_bytes=48 * MIB, dimension_semantics=("arbitrary",)
        ),
        cost_estimate=pl.CostEstimate(flops=18 * 10**9, bytes_accessed=MIB, transcendentals=0),
    )(scalars, *map(in_hbm, (qaug, kaug, vaug, mixed, lse, dout)), *small, *map(in_hbm, sources))


def halves_reader(side_ref, mine_ref, other_ref):
    half = mine_ref.shape[0]

    def get(at, count):
        found = []
        for which in range(2):
            first, last = max(at, which * half), min(at + count, (which + 1) * half)
            if first < last:
                span = slice(first - which * half, last - which * half)
                found.append(jnp.where(side_ref[0] == which, mine_ref[span, :], other_ref[span, :]))
        return found[0] if len(found) == 1 else jnp.concatenate(found, axis=0)

    return get


def layer_kernel(side_ref, mine_ref, other_ref, info_ref, small_ref, g1_out, g2_out, go_out, g1_ref, g2_ref, go_ref, sems):
    get = halves_reader(side_ref, mine_ref, other_ref)
    copies = Copies(sems)
    for n in range(4):
        cols = pl.ds(n * D, D)
        g1_ref[:, cols] = get(n * D, D).astype(F32)
        copies.start(g1_ref.at[:, cols], g1_out.at[:, cols])
        g2_ref[cols, :] = get(FF + n * D, D).astype(F32)
        copies.start(g2_ref.at[cols], g2_out.at[cols])
    go_ref[...] = get(2 * FF, D).astype(F32)
    copies.start(go_ref, go_out)
    base = 2 * FF + D
    small_ref[...] = get(base, 16).astype(F32)[:8]
    info_ref[...] = get(base + 16, info_ref.shape[0])
    copies.wait()


def last_kernel(
    everyone, side_ref, mine_ref, other_ref, info_ref, ada_ref, small_ref, bias_ref,
    gqkv_out, gada_out, table_out, gqkv_ref, gada_ref, table_ref, sems,
):
    get = halves_reader(side_ref, mine_ref, other_ref)
    copies = Copies(sems)
    act_t = info_ref[:everyone, :].T
    back = jnp.zeros((everyone, D), F32)
    for n in range(6):
        cols = pl.ds(n * D, D)
        dmod = get(3 * D + n * everyone, everyone)
        gada_ref[:, cols] = mm(act_t, dmod)
        copies.start(gada_ref.at[:, cols], gada_out.at[:, cols])
        bias_ref[n : n + 1, :] = jnp.sum(dmod.astype(F32), axis=0, keepdims=True)
        back = back + mm_t(dmod, ada_ref[:, cols])
    for n in range(3):
        cols = pl.ds(n * D, D)
        gqkv_ref[:, cols] = get(n * D, D).astype(F32)
        copies.start(gqkv_ref.at[:, cols], gqkv_out.at[:, cols])
    cond = info_ref[everyone : 2 * everyone, :].astype(F32) * back
    high = cond.astype(BF16)
    low = (cond - high.astype(F32)).astype(BF16)
    digits = info_ref[2 * everyone : 3 * everyone, :].astype(F32)
    label = (digits[:, 0:1] * GRID + digits[:, 1:2]).astype(jnp.int32)
    classes = table_ref.shape[0]
    wide = round_up(classes, 128)
    hot = (label == lax.broadcasted_iota(jnp.int32, (everyone, wide), 1)).astype(F32).astype(BF16).T
    table_ref[...] = (mm(hot, high) + mm(hot, low))[:classes]
    copies.start(table_ref, table_out)
    small_ref[...] = get(3 * D + 6 * everyone, 16).astype(F32)[:8]
    copies.wait()


def swap_cores(value, dp):
    return lax.ppermute(value, "dp", [(n, n ^ 1) for n in range(dp)])


def exchange(value, dp, seq):
    groups = [
        [(far * (dp // 2) + 2 * pair + core) * seq + at for pair in range(dp // 4) for at in range(seq)]
        for far in range(2)
        for core in range(2)
    ]
    return lax.all_to_all(value, AXES, 0, 0, axis_index_groups=groups)


def sum_pieces(pieces, dp):
    near = jnp.sum(pieces.astype(F32), axis=0).astype(BF16)
    far = lax.ppermute(near, "dp", [(n, (n + dp // 2) % dp) for n in range(dp)])
    return (near.astype(F32) + far.astype(F32)).astype(BF16)


def spread_out(chunk, dp, seq):
    peers = dp // 4 * seq
    return exchange(jnp.broadcast_to(chunk[None], (peers,) + chunk.shape), dp, seq).reshape(-1, D)


def scatter_rows(partial, seq):
    return [
        lax.ppermute(partial[step - 1], "seq", [(n, (n + step) % seq) for n in range(seq)])
        for step in range(1, seq)
    ]


def time_features(moments):
    half_width = D // 2
    frequency = jnp.exp(-math.log(10000.0) * jnp.arange(half_width, dtype=F32) / half_width)
    angles = moments.astype(F32)[:, None] * frequency[None, :]
    return jnp.concatenate([jnp.cos(angles), jnp.sin(angles)], axis=-1)


def offset_hot():
    first = jnp.arange(GRID, dtype=jnp.int32)
    offsets = first[None, :] - first[:, None] + GRID - 1
    return (offsets[..., None] == jnp.arange(2 * GRID - 1, dtype=jnp.int32)).astype(F32)


def bias_table(rel_bias):
    both = jnp.einsum("cho,ijo->cihj", rel_bias.astype(F32), offset_hot(), precision=highest)
    empty = jnp.zeros_like(both[0])
    top = jnp.concatenate([both[0], empty], axis=-1)
    low = jnp.concatenate([empty, both[1]], axis=-1)
    return jnp.concatenate([top, low], axis=0).reshape(2 * GRID, HEADS * 2 * GRID).astype(BF16)


def body(
    dp, seq, image_tokens, kept_index, kept_count, sample_valid, timestep, class_label, class_table,
    ada_weight, ada_bias, qkv_weight, qv_bias, rel_bias, out_weight, out_bias, fc1_weight,
    fc1_bias, fc2_weight, fc2_bias, grad_full, grad_masked,
):
    samples, own, width = image_tokens.shape
    held = kept_index.shape[1]
    slots = grad_masked.shape[1]
    padded = round_up(slots, 16)
    rows = own + padded
    total = own * seq
    everyone = dp * samples
    classes = class_table.shape[0]
    dp_place, seq_place = lax.axis_index("dp"), lax.axis_index("seq")

    conditioned = jnp.take(class_table, class_label, axis=0).astype(F32) + time_features(timestep)
    gate = jax.nn.sigmoid(conditioned)
    activated = (conditioned * gate).astype(BF16)
    slope = gate * (1.0 + conditioned * (1.0 - gate))
    modulation = jnp.dot(activated, ada_weight, preferred_element_type=F32) + ada_bias.astype(F32)
    modulation = jnp.pad(modulation.reshape(samples, 6, D), ((0, 0), (0, 2), (0, 0)))
    table = bias_table(rel_bias)
    valid = sample_valid.astype(F32)

    digits = jnp.stack([class_label // GRID, class_label % GRID], axis=1).astype(F32)
    digits = jnp.pad(digits, ((0, 0), (0, D - 2)))
    info = jnp.stack([activated.astype(F32), slope, digits], axis=0)
    info = info * (seq_place == 0).astype(F32)
    extra_rows = round_up(2 * FF + D + 16 + 3 * everyone, dp * seq * 8) - (2 * FF + D + 16)
    spread = (jnp.arange(everyone)[:, None] == dp_place * samples + jnp.arange(samples)[None, :])
    info = jnp.einsum("es,nsd->end", spread.astype(F32), info, precision=highest)
    info = info.transpose(1, 0, 2).reshape(3 * everyone, D).astype(BF16)
    info = jnp.pad(info, ((0, extra_rows - 3 * everyone), (0, 0)))

    slot_numbers = jnp.arange(held, dtype=jnp.int32)
    live_all = slot_numbers[None, :] < kept_count[:, None]
    slot_start = seq_place * slots
    peers = dp // 4 * seq
    side = dp_place % 2
    sides = side.astype(jnp.int32).reshape(1)
    half = (2 * FF + D + 16 + extra_rows) // 2
    tail_half = round_up(3 * D + 16 + 6 * everyone, dp * seq * 8) // 2
    starts = ((seq_place - jnp.arange(seq, dtype=jnp.int32)) % seq * own).astype(jnp.int32)
    block = blocks_of(0, rows, 432)[0][1]

    kept_of = []
    for s in range(samples):
        tokens = [image_tokens[s]]
        for step in range(1, seq):
            tokens.append(lax.ppermute(tokens[0], "seq", [(n, (n + step) % seq) for n in range(seq)]))
        kept = jnp.where(live_all[s], kept_index[s], -1)[:, None]
        picked = lax.dynamic_slice_in_dim(kept_index[s], slot_start, slots, 0)
        live = lax.dynamic_slice_in_dim(live_all[s], slot_start, slots, 0)
        picked = jnp.pad(picked, (0, padded - slots))[:, None]
        where = jnp.concatenate([starts[0] + jnp.arange(own, dtype=jnp.int32), picked[:, 0]])[:, None]
        weight = valid[s] * jnp.concatenate(
            [jnp.ones((own,), F32), jnp.pad(live.astype(F32), (0, padded - slots))]
        )
        cot = jnp.concatenate([grad_full[s], jnp.pad(grad_masked[s], ((0, padded - slots), (0, 0)))])
        qaug, kaug, vaug, x, mask, lowered, whole, slot = call(
            functools.partial(prep_kernel, own, seq),
            [
                ((HEADS, rows, 128), BF16), ((HEADS, total, 128), BF16), ((HEADS, total, 128), BF16),
                ((rows, D), BF16), ((8, total), F32),
                ((total, D), BF16), ((total, D), BF16), ((padded, D), BF16),
            ],
            [((total, D), BF16), ((total, D), BF16), ((total, D), BF16), ((padded, D), BF16)],
            [starts, *tokens, kept, picked, where, modulation[s], qkv_weight, qv_bias.astype(F32), table],
            scalars=1, away=3, copies=3, micros=5,
        )
        mixed, lse, qaug_far, kaug_far, vaug_far = call(
            functools.partial(attend_kernel, own),
            [
                ((HEADS // 2, rows, 128), F32), ((HEADS // 2, rows, 128), F32),
                (qaug.shape, BF16), (kaug.shape, BF16), (vaug.shape, BF16),
            ],
            [],
            [qaug, kaug, vaug, mask],
            away=3, copies=3, micros=12,
        )
        dout, small, keep, send, y_full, y_slot, dmid, mixed_far, lse_far, x_far, dout_far = call(
            functools.partial(feed_kernel, block, own),
            [
                ((HEADS // 2, rows, 128), BF16), ((8, D), F32), ((half, D), BF16), ((half, D), BF16),
                ((own, D), BF16), ((padded, D), BF16), ((rows, D), F32), (mixed.shape, F32),
                (lse.shape, F32), (x.shape, BF16), ((HEADS // 2, rows, 128), BF16),
            ],
            [
                ((rows, D), BF16), ((rows, D), F32),
                ((D, FF), F32), ((FF, D), F32), ((D, D), F32), ((1, FF), F32),
            ],
            [
                sides, mixed, lse, x, cot, weight[:, None], modulation[s],
                out_weight, out_bias.astype(F32)[None], fc1_weight, fc1_bias.astype(F32)[None],
                fc2_weight, fc2_bias.astype(F32)[None], info if s == 0 else jnp.zeros_like(info),
            ],
            scalars=1, away=7, copies=7, micros=14,
        )
        kept_of.append(dict(
            mask=mask, where=where,
            far=[
                qaug_far, kaug_far, vaug_far, mixed_far, lse_far, dout_far, mask, where, picked,
                whole, lowered, x_far, slot, qkv_weight, dmid,
            ],
            y_full=y_full, y_slot=y_slot, small=small, keep=keep, send=send,
        ))

    def added(arrays):
        if len(arrays) == 1:
            return arrays[0]
        return functools.reduce(jnp.add, [a.astype(F32) for a in arrays]).astype(arrays[0].dtype)

    keep, send = added([k["keep"] for k in kept_of]), added([k["send"] for k in kept_of])
    got = swap_cores(send, dp)

    firsts = [
        call(
            functools.partial(first_back_kernel, own),
            [
                ((1, 2 * GRID, 128), F32),
                ((1, rows, 128), BF16), ((1, total, 128), BF16), ((1, total, 128), BF16),
            ],
            [
                ((2, rows, 128), BF16), ((2, total, 128), BF16), ((2, total, 128), BF16),
                ((1, rows, 128), F32), ((1, rows, 128), F32), ((1, rows, 128), BF16),
                ((1, rows, 128), BF16), ((1, total, 128), BF16), ((1, total, 128), BF16),
                ((128, total), F32), ((128, total), F32),
            ],
            [k["mask"], k["where"], *map(in_hbm, k["far"][:6])],
            away=3, copies=6, far=6, micros=6,
        )
        for k in kept_of
    ]
    mine = (keep.astype(F32) + got.astype(F32)).astype(BF16)
    mine, firsts = lax.optimization_barrier((mine, firsts))
    pieces = exchange(mine.reshape(peers, half // peers, D), dp, seq)
    tails = []
    for number, (k, first) in enumerate(zip(kept_of, firsts)):
        place = (dp_place * samples + number).astype(jnp.int32)
        others = (seq_place + jnp.arange(1, seq, dtype=jnp.int32)) % seq * own
        scalars = jnp.concatenate([jnp.stack([sides[0], starts[0], place]), others.astype(jnp.int32)])
        tails.append(
            rest_back_call(own, everyone, k["far"], scalars, modulation[number], k["small"], first, tail_half)
        )

    keep, send = added([t[0] for t in tails]), added([t[1] for t in tails])
    got = swap_cores(send, dp)
    mine = (keep.astype(F32) + got.astype(F32)).astype(BF16).reshape(peers, tail_half // peers, D)
    mine, pieces = lax.optimization_barrier((mine, pieces))
    chunk = sum_pieces(pieces, dp)
    last_chunk = sum_pieces(exchange(mine, dp, seq), dp)
    moved = [scatter_rows(t[2], seq) for t in tails]
    layer_half = spread_out(chunk, dp, seq)
    layer_half, last_chunk, moved = lax.optimization_barrier((layer_half, last_chunk, moved))
    last_half = spread_out(last_chunk, dp, seq)
    grad_input = jnp.stack(
        [t[3] + functools.reduce(jnp.add, [m.astype(F32) for m in came]) for t, came in zip(tails, moved)]
    )
    out_full = jnp.stack([k["y_full"] for k in kept_of])
    out_masked = jnp.stack([k["y_slot"][:slots] for k in kept_of])
    info, layer_small, grad_fc1, grad_fc2, grad_out = call(
        layer_kernel,
        [((extra_rows, D), BF16), ((8, D), F32), ((D, FF), F32), ((FF, D), F32), ((D, D), F32)],
        [((D, FF), F32), ((FF, D), F32), ((D, D), F32)],
        [sides, layer_half, swap_cores(layer_half, dp)],
        scalars=1, away=3, copies=9, micros=3,
    )
    last_half, info, layer_small = lax.optimization_barrier((last_half, info, layer_small))
    grad_fc1_bias = layer_small[:4].reshape(FF)
    grad_fc2_bias, grad_out_bias = layer_small[4], layer_small[5]
    last_small, ada_small, grad_qkv, grad_ada, grad_table = call(
        functools.partial(last_kernel, everyone),
        [((8, D), F32), ((8, D), F32), ((D, 3 * D), F32), ((D, 6 * D), F32), ((classes, D), F32)],
        [((D, 3 * D), F32), ((D, 6 * D), F32), ((classes, D), F32)],
        [sides, last_half, swap_cores(last_half, dp), info, ada_weight],
        scalars=1, away=3, copies=10, micros=4,
    )
    grad_qv = last_small[:2]
    grad_rel = last_small[2:4].reshape(2, HEADS, 2 * GRID)[:, :, : 2 * GRID - 1]
    grad_ada_bias = ada_small[:6].reshape(6 * D)
    return (
        out_full, out_masked, grad_input, grad_table, grad_ada, grad_ada_bias, grad_qkv, grad_qv,
        grad_rel, grad_out, grad_out_bias, grad_fc1, grad_fc1_bias, grad_fc2, grad_fc2_bias,
    )


def solution(mesh):
    split = P("dp", "seq", None)
    placed = (split, P("dp", None)) + (P("dp"),) * 4 + (P(),) * 12 + (split, split)
    return jax.shard_map(
        functools.partial(body, mesh.shape["dp"], mesh.shape["seq"]),
        mesh=mesh,
        in_specs=placed,
        out_specs=(split,) * 3 + (P(),) * 12,
        check_vma=False,
    )
```

```python
import functools
import math

import jax
import jax.numpy as jnp
from jax import lax
from jax.experimental import pallas as pl
from jax.experimental.pallas import tpu as pltpu
from jax.sharding import PartitionSpec as P

D = 384
HEADS = 6
HDIM = 64
GRID = 32
FF = 1536
CHUNK = 256

AXES = ("dp", "seq")
F32 = jnp.float32
BF16 = jnp.bfloat16
MIB = 1024 * 1024
GELU_A = math.sqrt(2.0 / math.pi)
GELU_B = 0.044715

highest = lax.Precision.HIGHEST
big_negative = -1e30
vmem = pl.BlockSpec(memory_space=pltpu.VMEM)
smem = pl.BlockSpec(memory_space=pltpu.SMEM)
hbm = pl.BlockSpec(memory_space=pltpu.HBM)


def round_up(value, step):
    return -(-value // step) * step


def blocks_of(first, count, most):
    pieces = -(-count // most)
    size = round_up(-(-count // pieces), 16)
    found = []
    at = 0
    while at < count:
        found.append((first + at, min(size, count - at)))
        at += size
    return found


def mm(left, right):
    return lax.dot_general(left, right, (((1,), (0,)), ((), ())), preferred_element_type=F32)


def mm_t(left, right):
    return lax.dot_general(left, right, (((1,), (1,)), ((), ())), preferred_element_type=F32)


def norm_parts(value):
    average = jnp.mean(value, axis=-1, keepdims=True)
    centred = value - average
    variance = jnp.mean(centred * centred, axis=-1, keepdims=True)
    inverse = lax.rsqrt(variance + 1e-06)
    return (centred * inverse, inverse)


def norm_back(normed, inverse, grad):
    first = jnp.mean(grad, axis=-1, keepdims=True)
    second = jnp.mean(grad * normed, axis=-1, keepdims=True)
    return inverse * (grad - first - normed * second)


def place_onehot(position, turned=False):
    lane = lax.broadcasted_iota(jnp.int32, (position.shape[0], 2 * GRID), 1)
    if turned:
        lane = jnp.where(lane < GRID, GRID - 1 - lane, 3 * GRID - 1 - lane)
    wanted = jnp.where(lane < GRID, position // GRID, position % GRID + GRID)
    return (lane == wanted).astype(F32).astype(BF16)


class Copies:
    def __init__(self, sems):
        self.sems, self.made = sems, []

    def start(self, source, target):
        copy = pltpu.make_async_copy(source, target, self.sems.at[len(self.made)])
        copy.start()
        self.made.append(copy)

    def wait(self):
        for copy in self.made:
            copy.wait()


def split_halves(copies, side, payload_ref, keep_ref, send_ref):
    half = keep_ref.shape[0]
    for which, target in ((side, keep_ref), (1 - side, send_ref)):
        copies.start(payload_ref.at[pl.ds(pl.multiple_of(which * half, 16), half)], target)


def prep_kernel(
    own, seq, starts_ref, *refs,
):
    token_refs, refs = refs[:seq], refs[seq:]
    kept_ref, picked_ref, where_ref, mod_ref, weight_ref, qv_ref, table_ref = refs[:7]
    qaug_ref, kaug_ref, vaug_ref, x_ref, mask_ref, a_out, tok_out, slot_out = refs[7:15]
    qs_ref, a_ref, tok_ref, slot_ref, sems = refs[15:]
    copies = Copies(sems)
    total = own * seq
    slots = picked_ref.shape[0]
    for n in range(seq):
        tok_ref[pl.ds(pl.multiple_of(starts_ref[n], 16), own), :] = token_refs[n][...]
    copies.start(tok_ref, tok_out)
    shift, scale = mod_ref[0:1, :], mod_ref[1:2, :]
    normed, unused = norm_parts(tok_ref[...].astype(F32))
    lowered = (normed * (1.0 + scale) + shift).astype(BF16)
    a_ref[...] = lowered
    copies.start(a_ref, a_out)
    query = (mm(lowered, weight_ref[:, :D]) + qv_ref[0:1, :]).astype(BF16)
    scaled = (query.astype(F32) * (1.0 / math.sqrt(HDIM))).astype(BF16)
    qs_ref[...] = scaled
    keys = mm(lowered, weight_ref[:, D : 2 * D]).astype(BF16)
    values = (mm(lowered, weight_ref[:, 2 * D :]) + qv_ref[1:2, :]).astype(BF16)
    key_place = place_onehot(lax.broadcasted_iota(jnp.int32, (total, 1), 0))
    lane = lax.broadcasted_iota(jnp.int32, (total, HDIM), 1)
    ones = (lane < 2).astype(F32).astype(BF16)
    for head in range(HEADS):
        cols = slice(head * HDIM, (head + 1) * HDIM)
        kaug_ref[head] = jnp.concatenate([keys[:, cols], key_place], axis=1)
        vaug_ref[head] = jnp.concatenate([values[:, cols], ones], axis=1)
    chosen = (picked_ref[...] == lax.broadcasted_iota(jnp.int32, (slots, total), 1)).astype(F32)
    chosen = chosen.astype(BF16)
    x_ref[:own, :] = token_refs[0][...]
    x_ref[own:, :] = mm(chosen, tok_ref[...]).astype(BF16)
    slot_ref[...] = mm(chosen, lowered).astype(BF16)
    copies.start(slot_ref, slot_out)
    slot_query = mm(chosen, scaled).astype(BF16)
    own_query = qs_ref[pl.ds(pl.multiple_of(starts_ref[0], 16), own), :]
    offsets = mm(place_onehot(where_ref[...]), table_ref[...]).astype(BF16)
    for head in range(HEADS):
        cols = slice(head * HDIM, (head + 1) * HDIM)
        qaug_ref[head, :own] = jnp.concatenate([own_query[:, cols], offsets[:own, cols]], axis=1)
        qaug_ref[head, own:] = jnp.concatenate([slot_query[:, cols], offsets[own:, cols]], axis=1)
    held = kept_ref.shape[0]
    hit = kept_ref[...] == lax.broadcasted_iota(jnp.int32, (held, total), 1)
    count = jnp.sum(hit.astype(F32), axis=0, keepdims=True)
    mask_ref[...] = jnp.broadcast_to(jnp.where(count > 0.0, 0.0, big_negative), mask_ref.shape)
    copies.wait()


def attend_kernel(
    own, qaug_ref, kaug_ref, vaug_ref, mask_ref, o_ref, inverse_ref, e_out, qaug_out, kaug_out, vaug_out, e_ref, sems
):
    rows = qaug_ref.shape[1]
    copies = Copies(sems)
    copies.start(qaug_ref, qaug_out)
    copies.start(kaug_ref, kaug_out)
    copies.start(vaug_ref, vaug_out)
    spans = [(at, size, False) for at, size in blocks_of(0, own, 256)]
    spans += [(at, size, True) for at, size in blocks_of(own, rows - own, 256)]

    def pair(group, carry):
        items = [(side, *span) for side in range(2) for span in spans]
        scores, spread = {}, {}
        for n in range(len(items) + 2):
            if n < len(items):
                side, at, size, masked = items[n]
                head = 2 * group + side
                scores[n] = mm_t(qaug_ref[head, at : at + size, :], kaug_ref[head])
                if masked:
                    scores[n] = scores[n] + mask_ref[0:1, :]
            if 0 <= n - 1 < len(items):
                side, at, size, masked = items[n - 1]
                found = scores.pop(n - 1)
                spread[n - 1] = jnp.exp(found - jnp.max(found, axis=-1, keepdims=True)).astype(BF16)
                e_ref[2 * group + side, at : at + size, :] = spread[n - 1]
            if 0 <= n - 2:
                side, at, size, masked = items[n - 2]
                mixed = mm(spread.pop(n - 2), vaug_ref[2 * group + side])
                inverse = 1.0 / mixed[:, HDIM : HDIM + 1]
                lanes = slice(side * HDIM, (side + 1) * HDIM)
                o_ref[group, at : at + size, lanes] = mixed[:, :HDIM] * inverse
                inverse_ref[group, at : at + size, lanes] = jnp.broadcast_to(inverse, (size, HDIM))
        pltpu.make_async_copy(e_ref.at[pl.ds(2 * group, 2)], e_out.at[pl.ds(2 * group, 2)], sems.at[3 + group]).start()
        return carry

    lax.fori_loop(0, HEADS // 2, pair, 0)
    for group in range(HEADS // 2):
        heads = pl.ds(2 * group, 2)
        pltpu.make_async_copy(e_ref.at[heads], e_out.at[heads], sems.at[3 + group]).wait()
    copies.wait()


def feed_kernel(
    side_ref, o_ref, x_ref, cot_ref, wgt_ref, mod_ref, wout_ref, bout_ref, w1_ref, b1_ref, w2_ref, extra_ref,
    att_ref, hidden_ref, du_ref, keep_ref, send_ref, pay_ref, sems,
):
    rows = x_ref.shape[0]
    gate1, shift2, scale2, gate2 = [mod_ref[n : n + 1, :] for n in range(2, 6)]
    merged = jnp.concatenate([o_ref[n] for n in range(HEADS // 2)], axis=1).astype(BF16)
    attended = mm(merged, wout_ref[...]) + bout_ref[...]
    att_ref[...] = attended
    normed, unused = norm_parts(x_ref[...].astype(F32) + gate1 * attended)
    second = (normed * (1.0 + scale2) + shift2).astype(BF16)
    dz = (gate2 * (cot_ref[...].astype(F32) * wgt_ref[...])).astype(BF16)

    def products(c):
        cols = slice(c * CHUNK, (c + 1) * CHUNK)
        return mm(second, w1_ref[:, cols]) + b1_ref[:, cols], mm_t(dz, w2_ref[cols, :])

    chunks = FF // CHUNK
    ready = products(0)
    for c in range(chunks):
        u, back_u = ready
        if c + 1 < chunks:
            ready = products(c + 1)
        cols = slice(c * CHUNK, (c + 1) * CHUNK)
        square = u * u
        t = jnp.tanh(u * (square * (GELU_A * GELU_B) + GELU_A))
        cdf = t * 0.5 + 0.5
        hidden_ref[:, cols] = (u * cdf).astype(BF16)
        slope = cdf * ((1.0 - t) * (u * (square * (3.0 * GELU_A * GELU_B) + GELU_A)) + 1.0)
        du_ref[:, cols] = (slope * back_u).astype(BF16)
    ones = jnp.ones((16, rows), BF16)
    grad = mm(jnp.concatenate([second.T, ones], axis=0), du_ref[...])
    heads = []
    for n in range(4):
        cols = slice(n * D, (n + 1) * D)
        pay_ref[cols, :] = grad[:D, cols].astype(BF16)
        heads.append(grad[D : D + 1, cols])
    pay_ref[FF : 2 * FF, :] = mm(hidden_ref[...].T, dz).astype(BF16)
    heads += [jnp.sum(dz.astype(F32), axis=0, keepdims=True), jnp.zeros((11, D), F32)]
    pay_ref[2 * FF : 2 * FF + 16, :] = jnp.concatenate(heads, axis=0).astype(BF16)
    pay_ref[2 * FF + 16 :, :] = extra_ref[...]
    copies = Copies(sems)
    split_halves(copies, side_ref[0], pay_ref, keep_ref, send_ref)
    copies.wait()


def feed_rest_kernel(
    own, o_ref, inverse_ref, x_ref, cot_ref, wgt_ref, mod_ref, wout_ref, w1_ref, w2_ref, b2_ref,
    att_ref, hidden_ref, du_ref,
    small_ref, y_full_out, y_slot_out, dm_out, x_out, do_out, go_out, y_ref, dm_ref, do_ref, go_ref, sems,
):
    rows = x_ref.shape[0]
    copies = Copies(sems)
    copies.start(x_ref, x_out)
    gate1, shift2, scale2, gate2 = [mod_ref[n : n + 1, :] for n in range(2, 6)]
    weight = wgt_ref[...]
    back = mm_t(du_ref[...], w1_ref[...])
    branch = mm(hidden_ref[...], w2_ref[...]) + b2_ref[...]
    attended = att_ref[...]
    middle = x_ref[...].astype(F32) + gate1 * attended
    normed, inverse = norm_parts(middle)
    cot = cot_ref[...].astype(F32) * weight
    y_ref[...] = ((middle + gate2 * branch) * weight).astype(BF16)
    copies.start(y_ref.at[pl.ds(0, own)], y_full_out)
    copies.start(y_ref.at[pl.ds(own, rows - own)], y_slot_out)
    dmid = cot + norm_back(normed, inverse, back * (1.0 + scale2))
    dm_ref[...] = dmid
    copies.start(dm_ref, dm_out)
    datt = (gate1 * dmid).astype(BF16)
    merged_f = jnp.concatenate([o_ref[n] for n in range(HEADS // 2)], axis=1)
    dout = mm_t(datt, wout_ref[...]) * jnp.concatenate([inverse_ref[n] for n in range(HEADS // 2)], axis=1)
    dout = dout.astype(BF16).astype(F32)
    product = dout * merged_f
    high = product.astype(BF16)
    low = (product - high.astype(F32)).astype(BF16)
    row = lax.broadcasted_iota(jnp.int32, (D, 128), 0)
    lane = lax.broadcasted_iota(jnp.int32, (D, 128), 1)
    heads = jnp.where(row // HDIM == lane // 2, -1.0, 0.0).astype(BF16)
    less = mm(high, heads) + mm(low, heads)
    lane = lax.broadcasted_iota(jnp.int32, (rows, 128), 1)
    kept = less.astype(BF16).astype(F32)
    pair = jnp.where(lane % 2 == 0, kept, less - kept)
    for head in range(HEADS):
        tile = dout[:, head // 2 * 128 : (head // 2 + 1) * 128]
        if head % 2:
            tile = pltpu.roll(tile, HDIM, 1)
        more = pltpu.roll(pair, HDIM - 2 * head, 1)
        more = jnp.where(lane < HDIM + 2, more, 0.0)
        do_ref[head] = jnp.where(lane < HDIM, tile, more).astype(BF16)
    copies.start(do_ref, do_out)
    go_ref[...] = mm(merged_f.astype(BF16).T, datt).astype(BF16)
    copies.start(go_ref, go_out)
    column = lambda value: jnp.sum(value.astype(F32), axis=0, keepdims=True)
    sums = [dmid * attended, back, back * normed, cot * branch, datt]
    small_ref[...] = jnp.concatenate([column(value) for value in sums] + [jnp.zeros((3, D), F32)], axis=0)
    copies.wait()


def attend_back(own, e_ref, q_ref, k_ref, v_ref, do_ref, place_ref, outs, sums):
    dq_ref, dk_ref, dv_ref, tab_ref = outs
    dkt_ref, dvt_ref, part_ref = sums
    rows = q_ref.shape[1]
    spans = blocks_of(0, own, 256) + blocks_of(own, rows - own, 256)
    items = [(side, *span) for side in range(2) for span in spans]
    grads, found = {}, {}
    for n in range(len(items) + 2):
        if n < len(items):
            side, at, size = items[n]
            grads[n] = mm_t(do_ref[side, at : at + size, :], v_ref[side])
        if 0 <= n - 1 < len(items):
            side, at, size = items[n - 1]
            found[n - 1] = (e_ref[side, at : at + size, :].astype(F32) * grads.pop(n - 1)).astype(BF16)
        if 0 <= n - 2:
            side, at, size = items[n - 2]
            lanes = slice(side * HDIM, (side + 1) * HDIM)
            ds = found.pop(n - 2)
            dq = mm(ds, k_ref[side])
            dq_ref[at : at + size, lanes] = (dq[:, :HDIM] * (1.0 / math.sqrt(HDIM))).astype(BF16)
            part_ref[at : at + size, lanes] = dq[:, HDIM:].astype(BF16)
            dkt = mm(q_ref[side, at : at + size, :HDIM].T, ds)
            dvt = mm(do_ref[side, at : at + size, :HDIM].T, e_ref[side, at : at + size, :])
            if at == 0:
                dkt_ref[lanes, :] = dkt
                dvt_ref[lanes, :] = dvt
            else:
                dkt_ref[lanes, :] += dkt
                dvt_ref[lanes, :] += dvt
    tab_ref[...] = mm(place_ref[...], part_ref[...])
    dk_ref[...] = dkt_ref[...].astype(BF16).T
    dv_ref[...] = dvt_ref[...].astype(BF16).T


def back_kernel(own, everyone, scalar_ref, where_ref, picked_ref, mod_ref, prior_ref, *refs):
    group_sources, refs = refs[:5], refs[5:]
    sources, refs = refs[:7], refs[7:]
    keep_ref, send_ref, dx_ref, dx_own_ref, refs = *refs[:4], refs[4:]
    group_local, refs = refs[:5], refs[5:]
    local, refs = refs[:7], refs[7:]
    dq_ref, dk_ref, dv_ref, tab_ref, normed_ref, inverse_ref, dxs_ref, dkt_ref, dvt_ref, pay_ref = refs[:10]
    place_ref, part_ref, group_sems, sems, pay_sems = refs[10:]
    tok_ref, a_ref, x_ref, slot_ref, weight_ref, dm_ref, go_ref = local
    step = pl.program_id(0)
    last = pl.num_programs(0) - 1
    slot = step % 2

    def fetches(group, place):
        return [
            pltpu.make_async_copy(source.at[pl.ds(2 * group, 2)], target.at[place], group_sems.at[place, n])
            for n, (source, target) in enumerate(zip(group_sources, group_local))
        ]

    def copies():
        return [
            pltpu.make_async_copy(source, target, sems.at[n])
            for n, (source, target) in enumerate(zip(sources, local))
        ]

    @pl.when(step == 0)
    def first():
        whole = copies()
        whole[0].start()
        for copy in fetches(0, 0):
            copy.start()
        for copy in whole[1:]:
            copy.start()
        for copy in fetches(1, 1):
            copy.start()
        place_ref[...] = place_onehot(where_ref[...], turned=True).T
        whole[0].wait()
        normed, inverse = norm_parts(tok_ref[...].astype(F32))
        normed_ref[...] = normed
        inverse_ref[...] = jnp.broadcast_to(inverse, inverse_ref.shape)

    @pl.when((step > 0) & (step + 1 < last))
    def following():
        for copy in fetches(step + 1, 1 - slot):
            copy.start()

    @pl.when(step < last)
    def attention():
        for copy in fetches(step, slot):
            copy.wait()
        outs = dq_ref.at[step], dk_ref.at[step], dv_ref.at[step], tab_ref.at[step]
        attend_back(own, *[ref.at[slot] for ref in group_local], place_ref, outs, (dkt_ref, dvt_ref, part_ref))

    @pl.when(step == last)
    def projections():
        for copy in copies()[1:]:
            copy.wait()
        groups = dq_ref.shape[0]
        total = tok_ref.shape[0]
        rows = x_ref.shape[0]
        slots = rows - own
        scale = mod_ref[1:2, :]
        here = pl.ds(pl.multiple_of(scalar_ref[1], 16), own)

        def joined(ref, span):
            return jnp.concatenate([ref[n, span, :] for n in range(groups)], axis=1)

        every = slice(0, total)
        dk, dv = joined(dk_ref, every), joined(dv_ref, every)
        dq_own, dq_slot = joined(dq_ref, slice(0, own)), joined(dq_ref, slice(own, rows))
        column = lambda value: jnp.sum(value.astype(F32), axis=0, keepdims=True)
        lowered_t = a_ref[...].T
        pay_ref[0:D, :] = (mm(a_ref[here, :].T, dq_own) + mm(slot_ref[...].T, dq_slot)).astype(BF16)
        pay_ref[D : 2 * D, :] = mm(lowered_t, dk).astype(BF16)
        pay_ref[2 * D : 3 * D, :] = mm(lowered_t, dv).astype(BF16)
        pay_ref[3 * D : 4 * D, :] = go_ref[...]
        slot_normed, slot_inverse = norm_parts(x_ref[own:, :].astype(F32))
        da = mm_t(dq_slot, weight_ref[:, :D])
        shift_sum, scale_sum = column(da), column(da * slot_normed)
        spread = dm_ref[own:, :] + norm_back(slot_normed, slot_inverse, da * (1.0 + scale))
        chosen = (picked_ref[...] == lax.broadcasted_iota(jnp.int32, (slots, total), 1)).astype(F32)
        moved = mm(chosen.astype(BF16).T, spread.astype(BF16))
        dxs_ref[...] = mm_t(dk, weight_ref[:, D : 2 * D]) + mm_t(dv, weight_ref[:, 2 * D :])
        dxs_ref[here, :] += mm_t(dq_own, weight_ref[:, :D])
        da = dxs_ref[...]
        normed = normed_ref[...]
        shift_sum, scale_sum = shift_sum + column(da), scale_sum + column(da * normed)
        inverse = jnp.concatenate([inverse_ref[...]] * (D // 128), axis=1)
        dxs_ref[...] = moved + norm_back(normed, inverse, da * (1.0 + scale))
        dx_own_ref[...] = dxs_ref[here, :] + dm_ref[:own, :]
        for n in range(dx_ref.shape[0]):
            dx_ref[n] = dxs_ref[pl.ds(pl.multiple_of(scalar_ref[3 + n], 16), own), :].astype(BF16)
        rel = table_sums([tab_ref[n] for n in range(groups)])
        smalls = jnp.concatenate(
            [
                shift_sum, scale_sum, prior_ref[0:4, :], column(dq_own) + column(dq_slot), column(dv),
                *rel, prior_ref[4:5, :], jnp.zeros((5, D), F32),
            ],
            axis=0,
        ).astype(BF16)
        tail = pay_ref.shape[0] - 4 * D
        row = lax.broadcasted_iota(jnp.int32, (tail, 16), 0)
        lane = lax.broadcasted_iota(jnp.int32, (tail, 16), 1)
        wanted = jnp.where(row % everyone == scalar_ref[2], row // everyone, -1)
        wanted = jnp.where(row < 6 * everyone, wanted, row - 6 * everyone + 6)
        pay_ref[4 * D :, :] = mm((lane == wanted).astype(F32).astype(BF16), smalls).astype(BF16)
        halves = Copies(pay_sems)
        split_halves(halves, scalar_ref[0], pay_ref, keep_ref, send_ref)
        halves.wait()


def table_sums(tabs):
    found = ([], [])
    for tab in tabs:
        for side in range(2):
            for part in range(2):
                at = 2 * side * GRID + part * GRID
                square = tab[part * GRID : (part + 1) * GRID, at : at + GRID]
                wide = jnp.concatenate([square, jnp.zeros((GRID, 128 - GRID), F32)], axis=1)
                turned = pltpu.roll(wide, 0, 1, stride=1, stride_axis=0)
                found[part].append(jnp.sum(turned, axis=0, keepdims=True)[:, : 2 * GRID])
    return [jnp.concatenate(parts, axis=1) for parts in found]


def call(kernel, outs, scratch, args, scalars=0, far=0, away=0, copies=0, micros=1, limit=32):
    scratches = [pltpu.VMEM(shape, dtype) for shape, dtype in scratch]
    if copies:
        scratches.append(pltpu.SemaphoreType.DMA((copies,)))
    return pl.pallas_call(
        kernel,
        out_shape=[jax.ShapeDtypeStruct(shape, dtype) for shape, dtype in outs[: len(outs) - away]]
        + [pltpu.HBM(shape, dtype) for shape, dtype in outs[len(outs) - away :]],
        in_specs=[smem] * scalars + [vmem] * (len(args) - scalars - far) + [hbm] * far,
        out_specs=[vmem] * (len(outs) - away) + [hbm] * away,
        scratch_shapes=scratches,
        compiler_params=pltpu.CompilerParams(vmem_limit_bytes=limit * MIB),
        cost_estimate=pl.CostEstimate(flops=micros * 10**9, bytes_accessed=MIB, transcendentals=0),
    )(*args)


def in_hbm(value):
    return pltpu.with_memory_space_constraint(value, pltpu.HBM)


def add_kernel(left_ref, right_ref, sum_ref):
    sum_ref[...] = (left_ref[...].astype(F32) + right_ref[...].astype(F32)).astype(BF16)


def add_call(left, right, micros):
    return call(add_kernel, [(left.shape, BF16)], [], [left, right], micros=micros)[0]


def back_call(own, everyone, groups_of, sources, scalars, where, picked, mod, prior, tail_half):
    rows, total = groups_of[1].shape[1], groups_of[2].shape[1]
    groups = HEADS // 2
    others = total // own - 1
    whole = lambda shape: pl.BlockSpec(shape, lambda n: (0,) * len(shape))
    outs = [((tail_half, D), BF16), ((tail_half, D), BF16), ((others, own, D), BF16), ((own, D), F32)]
    scratch = [((2, 2) + value.shape[1:], value.dtype) for value in groups_of]
    scratch += [(value.shape, value.dtype) for value in sources]
    scratch += [
        ((groups, rows, 128), BF16), ((groups, total, 128), BF16), ((groups, total, 128), BF16),
        ((groups, 2 * GRID, 128), F32), ((total, D), F32), ((total, 128), F32), ((total, D), F32),
        ((128, total), F32), ((128, total), F32), ((2 * tail_half, D), BF16),
        ((2 * GRID, rows), BF16), ((rows, 128), BF16),
    ]
    small = [where, picked, mod, prior]
    return pl.pallas_call(
        functools.partial(back_kernel, own, everyone),
        grid=(groups + 1,),
        out_shape=[jax.ShapeDtypeStruct(shape, dtype) for shape, dtype in outs[:2]]
        + [pltpu.HBM(shape, dtype) for shape, dtype in outs[2:]],
        in_specs=[smem] + [whole(value.shape) for value in small] + [hbm] * (len(groups_of) + len(sources)),
        out_specs=[vmem, vmem] + [whole(shape) for shape, unused in outs[2:]],
        scratch_shapes=[pltpu.VMEM(shape, dtype) for shape, dtype in scratch]
        + [pltpu.SemaphoreType.DMA((2, 5)), pltpu.SemaphoreType.DMA((7,)), pltpu.SemaphoreType.DMA((2,))],
        compiler_params=pltpu.CompilerParams(
            vmem_limit_bytes=48 * MIB, dimension_semantics=("arbitrary",)
        ),
        cost_estimate=pl.CostEstimate(flops=18 * 10**9, bytes_accessed=MIB, transcendentals=0),
    )(scalars, *small, *map(in_hbm, groups_of), *map(in_hbm, sources))


def halves_reader(side_ref, mine_ref, other_ref):
    half = mine_ref.shape[0]

    def get(at, count):
        found = []
        for which in range(2):
            first, last = max(at, which * half), min(at + count, (which + 1) * half)
            if first < last:
                span = slice(first - which * half, last - which * half)
                found.append(jnp.where(side_ref[0] == which, mine_ref[span, :], other_ref[span, :]))
        return found[0] if len(found) == 1 else jnp.concatenate(found, axis=0)

    return get


def layer_kernel(side_ref, mine_ref, other_ref, info_ref, small_ref, g1_out, g2_out, g1_ref, g2_ref, sems):
    get = halves_reader(side_ref, mine_ref, other_ref)
    copies = Copies(sems)
    for n in range(4):
        cols = pl.ds(n * D, D)
        g1_ref[:, cols] = get(n * D, D).astype(F32)
        copies.start(g1_ref.at[:, cols], g1_out.at[:, cols])
        g2_ref[cols, :] = get(FF + n * D, D).astype(F32)
        copies.start(g2_ref.at[cols], g2_out.at[cols])
    small_ref[...] = get(2 * FF, 16).astype(F32)[:8]
    info_ref[...] = get(2 * FF + 16, info_ref.shape[0])
    copies.wait()


def last_kernel(
    everyone, side_ref, mine_ref, other_ref, info_ref, ada_ref, qv_ref, rel_ref, out_bias_ref, ada_bias_ref,
    gqkv_out, gada_out, table_out, go_out, gqkv_ref, gada_ref, table_ref, go_ref, sems,
):
    get = halves_reader(side_ref, mine_ref, other_ref)
    copies = Copies(sems)
    act_t = info_ref[:everyone, :].T
    back = jnp.zeros((everyone, D), F32)
    for n in range(6):
        cols = pl.ds(n * D, D)
        dmod = get(4 * D + n * everyone, everyone)
        gada_ref[:, cols] = mm(act_t, dmod)
        copies.start(gada_ref.at[:, cols], gada_out.at[:, cols])
        ada_bias_ref[cols] = jnp.sum(dmod.astype(F32), axis=0)
        back = back + mm_t(dmod, ada_ref[:, cols])
    for n in range(3):
        cols = pl.ds(n * D, D)
        gqkv_ref[:, cols] = get(n * D, D).astype(F32)
        copies.start(gqkv_ref.at[:, cols], gqkv_out.at[:, cols])
    go_ref[...] = get(3 * D, D).astype(F32)
    copies.start(go_ref, go_out)
    cond = info_ref[everyone : 2 * everyone, :].astype(F32) * back
    high = cond.astype(BF16)
    low = (cond - high.astype(F32)).astype(BF16)
    digits = info_ref[2 * everyone : 3 * everyone, :].astype(F32)
    label = (digits[:, 0:1] * GRID + digits[:, 1:2]).astype(jnp.int32)
    classes = table_ref.shape[0]
    wide = round_up(classes, 128)
    hot = (label == lax.broadcasted_iota(jnp.int32, (everyone, wide), 1)).astype(F32).astype(BF16).T
    table_ref[...] = (mm(hot, high) + mm(hot, low))[:classes]
    copies.start(table_ref, table_out)
    small = get(4 * D + 6 * everyone, 16).astype(F32)
    qv_ref[...] = small[:2]
    for part in range(2):
        for head in range(HEADS):
            at = 2 * GRID * head
            rel_ref[part, head : head + 1, :] = small[2 + part : 3 + part, at : at + 2 * GRID - 1]
    out_bias_ref[...] = small[4]
    copies.wait()


def swap_cores(value, dp):
    return lax.ppermute(value, "dp", [(n, n ^ 1) for n in range(dp)])


def exchange(value, dp, seq):
    groups = [
        [(far * (dp // 2) + 2 * pair + core) * seq + at for pair in range(dp // 4) for at in range(seq)]
        for far in range(2)
        for core in range(2)
    ]
    return lax.all_to_all(value, AXES, 0, 0, axis_index_groups=groups)


def sum_pieces(pieces, dp):
    near = jnp.sum(pieces.astype(F32), axis=0).astype(BF16)
    far = lax.ppermute(near, "dp", [(n, (n + dp // 2) % dp) for n in range(dp)])
    return (near.astype(F32) + far.astype(F32)).astype(BF16)


def spread_out(chunk, dp, seq):
    peers = dp // 4 * seq
    return exchange(jnp.broadcast_to(chunk[None], (peers,) + chunk.shape), dp, seq).reshape(-1, D)


def scatter_rows(partial, seq):
    return [
        lax.ppermute(partial[step - 1], "seq", [(n, (n + step) % seq) for n in range(seq)])
        for step in range(1, seq)
    ]


def time_features(moments):
    half_width = D // 2
    frequency = jnp.exp(-math.log(10000.0) * jnp.arange(half_width, dtype=F32) / half_width)
    angles = moments.astype(F32)[:, None] * frequency[None, :]
    return jnp.concatenate([jnp.cos(angles), jnp.sin(angles)], axis=-1)


def offset_hot():
    first = jnp.arange(GRID, dtype=jnp.int32)
    offsets = first[None, :] - first[:, None] + GRID - 1
    return (offsets[..., None] == jnp.arange(2 * GRID - 1, dtype=jnp.int32)).astype(F32)


def bias_table(rel_bias):
    both = jnp.einsum("cho,ijo->cihj", rel_bias.astype(F32), offset_hot(), precision=highest)
    empty = jnp.zeros_like(both[0])
    top = jnp.concatenate([both[0], empty], axis=-1)
    low = jnp.concatenate([empty, both[1]], axis=-1)
    return jnp.concatenate([top, low], axis=0).reshape(2 * GRID, HEADS * 2 * GRID).astype(BF16)


def body(
    dp, seq, image_tokens, kept_index, kept_count, sample_valid, timestep, class_label, class_table,
    ada_weight, ada_bias, qkv_weight, qv_bias, rel_bias, out_weight, out_bias, fc1_weight,
    fc1_bias, fc2_weight, fc2_bias, grad_full, grad_masked,
):
    samples, own, width = image_tokens.shape
    held = kept_index.shape[1]
    slots = grad_masked.shape[1]
    padded = round_up(slots, 16)
    rows = own + padded
    total = own * seq
    everyone = dp * samples
    classes = class_table.shape[0]
    dp_place, seq_place = lax.axis_index("dp"), lax.axis_index("seq")

    conditioned = jnp.take(class_table, class_label, axis=0).astype(F32) + time_features(timestep)
    gate = jax.nn.sigmoid(conditioned)
    activated = (conditioned * gate).astype(BF16)
    slope = gate * (1.0 + conditioned * (1.0 - gate))
    modulation = jnp.dot(activated, ada_weight, preferred_element_type=F32) + ada_bias.astype(F32)
    modulation = jnp.pad(modulation.reshape(samples, 6, D), ((0, 0), (0, 2), (0, 0)))
    table = bias_table(rel_bias)
    valid = sample_valid.astype(F32)

    digits = jnp.stack([class_label // GRID, class_label % GRID], axis=1).astype(F32)
    digits = jnp.pad(digits, ((0, 0), (0, D - 2)))
    info = jnp.stack([activated.astype(F32), slope, digits], axis=0)
    info = info * (seq_place == 0).astype(F32)
    extra_rows = round_up(2 * FF + 16 + 3 * everyone, dp * seq * 4) - (2 * FF + 16)
    spread = (jnp.arange(everyone)[:, None] == dp_place * samples + jnp.arange(samples)[None, :])
    info = jnp.einsum("es,nsd->end", spread.astype(F32), info, precision=highest)
    info = info.transpose(1, 0, 2).reshape(3 * everyone, D).astype(BF16)
    info = jnp.pad(info, ((0, extra_rows - 3 * everyone), (0, 0)))

    slot_numbers = jnp.arange(held, dtype=jnp.int32)
    live_all = slot_numbers[None, :] < kept_count[:, None]
    slot_start = seq_place * slots
    peers = dp // 4 * seq
    side = dp_place % 2
    sides = side.astype(jnp.int32).reshape(1)
    half = (2 * FF + 16 + extra_rows) // 2
    tail_half = round_up(4 * D + 16 + 6 * everyone, dp * seq * 4) // 2
    starts = ((seq_place - jnp.arange(seq, dtype=jnp.int32)) % seq * own).astype(jnp.int32)

    kept_of = []
    for s in range(samples):
        tokens = [image_tokens[s]]
        for step in range(1, seq):
            tokens.append(lax.ppermute(tokens[0], "seq", [(n, (n + step) % seq) for n in range(seq)]))
        kept = jnp.where(live_all[s], kept_index[s], -1)[:, None]
        picked = lax.dynamic_slice_in_dim(kept_index[s], slot_start, slots, 0)
        live = lax.dynamic_slice_in_dim(live_all[s], slot_start, slots, 0)
        picked = jnp.pad(picked, (0, padded - slots))[:, None]
        where = jnp.concatenate([starts[0] + jnp.arange(own, dtype=jnp.int32), picked[:, 0]])[:, None]
        weight = valid[s] * jnp.concatenate(
            [jnp.ones((own,), F32), jnp.pad(live.astype(F32), (0, padded - slots))]
        )
        cot = jnp.concatenate([grad_full[s], jnp.pad(grad_masked[s], ((0, padded - slots), (0, 0)))])
        qaug, kaug, vaug, x, mask, lowered, whole, slot = call(
            functools.partial(prep_kernel, own, seq),
            [
                ((HEADS, rows, 128), BF16), ((HEADS, total, 128), BF16), ((HEADS, total, 128), BF16),
                ((rows, D), BF16), ((8, total), F32),
                ((total, D), BF16), ((total, D), BF16), ((padded, D), BF16),
            ],
            [((total, D), BF16), ((total, D), BF16), ((total, D), BF16), ((padded, D), BF16)],
            [starts, *tokens, kept, picked, where, modulation[s], qkv_weight, qv_bias.astype(F32), table],
            scalars=1, away=3, copies=3, micros=5,
        )
        mixed, inverse, spread_far, qaug_far, kaug_far, vaug_far = call(
            functools.partial(attend_kernel, own),
            [
                ((HEADS // 2, rows, 128), F32), ((HEADS // 2, rows, 128), F32),
                ((HEADS, rows, total), BF16), (qaug.shape, BF16), (kaug.shape, BF16), (vaug.shape, BF16),
            ],
            [((HEADS, rows, total), BF16)],
            [qaug, kaug, vaug, mask],
            away=4, copies=3 + HEADS, micros=10, limit=40,
        )
        attended, hidden, du, keep, send = call(
            feed_kernel,
            [((rows, D), F32), ((rows, FF), BF16), ((rows, FF), BF16), ((half, D), BF16), ((half, D), BF16)],
            [((2 * half, D), BF16)],
            [
                sides, mixed, x, cot, weight[:, None], modulation[s], out_weight, out_bias.astype(F32)[None],
                fc1_weight, fc1_bias.astype(F32)[None], fc2_weight, info if s == 0 else jnp.zeros_like(info),
            ],
            scalars=1, copies=2, micros=10, limit=32,
        )
        kept_of.append(dict(
            rest=[
                mixed, inverse, x, cot, weight[:, None], modulation[s], out_weight, fc1_weight, fc2_weight,
                fc2_bias.astype(F32)[None], attended, hidden, du,
            ],
            groups=[spread_far, qaug_far, kaug_far, vaug_far], sources=[whole, lowered, slot, qkv_weight],
            where=where, picked=picked, keep=keep, send=send,
        ))

    def added(arrays):
        if len(arrays) == 1:
            return arrays[0]
        return functools.reduce(jnp.add, [a.astype(F32) for a in arrays]).astype(arrays[0].dtype)

    keep, send = added([k["keep"] for k in kept_of]), added([k["send"] for k in kept_of])
    got = swap_cores(send, dp)

    rests = [
        call(
            functools.partial(feed_rest_kernel, own),
            [
                ((8, D), F32), ((own, D), BF16), ((padded, D), BF16), ((rows, D), F32), ((rows, D), BF16),
                ((HEADS, rows, 128), BF16), ((D, D), BF16),
            ],
            [((rows, D), BF16), ((rows, D), F32), ((HEADS, rows, 128), BF16), ((D, D), BF16)],
            k["rest"],
            away=6, copies=6, micros=6, limit=32,
        )
        for k in kept_of
    ]
    mine = (keep.astype(F32) + got.astype(F32)).astype(BF16)
    mine, rests = lax.optimization_barrier((mine, rests))
    pieces = exchange(mine.reshape(peers, half // peers, D), dp, seq)
    tails = []
    for number, (k, rest) in enumerate(zip(kept_of, rests)):
        small, unused_full, unused_slot, dmid, x_far, dout_far, grad_out = rest
        place = (dp_place * samples + number).astype(jnp.int32)
        others = (seq_place + jnp.arange(1, seq, dtype=jnp.int32)) % seq * own
        scalars = jnp.concatenate([jnp.stack([sides[0], starts[0], place]), others.astype(jnp.int32)])
        whole, lowered, slot, weights = k["sources"]
        tails.append(
            back_call(
                own, everyone, [*k["groups"], dout_far], [whole, lowered, x_far, slot, weights, dmid, grad_out],
                scalars, k["where"], k["picked"], modulation[number], small, tail_half,
            )
        )

    keep, send = added([t[0] for t in tails]), added([t[1] for t in tails])
    keep, send, pieces = lax.optimization_barrier((keep, send, pieces))
    got = swap_cores(send, dp)
    mine = add_call(keep, got, 30).reshape(peers, tail_half // peers, D)
    chunk = sum_pieces(pieces, dp)
    last_chunk = sum_pieces(exchange(mine, dp, seq), dp)
    moved = [scatter_rows(t[2], seq) for t in tails]
    chunk, moved = lax.optimization_barrier((chunk, moved))
    layer_half = spread_out(chunk, dp, seq)
    layer_half, last_chunk = lax.optimization_barrier((layer_half, last_chunk))
    last_half = spread_out(last_chunk, dp, seq)
    grad_input = jnp.stack(
        [t[3] + functools.reduce(jnp.add, [m.astype(F32) for m in came]) for t, came in zip(tails, moved)]
    )
    out_full = jnp.stack([rest[1] for rest in rests])
    out_masked = jnp.stack([rest[2][:slots] for rest in rests])
    info, layer_small, grad_fc1, grad_fc2 = call(
        layer_kernel,
        [((extra_rows, D), BF16), ((8, D), F32), ((D, FF), F32), ((FF, D), F32)],
        [((D, FF), F32), ((FF, D), F32)],
        [sides, layer_half, swap_cores(layer_half, dp)],
        scalars=1, away=2, copies=8, micros=3,
    )
    grad_fc1_bias = layer_small[:4].reshape(FF)
    grad_fc2_bias = layer_small[4]
    last_half, info, grad_fc1_bias, grad_fc2_bias, grad_input = lax.optimization_barrier(
        (last_half, info, grad_fc1_bias, grad_fc2_bias, grad_input)
    )
    grad_qv, grad_rel, grad_out_bias, grad_ada_bias, grad_qkv, grad_ada, grad_table, grad_out = call(
        functools.partial(last_kernel, everyone),
        [
            ((2, D), F32), ((2, HEADS, 2 * GRID - 1), F32), ((D,), F32), ((6 * D,), F32),
            ((D, 3 * D), F32), ((D, 6 * D), F32), ((classes, D), F32), ((D, D), F32),
        ],
        [((D, 3 * D), F32), ((D, 6 * D), F32), ((classes, D), F32), ((D, D), F32)],
        [sides, last_half, swap_cores(last_half, dp), info, ada_weight],
        scalars=1, away=4, copies=11, micros=4, limit=16,
    )
    return (
        out_full, out_masked, grad_input, grad_table, grad_ada, grad_ada_bias, grad_qkv, grad_qv,
        grad_rel, grad_out, grad_out_bias, grad_fc1, grad_fc1_bias, grad_fc2, grad_fc2_bias,
    )


def solution(mesh):
    split = P("dp", "seq", None)
    placed = (split, P("dp", None)) + (P("dp"),) * 4 + (P(),) * 12 + (split, split)
    return jax.shard_map(
        functools.partial(body, mesh.shape["dp"], mesh.shape["seq"]),
        mesh=mesh,
        in_specs=placed,
        out_specs=(split,) * 3 + (P(),) * 12,
        check_vma=False,
    )
```

```python
import functools
import math

import jax
import jax.numpy as jnp
from jax import lax
from jax.experimental import pallas as pl
from jax.experimental.pallas import tpu as pltpu
from jax.sharding import PartitionSpec as P

D = 384
HEADS = 6
HDIM = 64
GRID = 32
FF = 1536
CHUNK = 256

AXES = ("dp", "seq")
F32 = jnp.float32
BF16 = jnp.bfloat16
MIB = 1024 * 1024
GELU_A = math.sqrt(2.0 / math.pi)
GELU_B = 0.044715

highest = lax.Precision.HIGHEST
big_negative = -1e30
vmem = pl.BlockSpec(memory_space=pltpu.VMEM)
smem = pl.BlockSpec(memory_space=pltpu.SMEM)
hbm = pl.BlockSpec(memory_space=pltpu.HBM)


def round_up(value, step):
    return -(-value // step) * step


def blocks_of(first, count, most):
    pieces = -(-count // most)
    size = round_up(-(-count // pieces), 16)
    found = []
    at = 0
    while at < count:
        found.append((first + at, min(size, count - at)))
        at += size
    return found


def mm(left, right):
    return lax.dot_general(left, right, (((1,), (0,)), ((), ())), preferred_element_type=F32)


def mm_t(left, right):
    return lax.dot_general(left, right, (((1,), (1,)), ((), ())), preferred_element_type=F32)


def norm_parts(value):
    average = jnp.mean(value, axis=-1, keepdims=True)
    centred = value - average
    variance = jnp.mean(centred * centred, axis=-1, keepdims=True)
    inverse = lax.rsqrt(variance + 1e-06)
    return (centred * inverse, inverse)


def norm_back(normed, inverse, grad):
    first = jnp.mean(grad, axis=-1, keepdims=True)
    second = jnp.mean(grad * normed, axis=-1, keepdims=True)
    return inverse * (grad - first - normed * second)


def place_onehot(position, turned=False):
    lane = lax.broadcasted_iota(jnp.int32, (position.shape[0], 2 * GRID), 1)
    if turned:
        lane = jnp.where(lane < GRID, GRID - 1 - lane, 3 * GRID - 1 - lane)
    wanted = jnp.where(lane < GRID, position // GRID, position % GRID + GRID)
    return (lane == wanted).astype(F32).astype(BF16)


class Copies:
    def __init__(self, sems):
        self.sems, self.made, self.count = sems, [], 0

    def start(self, source, target):
        copy = pltpu.make_async_copy(source, target, self.sems.at[self.count])
        copy.start()
        self.made.append(copy)
        self.count += 1

    def wait(self):
        for copy in self.made:
            copy.wait()


def split_halves(copies, side, payload_ref, keep_ref, send_ref):
    half = keep_ref.shape[0]
    for which, target in ((side, keep_ref), (1 - side, send_ref)):
        copies.start(payload_ref.at[pl.ds(pl.multiple_of(which * half, 16), half)], target)


SIDE, PLACE, SLOT_START, COUNT, VALID, LABEL, SEQ_PLACE, STARTS = range(8)


def row_span(scalar_ref, number, count):
    return pl.ds(pl.multiple_of(scalar_ref[number], 16), count)


def slot_places(scalar_ref, kept_ref, slots):
    return kept_ref[pl.ds(pl.multiple_of(scalar_ref[SLOT_START], 8), slots), :]


def row_places(scalar_ref, kept_ref, own, slots):
    mine = lax.broadcasted_iota(jnp.int32, (own, 1), 0) + scalar_ref[STARTS]
    return jnp.concatenate([mine, slot_places(scalar_ref, kept_ref, slots)], axis=0)


def row_weights(scalar_ref, own, slots, rows):
    row = lax.broadcasted_iota(jnp.int32, (rows, 1), 0)
    kept = (row < own + slots) & (row - own + scalar_ref[SLOT_START] < scalar_ref[COUNT])
    return jnp.where((row < own) | kept, scalar_ref[VALID], 0).astype(F32)


def project(tokens, mod_ref, weight_ref, line_ref):
    normed, unused = norm_parts(tokens.astype(F32))
    lowered = (normed * (1.0 + mod_ref[1:2, :]) + mod_ref[0:1, :]).astype(BF16)
    query = (mm(lowered, weight_ref[:, :D]) + line_ref[QV_LINE : QV_LINE + 1, :]).astype(BF16)
    scaled = (query.astype(F32) * (1.0 / math.sqrt(HDIM))).astype(BF16)
    keys = mm(lowered, weight_ref[:, D : 2 * D]).astype(BF16)
    values = (mm(lowered, weight_ref[:, 2 * D :]) + line_ref[QV_LINE + 1 : QV_LINE + 2, :]).astype(BF16)
    return lowered, scaled, keys, values


def head_cols(head):
    return slice(head * HDIM, (head + 1) * HDIM)


def ones_lanes(count):
    return (lax.broadcasted_iota(jnp.int32, (count, HDIM), 1) < 2).astype(F32).astype(BF16)


def bias_table(rel_ref):
    lane = lax.broadcasted_iota(jnp.int32, (GRID, 128), 1)
    parts = []
    for part in range(2):
        tiles = []
        for group in range(HEADS // 2):
            tile = jnp.zeros((GRID, 128), F32)
            for side in range(2):
                head = 2 * group + side
                line = rel_ref[head, part : part + 1, :].astype(F32)
                line = jnp.concatenate([line, jnp.zeros((1, 128 - line.shape[1]), F32)], axis=1)
                first = side * HDIM + part * GRID
                turned = pltpu.roll(
                    jnp.broadcast_to(line, (GRID, 128)), (first + 128 - (GRID - 1)) % 128, 1,
                    stride=1, stride_axis=0,
                )
                tile = jnp.where((lane >= first) & (lane < first + GRID), turned, tile)
            tiles.append(tile)
        parts.append(jnp.concatenate(tiles, axis=1))
    return jnp.concatenate(parts, axis=0).astype(BF16)


QV_LINE, OUT_LINE, FC1_LINE, FC2_LINE = 6, 8, 9, 13


def time_features(moment):
    half = D // 2
    lane = lax.broadcasted_iota(jnp.int32, (1, D), 1)
    number = jnp.where(lane < half, lane, lane - half).astype(F32)
    angle = moment.astype(F32) * jnp.exp(-math.log(10000.0) * number / half)
    return jnp.where(lane < half, jnp.cos(angle), jnp.sin(angle))


def own_kernel(
    start_ref, count_ref, valid_ref, moment_ref, label_ref,
    *refs,
):
    sources, outs, local, sems = refs[:11], refs[11:23], refs[23:34], refs[34]
    scalar_ref, kept_ref, fact_ref, line_ref, mod_ref, a_ref, qs_ref, qaug_ref, kaug_ref, vaug_ref = outs[:10]
    offset_ref, mask_ref = outs[10:]
    kept_in, rel_ref, ada_bias_ref, qv_bias_ref, out_bias_ref, fc1_bias_ref, fc2_bias_ref = local[:7]
    table_ref, ada_ref, tok_ref, weight_ref = local[7:]
    fetched = [pltpu.make_async_copy(*pair, sems.at[n]) for n, pair in enumerate(zip(sources, local))]
    for copy in fetched:
        copy.start()
    for copy in fetched[:7]:
        copy.wait()
    own = tok_ref.shape[0]
    slots = offset_ref.shape[0]
    total = mask_ref.shape[1]
    held = kept_ref.shape[0]
    label = label_ref[0]
    for n in range(scalar_ref.shape[0]):
        scalar_ref[n] = start_ref[n]
    scalar_ref[COUNT] = count_ref[0]
    scalar_ref[VALID] = valid_ref[0]
    scalar_ref[LABEL] = label
    width = round_up(held, 128)
    kept = jnp.concatenate([kept_in[...], jnp.zeros((1, width - kept_in.shape[1]), jnp.int32)], axis=1)
    kept_ref[...] = jnp.broadcast_to(kept, (8, width)).T[:held, :1]
    place = place_onehot(row_places(start_ref, kept_ref, own, slots))
    offsets = mm(place, bias_table(rel_ref)).astype(BF16)
    offset_ref[...] = offsets[own:]
    number = lax.broadcasted_iota(jnp.int32, (held, 1), 0)
    live = jnp.where(number < count_ref[0], kept_ref[...], -1)
    hit = live == lax.broadcasted_iota(jnp.int32, (held, total), 1)
    count = jnp.sum(hit.astype(F32), axis=0, keepdims=True)
    mask_ref[...] = jnp.broadcast_to(jnp.where(count > 0.0, 0.0, big_negative), mask_ref.shape)
    for n in range(6):
        line_ref[n : n + 1, :] = ada_bias_ref[pl.ds(n * D, D)].astype(F32).reshape(1, D)
    line_ref[QV_LINE : QV_LINE + 2, :] = qv_bias_ref[...].astype(F32)
    line_ref[OUT_LINE : OUT_LINE + 1, :] = out_bias_ref[...].astype(F32).reshape(1, D)
    for n in range(4):
        line_ref[FC1_LINE + n : FC1_LINE + n + 1, :] = fc1_bias_ref[pl.ds(n * D, D)].astype(F32).reshape(1, D)
    line_ref[FC2_LINE : FC2_LINE + 1, :] = fc2_bias_ref[...].astype(F32).reshape(1, D)
    line_ref[FC2_LINE + 1 :, :] = jnp.zeros((2, D), F32)
    for copy in fetched[7:]:
        copy.wait()
    hot = lax.broadcasted_iota(jnp.int32, (16, table_ref.shape[0]), 1) == label
    conditioned = mm(hot.astype(F32).astype(BF16), table_ref[...]) + time_features(moment_ref[0])
    gate = 1.0 / (1.0 + jnp.exp(-conditioned))
    activated = (conditioned * gate).astype(BF16)
    line = lax.broadcasted_iota(jnp.int32, (16, D), 0)
    slope = gate * (1.0 + conditioned * (1.0 - gate))
    fact_ref[...] = jnp.where(line == 0, activated.astype(F32), jnp.where(line == 1, slope, 0.0)).astype(BF16)
    for n in range(6):
        mod_ref[n : n + 1, :] = mm(activated, ada_ref[:, n * D : (n + 1) * D])[:1] + line_ref[n : n + 1, :]
    mod_ref[6:8, :] = jnp.zeros((2, D), F32)
    lowered, scaled, keys, values = project(tok_ref[...], mod_ref, weight_ref, line_ref)
    a_ref[...] = lowered
    qs_ref[...] = scaled
    for head in range(HEADS):
        cols = head_cols(head)
        qaug_ref[head] = jnp.concatenate([scaled[:, cols], offsets[:own, cols]], axis=1)
        kaug_ref[head] = jnp.concatenate([keys[:, cols], place[:own]], axis=1)
        vaug_ref[head] = jnp.concatenate([values[:, cols], ones_lanes(own)], axis=1)


def prep_kernel(seq, scalar_ref, *refs):
    token_refs, refs = refs[:seq], refs[seq:]
    own_a_ref, own_qs_ref, own_qaug_ref, own_kaug_ref, own_vaug_ref, offset_ref = refs[:6]
    kept_ref, mod_ref, weight_ref, line_ref = refs[6:10]
    qaug_ref, kaug_ref, vaug_ref, x_ref, a_out, tok_out, slot_out = refs[10:17]
    qs_ref, a_ref, tok_ref, slot_ref, sems = refs[17:]
    copies = Copies(sems)
    own = token_refs[0].shape[0]
    slots, total = offset_ref.shape[0], tok_ref.shape[0]
    for n in range(seq):
        tok_ref[row_span(scalar_ref, STARTS + n, own), :] = token_refs[n][...]
    copies.start(tok_ref, tok_out)
    others = [token_refs[n][...] for n in range(1, seq)]
    others = others[0] if seq == 2 else jnp.concatenate(others, axis=0)
    lowered, scaled, keys, values = project(others, mod_ref, weight_ref, line_ref)
    here = row_span(scalar_ref, STARTS, own)
    a_ref[here, :] = own_a_ref[...]
    qs_ref[here, :] = own_qs_ref[...]
    for head in range(HEADS):
        kaug_ref[head, here, :] = own_kaug_ref[head]
        vaug_ref[head, here, :] = own_vaug_ref[head]
        qaug_ref[head, :own, :] = own_qaug_ref[head]
    for n in range(1, seq):
        there = row_span(scalar_ref, STARTS + n, own)
        span = slice((n - 1) * own, n * own)
        a_ref[there, :] = lowered[span]
        qs_ref[there, :] = scaled[span]
        place = place_onehot(lax.broadcasted_iota(jnp.int32, (own, 1), 0) + scalar_ref[STARTS + n])
        for head in range(HEADS):
            cols = head_cols(head)
            kaug_ref[head, there, :] = jnp.concatenate([keys[span, cols], place], axis=1)
            vaug_ref[head, there, :] = jnp.concatenate([values[span, cols], ones_lanes(own)], axis=1)
    copies.start(a_ref, a_out)
    chosen = slot_places(scalar_ref, kept_ref, slots) == lax.broadcasted_iota(jnp.int32, (slots, total), 1)
    chosen = chosen.astype(F32).astype(BF16)
    x_ref[:own, :] = token_refs[0][...]
    x_ref[own:, :] = mm(chosen, tok_ref[...]).astype(BF16)
    slot_ref[...] = mm(chosen, a_ref[...]).astype(BF16)
    copies.start(slot_ref, slot_out)
    query = mm(chosen, qs_ref[...]).astype(BF16)
    for head in range(HEADS):
        cols = head_cols(head)
        qaug_ref[head, own:, :] = jnp.concatenate([query[:, cols], offset_ref[:, cols]], axis=1)
    copies.wait()


def attend_kernel(
    own, qaug_ref, kaug_ref, vaug_ref, mask_ref, o_ref, inverse_ref, e_out, qaug_out, kaug_out, vaug_out, e_ref, sems
):
    rows = qaug_ref.shape[1]
    copies = Copies(sems)
    copies.start(qaug_ref, qaug_out)
    copies.start(kaug_ref, kaug_out)
    copies.start(vaug_ref, vaug_out)
    spans = [(at, size, False) for at, size in blocks_of(0, own, 256)]
    spans += [(at, size, True) for at, size in blocks_of(own, rows - own, 256)]

    def pair(group, carry):
        items = [(side, *span) for side in range(2) for span in spans]
        scores, spread = {}, {}
        for n in range(len(items) + 2):
            if n < len(items):
                side, at, size, masked = items[n]
                head = 2 * group + side
                scores[n] = mm_t(qaug_ref[head, at : at + size, :], kaug_ref[head])
                if masked:
                    scores[n] = scores[n] + mask_ref[0:1, :]
            if 0 <= n - 1 < len(items):
                side, at, size, masked = items[n - 1]
                found = scores.pop(n - 1)
                spread[n - 1] = jnp.exp(found - jnp.max(found, axis=-1, keepdims=True)).astype(BF16)
                e_ref[2 * group + side, at : at + size, :] = spread[n - 1]
            if 0 <= n - 2:
                side, at, size, masked = items[n - 2]
                mixed = mm(spread.pop(n - 2), vaug_ref[2 * group + side])
                inverse = 1.0 / mixed[:, HDIM : HDIM + 1]
                lanes = slice(side * HDIM, (side + 1) * HDIM)
                o_ref[group, at : at + size, lanes] = mixed[:, :HDIM] * inverse
                inverse_ref[group, at : at + size, lanes] = jnp.broadcast_to(inverse, (size, HDIM))
        pltpu.make_async_copy(e_ref.at[pl.ds(2 * group, 2)], e_out.at[pl.ds(2 * group, 2)], sems.at[3 + group]).start()
        return carry

    lax.fori_loop(0, HEADS // 2, pair, 0)
    for group in range(HEADS // 2):
        heads = pl.ds(2 * group, 2)
        pltpu.make_async_copy(e_ref.at[heads], e_out.at[heads], sems.at[3 + group]).wait()
    copies.wait()


def cotangents(scalar_ref, slots, full_ref, slot_ref):
    own = full_ref.shape[0]
    weight = row_weights(scalar_ref, own, slots, own + slot_ref.shape[0])
    return weight, jnp.concatenate([full_ref[...], slot_ref[...]], axis=0).astype(F32) * weight


def feed_kernel(
    slots, everyone, scalar_ref, o_ref, x_ref, cot_full_ref, cot_slot_ref, mod_ref, wout_ref, w1_ref,
    w2_ref, line_ref, fact_ref,
    att_ref, hidden_ref, du_ref, keep_ref, send_ref, pay_ref, sems,
):
    rows = x_ref.shape[0]
    gate1, shift2, scale2, gate2 = [mod_ref[n : n + 1, :] for n in range(2, 6)]
    merged = jnp.concatenate([o_ref[n] for n in range(HEADS // 2)], axis=1).astype(BF16)
    attended = mm(merged, wout_ref[...]) + line_ref[OUT_LINE : OUT_LINE + 1, :]
    att_ref[...] = attended
    normed, unused = norm_parts(x_ref[...].astype(F32) + gate1 * attended)
    second = (normed * (1.0 + scale2) + shift2).astype(BF16)
    unused, cot = cotangents(scalar_ref, slots, cot_full_ref, cot_slot_ref)
    dz = (gate2 * cot).astype(BF16)

    bias = jnp.concatenate([line_ref[FC1_LINE + n : FC1_LINE + n + 1, :] for n in range(4)], axis=1)

    def products(c):
        cols = slice(c * CHUNK, (c + 1) * CHUNK)
        return mm(second, w1_ref[:, cols]) + bias[:, cols], mm_t(dz, w2_ref[cols, :])

    chunks = FF // CHUNK
    ready = products(0)
    for c in range(chunks):
        u, back_u = ready
        if c + 1 < chunks:
            ready = products(c + 1)
        cols = slice(c * CHUNK, (c + 1) * CHUNK)
        square = u * u
        t = jnp.tanh(u * (square * (GELU_A * GELU_B) + GELU_A))
        cdf = t * 0.5 + 0.5
        hidden_ref[:, cols] = (u * cdf).astype(BF16)
        slope = cdf * ((1.0 - t) * (u * (square * (3.0 * GELU_A * GELU_B) + GELU_A)) + 1.0)
        du_ref[:, cols] = (slope * back_u).astype(BF16)
    ones = jnp.ones((16, rows), BF16)
    grad = mm(jnp.concatenate([second.T, ones], axis=0), du_ref[...])
    heads = []
    for n in range(4):
        cols = slice(n * D, (n + 1) * D)
        pay_ref[cols, :] = grad[:D, cols].astype(BF16)
        heads.append(grad[D : D + 1, cols])
    pay_ref[FF : 2 * FF, :] = mm(hidden_ref[...].T, dz).astype(BF16)
    heads += [jnp.sum(dz.astype(F32), axis=0, keepdims=True), jnp.zeros((11, D), F32)]
    pay_ref[2 * FF : 2 * FF + 16, :] = jnp.concatenate(heads, axis=0).astype(BF16)
    lane = lax.broadcasted_iota(jnp.int32, (16, D), 1)
    line = lax.broadcasted_iota(jnp.int32, (16, D), 0)
    label = scalar_ref[LABEL]
    digits = jnp.where(lane == 0, label // GRID, jnp.where(lane == 1, label % GRID, 0)).astype(F32)
    facts = jnp.where(line == 2, digits, fact_ref[...].astype(F32)).astype(BF16)
    extra = pay_ref.shape[0] - 2 * FF - 16
    row = lax.broadcasted_iota(jnp.int32, (extra, 16), 0)
    mine = (row % everyone == scalar_ref[PLACE]) & (row < 3 * everyone) & (scalar_ref[SEQ_PLACE] == 0)
    hot = lax.broadcasted_iota(jnp.int32, (extra, 16), 1) == jnp.where(mine, row // everyone, -1)
    pay_ref[2 * FF + 16 :, :] = mm(hot.astype(F32).astype(BF16), facts).astype(BF16)
    copies = Copies(sems)
    split_halves(copies, scalar_ref[SIDE], pay_ref, keep_ref, send_ref)
    copies.wait()


def feed_rest_kernel(
    slots, scalar_ref, o_ref, inverse_ref, x_ref, cot_full_ref, cot_slot_ref, mod_ref, wout_ref, w1_ref,
    w2_ref, line_ref,
    att_ref, hidden_ref, du_ref,
    small_ref, y_full_out, y_slot_out, dm_out, x_out, do_out, go_out, y_ref, dm_ref, do_ref, go_ref, sems,
):
    rows, own = x_ref.shape[0], cot_full_ref.shape[0]
    copies = Copies(sems)
    copies.start(x_ref, x_out)
    gate1, shift2, scale2, gate2 = [mod_ref[n : n + 1, :] for n in range(2, 6)]
    weight, cot = cotangents(scalar_ref, slots, cot_full_ref, cot_slot_ref)
    back = mm_t(du_ref[...], w1_ref[...])
    branch = mm(hidden_ref[...], w2_ref[...]) + line_ref[FC2_LINE : FC2_LINE + 1, :]
    attended = att_ref[...]
    middle = x_ref[...].astype(F32) + gate1 * attended
    normed, inverse = norm_parts(middle)
    y_ref[...] = ((middle + gate2 * branch) * weight).astype(BF16)
    copies.start(y_ref.at[pl.ds(0, own)], y_full_out)
    copies.start(y_ref.at[pl.ds(own, rows - own)], y_slot_out)
    dmid = cot + norm_back(normed, inverse, back * (1.0 + scale2))
    dm_ref[...] = dmid
    copies.start(dm_ref, dm_out)
    datt = (gate1 * dmid).astype(BF16)
    merged_f = jnp.concatenate([o_ref[n] for n in range(HEADS // 2)], axis=1)
    dout = mm_t(datt, wout_ref[...]) * jnp.concatenate([inverse_ref[n] for n in range(HEADS // 2)], axis=1)
    dout = dout.astype(BF16).astype(F32)
    product = dout * merged_f
    high = product.astype(BF16)
    low = (product - high.astype(F32)).astype(BF16)
    row = lax.broadcasted_iota(jnp.int32, (D, 128), 0)
    lane = lax.broadcasted_iota(jnp.int32, (D, 128), 1)
    heads = jnp.where(row // HDIM == lane // 2, -1.0, 0.0).astype(BF16)
    less = mm(high, heads) + mm(low, heads)
    lane = lax.broadcasted_iota(jnp.int32, (rows, 128), 1)
    kept = less.astype(BF16).astype(F32)
    pair = jnp.where(lane % 2 == 0, kept, less - kept)
    for head in range(HEADS):
        tile = dout[:, head // 2 * 128 : (head // 2 + 1) * 128]
        if head % 2:
            tile = pltpu.roll(tile, HDIM, 1)
        more = pltpu.roll(pair, HDIM - 2 * head, 1)
        more = jnp.where(lane < HDIM + 2, more, 0.0)
        do_ref[head] = jnp.where(lane < HDIM, tile, more).astype(BF16)
    copies.start(do_ref, do_out)
    go_ref[...] = mm(merged_f.astype(BF16).T, datt).astype(BF16)
    copies.start(go_ref, go_out)
    column = lambda value: jnp.sum(value.astype(F32), axis=0, keepdims=True)
    sums = [dmid * attended, back, back * normed, cot * branch, datt]
    small_ref[...] = jnp.concatenate([column(value) for value in sums] + [jnp.zeros((3, D), F32)], axis=0)
    copies.wait()


def attend_back(own, e_ref, q_ref, k_ref, v_ref, do_ref, place_ref, outs, sums):
    dq_ref, dk_ref, dv_ref, tab_ref = outs
    dkt_ref, dvt_ref, part_ref = sums
    rows = q_ref.shape[1]
    spans = blocks_of(0, own, 256) + blocks_of(own, rows - own, 256)
    items = [(side, *span) for side in range(2) for span in spans]
    grads, found = {}, {}
    for n in range(len(items) + 2):
        if n < len(items):
            side, at, size = items[n]
            grads[n] = mm_t(do_ref[side, at : at + size, :], v_ref[side])
        if 0 <= n - 1 < len(items):
            side, at, size = items[n - 1]
            found[n - 1] = (e_ref[side, at : at + size, :].astype(F32) * grads.pop(n - 1)).astype(BF16)
        if 0 <= n - 2:
            side, at, size = items[n - 2]
            lanes = slice(side * HDIM, (side + 1) * HDIM)
            ds = found.pop(n - 2)
            dq = mm(ds, k_ref[side])
            dq_ref[at : at + size, lanes] = (dq[:, :HDIM] * (1.0 / math.sqrt(HDIM))).astype(BF16)
            part_ref[at : at + size, lanes] = dq[:, HDIM:].astype(BF16)
            dkt = mm(q_ref[side, at : at + size, :HDIM].T, ds)
            dvt = mm(do_ref[side, at : at + size, :HDIM].T, e_ref[side, at : at + size, :])
            if at == 0:
                dkt_ref[lanes, :] = dkt
                dvt_ref[lanes, :] = dvt
            else:
                dkt_ref[lanes, :] += dkt
                dvt_ref[lanes, :] += dvt
    tab_ref[...] = mm(place_ref[...], part_ref[...])
    dk_ref[...] = dkt_ref[...].astype(BF16).T
    dv_ref[...] = dvt_ref[...].astype(BF16).T


def back_kernel(own, everyone, scalar_ref, kept_ref, mod_ref, prior_ref, *refs):
    group_sources, refs = refs[:5], refs[5:]
    sources, refs = refs[:7], refs[7:]
    keep_ref, send_ref, dx_ref, dx_own_ref, refs = *refs[:4], refs[4:]
    group_local, refs = refs[:5], refs[5:]
    local, refs = refs[:7], refs[7:]
    dq_ref, dk_ref, dv_ref, tab_ref, normed_ref, inverse_ref, dxs_ref, dkt_ref, dvt_ref, pay_ref = refs[:10]
    place_ref, part_ref, group_sems, sems, pay_sems = refs[10:]
    tok_ref, a_ref, x_ref, slot_ref, weight_ref, dm_ref, go_ref = local
    step = pl.program_id(0)
    last = pl.num_programs(0) - 1
    slot = step % 2

    def fetches(group, place):
        return [
            pltpu.make_async_copy(source.at[pl.ds(2 * group, 2)], target.at[place], group_sems.at[place, n])
            for n, (source, target) in enumerate(zip(group_sources, group_local))
        ]

    def copies():
        return [
            pltpu.make_async_copy(source, target, sems.at[n])
            for n, (source, target) in enumerate(zip(sources, local))
        ]

    @pl.when(step == 0)
    def first():
        whole = copies()
        whole[0].start()
        for copy in fetches(0, 0):
            copy.start()
        for copy in whole[1:]:
            copy.start()
        for copy in fetches(1, 1):
            copy.start()
        slots = x_ref.shape[0] - own
        place_ref[...] = place_onehot(row_places(scalar_ref, kept_ref, own, slots), turned=True).T
        whole[0].wait()
        normed, inverse = norm_parts(tok_ref[...].astype(F32))
        normed_ref[...] = normed
        inverse_ref[...] = jnp.broadcast_to(inverse, inverse_ref.shape)

    @pl.when((step > 0) & (step + 1 < last))
    def following():
        for copy in fetches(step + 1, 1 - slot):
            copy.start()

    @pl.when(step < last)
    def attention():
        for copy in fetches(step, slot):
            copy.wait()
        outs = dq_ref.at[step], dk_ref.at[step], dv_ref.at[step], tab_ref.at[step]
        attend_back(own, *[ref.at[slot] for ref in group_local], place_ref, outs, (dkt_ref, dvt_ref, part_ref))

    @pl.when(step == last)
    def projections():
        for copy in copies()[1:]:
            copy.wait()
        groups = dq_ref.shape[0]
        total = tok_ref.shape[0]
        rows = x_ref.shape[0]
        slots = rows - own
        scale = mod_ref[1:2, :]
        here = row_span(scalar_ref, STARTS, own)

        def joined(ref, span):
            return jnp.concatenate([ref[n, span, :] for n in range(groups)], axis=1)

        every = slice(0, total)
        dk, dv = joined(dk_ref, every), joined(dv_ref, every)
        dq_own, dq_slot = joined(dq_ref, slice(0, own)), joined(dq_ref, slice(own, rows))
        column = lambda value: jnp.sum(value.astype(F32), axis=0, keepdims=True)
        lowered_t = a_ref[...].T
        pay_ref[0:D, :] = (mm(a_ref[here, :].T, dq_own) + mm(slot_ref[...].T, dq_slot)).astype(BF16)
        pay_ref[D : 2 * D, :] = mm(lowered_t, dk).astype(BF16)
        pay_ref[2 * D : 3 * D, :] = mm(lowered_t, dv).astype(BF16)
        pay_ref[3 * D : 4 * D, :] = go_ref[...]
        slot_normed, slot_inverse = norm_parts(x_ref[own:, :].astype(F32))
        da = mm_t(dq_slot, weight_ref[:, :D])
        shift_sum, scale_sum = column(da), column(da * slot_normed)
        spread = dm_ref[own:, :] + norm_back(slot_normed, slot_inverse, da * (1.0 + scale))
        chosen = slot_places(scalar_ref, kept_ref, slots) == lax.broadcasted_iota(jnp.int32, (slots, total), 1)
        chosen = chosen.astype(F32)
        moved = mm(chosen.astype(BF16).T, spread.astype(BF16))
        dxs_ref[...] = mm_t(dk, weight_ref[:, D : 2 * D]) + mm_t(dv, weight_ref[:, 2 * D :])
        dxs_ref[here, :] += mm_t(dq_own, weight_ref[:, :D])
        da = dxs_ref[...]
        normed = normed_ref[...]
        shift_sum, scale_sum = shift_sum + column(da), scale_sum + column(da * normed)
        inverse = jnp.concatenate([inverse_ref[...]] * (D // 128), axis=1)
        dxs_ref[...] = moved + norm_back(normed, inverse, da * (1.0 + scale))
        dx_own_ref[...] = dxs_ref[here, :] + dm_ref[:own, :]
        others = dx_ref.shape[0]
        for n in range(others):
            dx_ref[n] = dxs_ref[row_span(scalar_ref, STARTS + 1 + others + n, own), :].astype(BF16)
        rel = table_sums([tab_ref[n] for n in range(groups)])
        smalls = jnp.concatenate(
            [
                shift_sum, scale_sum, prior_ref[0:4, :], column(dq_own) + column(dq_slot), column(dv),
                *rel, prior_ref[4:5, :], jnp.zeros((5, D), F32),
            ],
            axis=0,
        ).astype(BF16)
        tail = pay_ref.shape[0] - 4 * D
        row = lax.broadcasted_iota(jnp.int32, (tail, 16), 0)
        lane = lax.broadcasted_iota(jnp.int32, (tail, 16), 1)
        wanted = jnp.where(row % everyone == scalar_ref[PLACE], row // everyone, -1)
        wanted = jnp.where(row < 6 * everyone, wanted, row - 6 * everyone + 6)
        pay_ref[4 * D :, :] = mm((lane == wanted).astype(F32).astype(BF16), smalls).astype(BF16)
        halves = Copies(pay_sems)
        split_halves(halves, scalar_ref[SIDE], pay_ref, keep_ref, send_ref)
        halves.wait()


def table_sums(tabs):
    found = ([], [])
    for tab in tabs:
        for side in range(2):
            for part in range(2):
                at = 2 * side * GRID + part * GRID
                square = tab[part * GRID : (part + 1) * GRID, at : at + GRID]
                wide = jnp.concatenate([square, jnp.zeros((GRID, 128 - GRID), F32)], axis=1)
                turned = pltpu.roll(wide, 0, 1, stride=1, stride_axis=0)
                found[part].append(jnp.sum(turned, axis=0, keepdims=True)[:, : 2 * GRID])
    return [jnp.concatenate(parts, axis=1) for parts in found]


def call(kernel, outs, scratch, args, scalars=0, far=0, away=0, copies=0, micros=1, limit=32):
    scratches = [pltpu.VMEM(shape, dtype) for shape, dtype in scratch]
    if copies:
        scratches.append(pltpu.SemaphoreType.DMA((copies,)))
    return pl.pallas_call(
        kernel,
        out_shape=[jax.ShapeDtypeStruct(shape, dtype) for shape, dtype in outs[: len(outs) - away]]
        + [pltpu.HBM(shape, dtype) for shape, dtype in outs[len(outs) - away :]],
        in_specs=[smem] * scalars + [vmem] * (len(args) - scalars - far) + [hbm] * far,
        out_specs=[vmem] * (len(outs) - away) + [hbm] * away,
        scratch_shapes=scratches,
        compiler_params=pltpu.CompilerParams(vmem_limit_bytes=limit * MIB),
        cost_estimate=pl.CostEstimate(flops=micros * 10**9, bytes_accessed=MIB, transcendentals=0),
    )(*args)


def own_call(outs, scalars, sources):
    return pl.pallas_call(
        own_kernel,
        out_shape=[jax.ShapeDtypeStruct(shape, dtype) for shape, dtype in outs],
        in_specs=[smem] * len(scalars) + [hbm] * len(sources),
        out_specs=[smem] + [vmem] * (len(outs) - 1),
        scratch_shapes=[pltpu.VMEM(value.shape, value.dtype) for value in sources]
        + [pltpu.SemaphoreType.DMA((len(sources),))],
        compiler_params=pltpu.CompilerParams(vmem_limit_bytes=16 * MIB),
        cost_estimate=pl.CostEstimate(flops=3 * 10**9, bytes_accessed=MIB, transcendentals=0),
    )(*scalars, *map(in_hbm, sources))


def in_hbm(value):
    return pltpu.with_memory_space_constraint(value, pltpu.HBM)


def add_kernel(left_ref, right_ref, sum_ref):
    sum_ref[...] = (left_ref[...].astype(F32) + right_ref[...].astype(F32)).astype(BF16)


def add_call(left, right, micros):
    return call(add_kernel, [(left.shape, BF16)], [], [left, right], micros=micros)[0]


def back_call(own, everyone, groups_of, sources, scalars, kept, mod, prior, tail_half):
    rows, total = groups_of[1].shape[1], groups_of[2].shape[1]
    groups = HEADS // 2
    others = total // own - 1
    whole = lambda shape: pl.BlockSpec(shape, lambda n: (0,) * len(shape))
    outs = [((tail_half, D), BF16), ((tail_half, D), BF16), ((others, own, D), BF16), ((own, D), F32)]
    scratch = [((2, 2) + value.shape[1:], value.dtype) for value in groups_of]
    scratch += [(value.shape, value.dtype) for value in sources]
    scratch += [
        ((groups, rows, 128), BF16), ((groups, total, 128), BF16), ((groups, total, 128), BF16),
        ((groups, 2 * GRID, 128), F32), ((total, D), F32), ((total, 128), F32), ((total, D), F32),
        ((128, total), F32), ((128, total), F32), ((2 * tail_half, D), BF16),
        ((2 * GRID, rows), BF16), ((rows, 128), BF16),
    ]
    small = [kept, mod, prior]
    return pl.pallas_call(
        functools.partial(back_kernel, own, everyone),
        grid=(groups + 1,),
        out_shape=[jax.ShapeDtypeStruct(shape, dtype) for shape, dtype in outs[:2]]
        + [pltpu.HBM(shape, dtype) for shape, dtype in outs[2:]],
        in_specs=[smem] + [whole(value.shape) for value in small] + [hbm] * (len(groups_of) + len(sources)),
        out_specs=[vmem, vmem] + [whole(shape) for shape, unused in outs[2:]],
        scratch_shapes=[pltpu.VMEM(shape, dtype) for shape, dtype in scratch]
        + [pltpu.SemaphoreType.DMA((2, 5)), pltpu.SemaphoreType.DMA((7,)), pltpu.SemaphoreType.DMA((2,))],
        compiler_params=pltpu.CompilerParams(
            vmem_limit_bytes=48 * MIB, dimension_semantics=("arbitrary",)
        ),
        cost_estimate=pl.CostEstimate(flops=18 * 10**9, bytes_accessed=MIB, transcendentals=0),
    )(scalars, *small, *map(in_hbm, groups_of), *map(in_hbm, sources))


def halves_reader(side_ref, mine_ref, other_ref):
    half = mine_ref.shape[0]

    def get(at, count):
        found = []
        for which in range(2):
            first, last = max(at, which * half), min(at + count, (which + 1) * half)
            if first < last:
                span = slice(first - which * half, last - which * half)
                found.append(jnp.where(side_ref[0] == which, mine_ref[span, :], other_ref[span, :]))
        return found[0] if len(found) == 1 else jnp.concatenate(found, axis=0)

    return get


def layer_kernel(side_ref, mine_ref, other_ref, info_ref, small_ref, g1_out, g2_out, g1_ref, g2_ref, sems):
    get = halves_reader(side_ref, mine_ref, other_ref)
    copies = Copies(sems)
    for n in range(4):
        cols = pl.ds(n * D, D)
        g1_ref[:, cols] = get(n * D, D).astype(F32)
        copies.start(g1_ref.at[:, cols], g1_out.at[:, cols])
        g2_ref[cols, :] = get(FF + n * D, D).astype(F32)
        copies.start(g2_ref.at[cols], g2_out.at[cols])
    small_ref[...] = get(2 * FF, 16).astype(F32)[:8]
    info_ref[...] = get(2 * FF + 16, info_ref.shape[0])
    copies.wait()


def last_kernel(
    everyone, side_ref, mine_ref, other_ref, info_ref, ada_in, qv_ref, rel_ref, out_bias_ref, ada_bias_ref,
    gqkv_out, gada_out, table_out, go_out, gqkv_ref, gada_ref, table_ref, go_ref, ada_ref, sems,
):
    get = halves_reader(side_ref, mine_ref, other_ref)
    copies = Copies(sems)
    copies.start(ada_in, ada_ref)
    for n in range(3):
        cols = pl.ds(n * D, D)
        gqkv_ref[:, cols] = get(n * D, D).astype(F32)
        copies.start(gqkv_ref.at[:, cols], gqkv_out.at[:, cols])
    go_ref[...] = get(3 * D, D).astype(F32)
    copies.start(go_ref, go_out)
    act_t = info_ref[:everyone, :].T
    dmods = [get(4 * D + n * everyone, everyone) for n in range(6)]
    for n in range(6):
        cols = pl.ds(n * D, D)
        gada_ref[:, cols] = mm(act_t, dmods[n])
        copies.start(gada_ref.at[:, cols], gada_out.at[:, cols])
        ada_bias_ref[cols] = jnp.sum(dmods[n].astype(F32), axis=0)
    copies.made.pop(0).wait()
    back = jnp.zeros((everyone, D), F32)
    for n in range(6):
        back = back + mm_t(dmods[n], ada_ref[:, n * D : (n + 1) * D])
    cond = info_ref[everyone : 2 * everyone, :].astype(F32) * back
    high = cond.astype(BF16)
    low = (cond - high.astype(F32)).astype(BF16)
    digits = info_ref[2 * everyone : 3 * everyone, :].astype(F32)
    label = (digits[:, 0:1] * GRID + digits[:, 1:2]).astype(jnp.int32)
    classes = table_ref.shape[0]
    wide = round_up(classes, 128)
    hot = (label == lax.broadcasted_iota(jnp.int32, (everyone, wide), 1)).astype(F32).astype(BF16).T
    table_ref[...] = (mm(hot, high) + mm(hot, low))[:classes]
    copies.start(table_ref, table_out)
    small = get(4 * D + 6 * everyone, 16).astype(F32)
    qv_ref[...] = small[:2]
    for part in range(2):
        for head in range(HEADS):
            at = 2 * GRID * head
            rel_ref[head, part : part + 1, :] = small[2 + part : 3 + part, at : at + 2 * GRID - 1]
    out_bias_ref[...] = small[4]
    copies.wait()


def swap_cores(value, dp):
    return lax.ppermute(value, "dp", [(n, n ^ 1) for n in range(dp)])


def exchange(value, dp, seq):
    groups = [
        [(far * (dp // 2) + 2 * pair + core) * seq + at for pair in range(dp // 4) for at in range(seq)]
        for far in range(2)
        for core in range(2)
    ]
    return lax.all_to_all(value, AXES, 0, 0, axis_index_groups=groups)


def sum_pieces(pieces, dp):
    near = jnp.sum(pieces.astype(F32), axis=0).astype(BF16)
    far = lax.ppermute(near, "dp", [(n, (n + dp // 2) % dp) for n in range(dp)])
    return (near.astype(F32) + far.astype(F32)).astype(BF16)


def spread_out(chunk, dp, seq):
    peers = dp // 4 * seq
    return exchange(jnp.broadcast_to(chunk[None], (peers,) + chunk.shape), dp, seq).reshape(-1, D)


def scatter_rows(partial, seq):
    return [
        lax.ppermute(partial[step - 1], "seq", [(n, (n + step) % seq) for n in range(seq)])
        for step in range(1, seq)
    ]


def body(
    dp, seq, image_tokens, kept_index, kept_count, sample_valid, timestep, class_label, class_table,
    ada_weight, ada_bias, qkv_weight, qv_bias, rel_bias, out_weight, out_bias, fc1_weight,
    fc1_bias, fc2_weight, fc2_bias, grad_full, grad_masked,
):
    samples, own, width = image_tokens.shape
    held = kept_index.shape[1]
    slots = grad_masked.shape[1]
    padded = round_up(slots, 16)
    rows = own + padded
    total = own * seq
    everyone = dp * samples
    classes = class_table.shape[0]
    dp_place, seq_place = lax.axis_index("dp"), lax.axis_index("seq")

    extra_rows = round_up(2 * FF + 16 + 3 * everyone, dp * seq * 4) - (2 * FF + 16)
    peers = dp // 4 * seq
    side = dp_place % 2
    sides = side.astype(jnp.int32).reshape(1)
    half = (2 * FF + 16 + extra_rows) // 2
    tail_half = round_up(4 * D + 16 + 6 * everyone, dp * seq * 4) // 2
    kept_of = []
    for s in range(samples):
        tokens = [image_tokens[s]]
        for step in range(1, seq):
            tokens.append(lax.ppermute(tokens[0], "seq", [(n, (n + step) % seq) for n in range(seq)]))
        number = jnp.arange(STARTS + 2 * seq - 1, dtype=jnp.int32)
        block = number - STARTS
        scalars = jnp.where(block < seq, seq_place - block, seq_place + block - seq + 1) % seq * own
        entries = {
            SIDE: side, PLACE: dp_place * samples + s, SLOT_START: seq_place * slots, SEQ_PLACE: seq_place,
        }
        for at, entry in entries.items():
            scalars = jnp.where(number == at, entry, scalars)
        places = scalars.astype(jnp.int32)
        held_rows = held + padded - slots
        cot_slot = jnp.pad(grad_masked[s], ((0, padded - slots), (0, 0)))
        one = slice(s, s + 1)
        scalars, kept, facts, lines, mod, *owned, mask = own_call(
            [
                (places.shape, jnp.int32), ((held_rows, 1), jnp.int32), ((16, D), BF16), ((16, D), F32),
                ((8, D), F32), ((own, D), BF16), ((own, D), BF16), ((HEADS, own, 128), BF16),
                ((HEADS, own, 128), BF16), ((HEADS, own, 128), BF16), ((padded, D), BF16), ((8, total), F32),
            ],
            [places, kept_count[one], sample_valid[one], timestep[one], class_label[one]],
            [
                kept_index[one], rel_bias.transpose(1, 0, 2), ada_bias, qv_bias, out_bias, fc1_bias, fc2_bias,
                class_table, ada_weight, tokens[0], qkv_weight,
            ],
        )
        qaug, kaug, vaug, x, lowered, whole, slot = call(
            functools.partial(prep_kernel, seq),
            [
                ((HEADS, rows, 128), BF16), ((HEADS, total, 128), BF16), ((HEADS, total, 128), BF16),
                ((rows, D), BF16), ((total, D), BF16), ((total, D), BF16), ((padded, D), BF16),
            ],
            [((total, D), BF16), ((total, D), BF16), ((total, D), BF16), ((padded, D), BF16)],
            [scalars, *tokens, *owned, kept, mod, qkv_weight, lines],
            scalars=1, away=3, copies=3, micros=3, limit=16,
        )
        mixed, inverse, spread_far, qaug_far, kaug_far, vaug_far = call(
            functools.partial(attend_kernel, own),
            [
                ((HEADS // 2, rows, 128), F32), ((HEADS // 2, rows, 128), F32),
                ((HEADS, rows, total), BF16), (qaug.shape, BF16), (kaug.shape, BF16), (vaug.shape, BF16),
            ],
            [((HEADS, rows, total), BF16)],
            [qaug, kaug, vaug, mask],
            away=4, copies=3 + HEADS, micros=10, limit=32,
        )
        attended, hidden, du, keep, send = call(
            functools.partial(feed_kernel, slots, everyone),
            [((rows, D), F32), ((rows, FF), BF16), ((rows, FF), BF16), ((half, D), BF16), ((half, D), BF16)],
            [((2 * half, D), BF16)],
            [
                scalars, mixed, x, grad_full[s], cot_slot, mod, out_weight, fc1_weight, fc2_weight, lines,
                facts,
            ],
            scalars=1, copies=2, micros=10, limit=24,
        )
        kept_of.append(dict(
            rest=[
                scalars, mixed, inverse, x, grad_full[s], cot_slot, mod, out_weight, fc1_weight, fc2_weight,
                lines, attended, hidden, du,
            ],
            groups=[spread_far, qaug_far, kaug_far, vaug_far], sources=[whole, lowered, slot, qkv_weight],
            small=[scalars, kept, mod], keep=keep, send=send,
        ))

    def added(arrays):
        if len(arrays) == 1:
            return arrays[0]
        return functools.reduce(jnp.add, [a.astype(F32) for a in arrays]).astype(arrays[0].dtype)

    keep, send = added([k["keep"] for k in kept_of]), added([k["send"] for k in kept_of])
    got = swap_cores(send, dp)

    rests = [
        call(
            functools.partial(feed_rest_kernel, slots),
            [
                ((8, D), F32), ((own, D), BF16), ((padded, D), BF16), ((rows, D), F32), ((rows, D), BF16),
                ((HEADS, rows, 128), BF16), ((D, D), BF16),
            ],
            [((rows, D), BF16), ((rows, D), F32), ((HEADS, rows, 128), BF16), ((D, D), BF16)],
            k["rest"],
            scalars=1, away=6, copies=6, micros=6, limit=24,
        )
        for k in kept_of
    ]
    mine = (keep.astype(F32) + got.astype(F32)).astype(BF16)
    mine, rests = lax.optimization_barrier((mine, rests))
    pieces = exchange(mine.reshape(peers, half // peers, D), dp, seq)
    tails = []
    for k, rest in zip(kept_of, rests):
        small, unused_full, unused_slot, dmid, x_far, dout_far, grad_out = rest
        whole, lowered, slot, weights = k["sources"]
        tails.append(
            back_call(
                own, everyone, [*k["groups"], dout_far], [whole, lowered, x_far, slot, weights, dmid, grad_out],
                *k["small"], small, tail_half,
            )
        )

    keep, send = added([t[0] for t in tails]), added([t[1] for t in tails])
    keep, send, pieces = lax.optimization_barrier((keep, send, pieces))
    got = swap_cores(send, dp)
    mine = add_call(keep, got, 30).reshape(peers, tail_half // peers, D)
    chunk = sum_pieces(pieces, dp)
    last_chunk = sum_pieces(exchange(mine, dp, seq), dp)
    first_moved = [scatter_rows(t[2][:, : own // 2], seq) for t in tails]
    chunk, first_moved = lax.optimization_barrier((chunk, first_moved))
    last_moved = [scatter_rows(t[2][:, own // 2 :], seq) for t in tails]
    layer_half = spread_out(chunk, dp, seq)
    layer_half, last_chunk = lax.optimization_barrier((layer_half, last_chunk))
    last_half = spread_out(last_chunk, dp, seq)
    out_full = jnp.stack([rest[1] for rest in rests])
    out_masked = jnp.stack([rest[2][:slots] for rest in rests])
    info, layer_small, grad_fc1, grad_fc2 = call(
        layer_kernel,
        [((extra_rows, D), BF16), ((8, D), F32), ((D, FF), F32), ((FF, D), F32)],
        [((D, FF), F32), ((FF, D), F32)],
        [sides, layer_half, swap_cores(layer_half, dp)],
        scalars=1, away=2, copies=8, micros=3,
    )
    grad_fc1_bias = layer_small[:4].reshape(FF)
    grad_fc2_bias = layer_small[4]
    last_half, info, grad_fc1_bias, grad_fc2_bias = lax.optimization_barrier(
        (last_half, info, grad_fc1_bias, grad_fc2_bias)
    )
    grad_qv, grad_rel, grad_out_bias, grad_ada_bias, grad_qkv, grad_ada, grad_table, grad_out = call(
        functools.partial(last_kernel, everyone),
        [
            ((2, D), F32), ((HEADS, 2, 2 * GRID - 1), F32), ((D,), F32), ((6 * D,), F32),
            ((D, 3 * D), F32), ((D, 6 * D), F32), ((classes, D), F32), ((D, D), F32),
        ],
        [((D, 3 * D), F32), ((D, 6 * D), F32), ((classes, D), F32), ((D, D), F32), (ada_weight.shape, BF16)],
        [sides, last_half, swap_cores(last_half, dp), info, in_hbm(ada_weight)],
        scalars=1, far=1, away=4, copies=12, micros=4, limit=16,
    )
    grad_rel = grad_rel.transpose(1, 0, 2)
    grad_qkv, last_moved = lax.optimization_barrier((grad_qkv, last_moved))
    grad_input = []
    for tail, *moved in zip(tails, first_moved, last_moved):
        came = [jnp.concatenate(both).astype(F32) for both in zip(*moved)]
        grad_input.append(functools.reduce(jnp.add, came, tail[3]))
    grad_input = jnp.stack(grad_input)
    return (
        out_full, out_masked, grad_input, grad_table, grad_ada, grad_ada_bias, grad_qkv, grad_qv,
        grad_rel, grad_out, grad_out_bias, grad_fc1, grad_fc1_bias, grad_fc2, grad_fc2_bias,
    )


def solution(mesh):
    split = P("dp", "seq", None)
    placed = (split, P("dp", None)) + (P("dp"),) * 4 + (P(),) * 12 + (split, split)
    return jax.shard_map(
        functools.partial(body, mesh.shape["dp"], mesh.shape["seq"]),
        mesh=mesh,
        in_specs=placed,
        out_specs=(split,) * 3 + (P(),) * 12,
        check_vma=False,
    )
```

```python
import functools
import math

import jax
import jax.numpy as jnp
from jax import lax
from jax.experimental import pallas as pl
from jax.experimental.pallas import tpu as pltpu
from jax.sharding import PartitionSpec as P

D = 384
HEADS = 6
HDIM = 64
GRID = 32
FF = 1536
CHUNK = 256

AXES = ("dp", "seq")
F32 = jnp.float32
BF16 = jnp.bfloat16
MIB = 1024 * 1024
GELU_A = math.sqrt(2.0 / math.pi)
GELU_B = 0.044715

highest = lax.Precision.HIGHEST
big_negative = -1e30
vmem = pl.BlockSpec(memory_space=pltpu.VMEM)
smem = pl.BlockSpec(memory_space=pltpu.SMEM)
hbm = pl.BlockSpec(memory_space=pltpu.HBM)


def round_up(value, step):
    return -(-value // step) * step


def blocks_of(first, count, most):
    pieces = -(-count // most)
    size = round_up(-(-count // pieces), 16)
    found = []
    at = 0
    while at < count:
        found.append((first + at, min(size, count - at)))
        at += size
    return found


def mm(left, right):
    return lax.dot_general(left, right, (((1,), (0,)), ((), ())), preferred_element_type=F32)


def mm_t(left, right):
    return lax.dot_general(left, right, (((1,), (1,)), ((), ())), preferred_element_type=F32)


def norm_parts(value):
    average = jnp.mean(value, axis=-1, keepdims=True)
    centred = value - average
    variance = jnp.mean(centred * centred, axis=-1, keepdims=True)
    inverse = lax.rsqrt(variance + 1e-06)
    return (centred * inverse, inverse)


def norm_back(normed, inverse, grad):
    first = jnp.mean(grad, axis=-1, keepdims=True)
    second = jnp.mean(grad * normed, axis=-1, keepdims=True)
    return inverse * (grad - first - normed * second)


def place_onehot(position, turned=False):
    lane = lax.broadcasted_iota(jnp.int32, (position.shape[0], 2 * GRID), 1)
    if turned:
        lane = jnp.where(lane < GRID, GRID - 1 - lane, 3 * GRID - 1 - lane)
    wanted = jnp.where(lane < GRID, position // GRID, position % GRID + GRID)
    return (lane == wanted).astype(F32).astype(BF16)


class Copies:
    def __init__(self, sems):
        self.sems, self.made, self.count = sems, [], 0

    def start(self, source, target):
        copy = pltpu.make_async_copy(source, target, self.sems.at[self.count])
        copy.start()
        self.made.append(copy)
        self.count += 1

    def wait(self):
        for copy in self.made:
            copy.wait()


def half_copies(side, payload_ref, keep_ref, send_ref, sems, which):
    for target, chosen in ((keep_ref, side == which), (send_ref, side != which)):

        @pl.when(chosen)
        def start():
            pltpu.make_async_copy(payload_ref.at[which], target, sems.at[which]).start()


def split_halves(copies, side, payload_ref, keep_ref, send_ref):
    half = keep_ref.shape[0]
    for which, target in ((side, keep_ref), (1 - side, send_ref)):
        copies.start(payload_ref.at[pl.ds(pl.multiple_of(which * half, 16), half)], target)


SIDE, PLACE, SLOT_START, COUNT, VALID, LABEL, SEQ_PLACE, STARTS = range(8)


def row_span(scalar_ref, number, count):
    return pl.ds(pl.multiple_of(scalar_ref[number], 16), count)


def slot_places(scalar_ref, kept_ref, slots):
    return kept_ref[pl.ds(pl.multiple_of(scalar_ref[SLOT_START], 8), slots), :]


def row_places(scalar_ref, kept_ref, own, slots):
    mine = lax.broadcasted_iota(jnp.int32, (own, 1), 0) + scalar_ref[STARTS]
    return jnp.concatenate([mine, slot_places(scalar_ref, kept_ref, slots)], axis=0)


def row_weights(scalar_ref, own, slots, rows):
    row = lax.broadcasted_iota(jnp.int32, (rows, 1), 0)
    kept = (row < own + slots) & (row - own + scalar_ref[SLOT_START] < scalar_ref[COUNT])
    return jnp.where((row < own) | kept, scalar_ref[VALID], 0).astype(F32)


def project(tokens, mod_ref, weight_ref, line_ref):
    normed, unused = norm_parts(tokens.astype(F32))
    lowered = (normed * (1.0 + mod_ref[1:2, :]) + mod_ref[0:1, :]).astype(BF16)
    query = (mm(lowered, weight_ref[:, :D]) + line_ref[QV_LINE : QV_LINE + 1, :]).astype(BF16)
    scaled = (query.astype(F32) * (1.0 / math.sqrt(HDIM))).astype(BF16)
    keys = mm(lowered, weight_ref[:, D : 2 * D]).astype(BF16)
    values = (mm(lowered, weight_ref[:, 2 * D :]) + line_ref[QV_LINE + 1 : QV_LINE + 2, :]).astype(BF16)
    return lowered, scaled, keys, values


def head_cols(head):
    return slice(head * HDIM, (head + 1) * HDIM)


def ones_lanes(count):
    return (lax.broadcasted_iota(jnp.int32, (count, HDIM), 1) < 2).astype(F32).astype(BF16)


def bias_table(rel_ref):
    lane = lax.broadcasted_iota(jnp.int32, (GRID, 128), 1)
    parts = []
    for part in range(2):
        tiles = []
        for group in range(HEADS // 2):
            tile = jnp.zeros((GRID, 128), F32)
            for side in range(2):
                head = 2 * group + side
                line = rel_ref[head, part : part + 1, :].astype(F32)
                line = jnp.concatenate([line, jnp.zeros((1, 128 - line.shape[1]), F32)], axis=1)
                first = side * HDIM + part * GRID
                turned = pltpu.roll(
                    jnp.broadcast_to(line, (GRID, 128)), (first + 128 - (GRID - 1)) % 128, 1,
                    stride=1, stride_axis=0,
                )
                tile = jnp.where((lane >= first) & (lane < first + GRID), turned, tile)
            tiles.append(tile)
        parts.append(jnp.concatenate(tiles, axis=1))
    return jnp.concatenate(parts, axis=0).astype(BF16)


QV_LINE, OUT_LINE, FC1_LINE, FC2_LINE = 6, 8, 9, 13
COND_LINE = 6


def time_features(moment):
    half = D // 2
    lane = lax.broadcasted_iota(jnp.int32, (1, D), 1)
    number = jnp.where(lane < half, lane, lane - half).astype(F32)
    angle = moment.astype(F32) * jnp.exp(-math.log(10000.0) * number / half)
    return jnp.where(lane < half, jnp.cos(angle), jnp.sin(angle))


def own_kernel(
    start_ref, count_ref, valid_ref, moment_ref, label_ref,
    *refs,
):
    sources, outs, local, sems = refs[:11], refs[11:22], refs[22:33], refs[33]
    scalar_ref, kept_ref, line_ref, mod_ref, a_ref, qs_ref, qaug_ref, kaug_ref, vaug_ref = outs[:9]
    offset_ref, mask_ref = outs[9:]
    kept_in, rel_ref, ada_bias_ref, qv_bias_ref, out_bias_ref, fc1_bias_ref, fc2_bias_ref = local[:7]
    table_ref, ada_ref, tok_ref, weight_ref = local[7:]
    fetched = [pltpu.make_async_copy(*pair, sems.at[n]) for n, pair in enumerate(zip(sources, local))]
    for copy in fetched:
        copy.start()
    for copy in fetched[:7]:
        copy.wait()
    own = tok_ref.shape[0]
    slots = offset_ref.shape[0]
    total = mask_ref.shape[1]
    held = kept_ref.shape[0]
    label = label_ref[0]
    for n in range(scalar_ref.shape[0]):
        scalar_ref[n] = start_ref[n]
    scalar_ref[COUNT] = count_ref[0]
    scalar_ref[VALID] = valid_ref[0]
    scalar_ref[LABEL] = label
    width = round_up(held, 128)
    kept = jnp.concatenate([kept_in[...], jnp.zeros((1, width - kept_in.shape[1]), jnp.int32)], axis=1)
    kept_ref[...] = jnp.broadcast_to(kept, (8, width)).T[:held, :1]
    place = place_onehot(row_places(start_ref, kept_ref, own, slots))
    offsets = mm(place, bias_table(rel_ref)).astype(BF16)
    offset_ref[...] = offsets[own:]
    number = lax.broadcasted_iota(jnp.int32, (held, 1), 0)
    live = jnp.where(number < count_ref[0], kept_ref[...], -1)
    hit = live == lax.broadcasted_iota(jnp.int32, (held, total), 1)
    count = jnp.sum(hit.astype(F32), axis=0, keepdims=True)
    mask_ref[...] = jnp.broadcast_to(jnp.where(count > 0.0, 0.0, big_negative), mask_ref.shape)
    for n in range(6):
        line_ref[n : n + 1, :] = ada_bias_ref[pl.ds(n * D, D)].astype(F32).reshape(1, D)
    line_ref[QV_LINE : QV_LINE + 2, :] = qv_bias_ref[...].astype(F32)
    line_ref[OUT_LINE : OUT_LINE + 1, :] = out_bias_ref[...].astype(F32).reshape(1, D)
    for n in range(4):
        line_ref[FC1_LINE + n : FC1_LINE + n + 1, :] = fc1_bias_ref[pl.ds(n * D, D)].astype(F32).reshape(1, D)
    line_ref[FC2_LINE : FC2_LINE + 1, :] = fc2_bias_ref[...].astype(F32).reshape(1, D)
    line_ref[FC2_LINE + 1 :, :] = jnp.zeros((2, D), F32)
    for copy in fetched[7:]:
        copy.wait()
    hot = lax.broadcasted_iota(jnp.int32, (16, table_ref.shape[0]), 1) == label
    conditioned = mm(hot.astype(F32).astype(BF16), table_ref[...]) + time_features(moment_ref[0])
    gate = 1.0 / (1.0 + jnp.exp(-conditioned))
    activated = (conditioned * gate).astype(BF16)
    for n in range(6):
        mod_ref[n : n + 1, :] = mm(activated, ada_ref[:, n * D : (n + 1) * D])[:1] + line_ref[n : n + 1, :]
    mod_ref[COND_LINE : COND_LINE + 1, :] = conditioned[:1]
    mod_ref[COND_LINE + 1 :, :] = jnp.zeros((1, D), F32)
    lowered, scaled, keys, values = project(tok_ref[...], mod_ref, weight_ref, line_ref)
    a_ref[...] = lowered
    qs_ref[...] = scaled
    for head in range(HEADS):
        cols = head_cols(head)
        qaug_ref[head] = jnp.concatenate([scaled[:, cols], offsets[:own, cols]], axis=1)
        kaug_ref[head] = jnp.concatenate([keys[:, cols], place[:own]], axis=1)
        vaug_ref[head] = jnp.concatenate([values[:, cols], ones_lanes(own)], axis=1)


def prep_kernel(seq, scalar_ref, *refs):
    token_refs, refs = refs[:seq], refs[seq:]
    own_a_ref, own_qs_ref, own_qaug_ref, own_kaug_ref, own_vaug_ref, offset_ref = refs[:6]
    kept_ref, mod_ref, weight_ref, line_ref = refs[6:10]
    qaug_ref, kaug_ref, vaug_ref, x_ref, a_out, tok_out, slot_out = refs[10:17]
    qs_ref, a_ref, tok_ref, slot_ref, sems = refs[17:]
    copies = Copies(sems)
    own = token_refs[0].shape[0]
    slots, total = offset_ref.shape[0], tok_ref.shape[0]
    for n in range(seq):
        tok_ref[row_span(scalar_ref, STARTS + n, own), :] = token_refs[n][...]
    copies.start(tok_ref, tok_out)
    others = [token_refs[n][...] for n in range(1, seq)]
    others = others[0] if seq == 2 else jnp.concatenate(others, axis=0)
    lowered, scaled, keys, values = project(others, mod_ref, weight_ref, line_ref)
    here = row_span(scalar_ref, STARTS, own)
    a_ref[here, :] = own_a_ref[...]
    qs_ref[here, :] = own_qs_ref[...]
    for head in range(HEADS):
        kaug_ref[head, here, :] = own_kaug_ref[head]
        vaug_ref[head, here, :] = own_vaug_ref[head]
        qaug_ref[head, :own, :] = own_qaug_ref[head]
    for n in range(1, seq):
        there = row_span(scalar_ref, STARTS + n, own)
        span = slice((n - 1) * own, n * own)
        a_ref[there, :] = lowered[span]
        qs_ref[there, :] = scaled[span]
        place = place_onehot(lax.broadcasted_iota(jnp.int32, (own, 1), 0) + scalar_ref[STARTS + n])
        for head in range(HEADS):
            cols = head_cols(head)
            kaug_ref[head, there, :] = jnp.concatenate([keys[span, cols], place], axis=1)
            vaug_ref[head, there, :] = jnp.concatenate([values[span, cols], ones_lanes(own)], axis=1)
    copies.start(a_ref, a_out)
    chosen = slot_places(scalar_ref, kept_ref, slots) == lax.broadcasted_iota(jnp.int32, (slots, total), 1)
    chosen = chosen.astype(F32).astype(BF16)
    x_ref[:own, :] = token_refs[0][...]
    x_ref[own:, :] = mm(chosen, tok_ref[...]).astype(BF16)
    slot_ref[...] = mm(chosen, a_ref[...]).astype(BF16)
    copies.start(slot_ref, slot_out)
    query = mm(chosen, qs_ref[...]).astype(BF16)
    for head in range(HEADS):
        cols = head_cols(head)
        qaug_ref[head, own:, :] = jnp.concatenate([query[:, cols], offset_ref[:, cols]], axis=1)
    copies.wait()


def attend_kernel(
    own, qaug_ref, kaug_ref, vaug_ref, mask_ref, o_ref, inverse_ref, e_out, qaug_out, kaug_out, vaug_out, e_ref, sems
):
    rows = qaug_ref.shape[1]
    copies = Copies(sems)
    copies.start(qaug_ref, qaug_out)
    copies.start(kaug_ref, kaug_out)
    copies.start(vaug_ref, vaug_out)
    spans = [(at, size, False) for at, size in blocks_of(0, own, 256)]
    spans += [(at, size, True) for at, size in blocks_of(own, rows - own, 256)]
    items = [(side, *span) for side in range(2) for span in spans]

    def e_copy(head, n):
        side, at, size, masked = items[n]
        span = pl.ds(at, size)
        return pltpu.make_async_copy(
            e_ref.at[head, span], e_out.at[head, span], sems.at[3 + len(spans) * head + n % len(spans)]
        )

    def pair(group, carry):
        scores, spread = {}, {}
        for n in range(len(items) + 2):
            if n < len(items):
                side, at, size, masked = items[n]
                head = 2 * group + side
                scores[n] = mm_t(qaug_ref[head, at : at + size, :], kaug_ref[head])
                if masked:
                    scores[n] = scores[n] + mask_ref[0:1, :]
            if 0 <= n - 1 < len(items):
                side, at, size, masked = items[n - 1]
                found = scores.pop(n - 1)
                spread[n - 1] = jnp.exp(found - jnp.max(found, axis=-1, keepdims=True)).astype(BF16)
                e_ref[2 * group + side, at : at + size, :] = spread[n - 1]
                e_copy(2 * group + side, n - 1).start()
            if 0 <= n - 2:
                side, at, size, masked = items[n - 2]
                mixed = mm(spread.pop(n - 2), vaug_ref[2 * group + side])
                inverse = 1.0 / mixed[:, HDIM : HDIM + 1]
                lanes = slice(side * HDIM, (side + 1) * HDIM)
                o_ref[group, at : at + size, lanes] = mixed[:, :HDIM] * inverse
                inverse_ref[group, at : at + size, lanes] = jnp.broadcast_to(inverse, (size, HDIM))
        return carry

    lax.fori_loop(0, HEADS // 2, pair, 0)
    for head in range(HEADS):
        for n in range(len(spans)):
            e_copy(head, head % 2 * len(spans) + n).wait()
    copies.wait()


def cotangents(scalar_ref, slots, full_ref, slot_ref):
    own = full_ref.shape[0]
    weight = row_weights(scalar_ref, own, slots, own + slot_ref.shape[0])
    return weight, jnp.concatenate([full_ref[...], slot_ref[...]], axis=0).astype(F32) * weight


def feed_kernel(
    slots, scalar_ref, o_ref, x_ref, cot_full_ref, cot_slot_ref, mod_ref, wout_ref, w1_ref,
    w2_ref, line_ref,
    att_ref, hidden_ref, du_ref, keep_ref, send_ref, pay_ref, sems,
):
    rows = x_ref.shape[0]
    gate1, shift2, scale2, gate2 = [mod_ref[n : n + 1, :] for n in range(2, 6)]
    merged = jnp.concatenate([o_ref[n] for n in range(HEADS // 2)], axis=1).astype(BF16)
    attended = mm(merged, wout_ref[...]) + line_ref[OUT_LINE : OUT_LINE + 1, :]
    att_ref[...] = attended
    normed, unused = norm_parts(x_ref[...].astype(F32) + gate1 * attended)
    second = (normed * (1.0 + scale2) + shift2).astype(BF16)
    unused, cot = cotangents(scalar_ref, slots, cot_full_ref, cot_slot_ref)
    dz = (gate2 * cot).astype(BF16)

    bias = jnp.concatenate([line_ref[FC1_LINE + n : FC1_LINE + n + 1, :] for n in range(4)], axis=1)

    def products(c):
        cols = slice(c * CHUNK, (c + 1) * CHUNK)
        return mm(second, w1_ref[:, cols]) + bias[:, cols], mm_t(dz, w2_ref[cols, :])

    chunks = FF // CHUNK
    ready = products(0)
    for c in range(chunks):
        u, back_u = ready
        if c + 1 < chunks:
            ready = products(c + 1)
        cols = slice(c * CHUNK, (c + 1) * CHUNK)
        square = u * u
        t = jnp.tanh(u * (square * (GELU_A * GELU_B) + GELU_A))
        cdf = t * 0.5 + 0.5
        hidden_ref[:, cols] = (u * cdf).astype(BF16)
        slope = cdf * ((1.0 - t) * (u * (square * (3.0 * GELU_A * GELU_B) + GELU_A)) + 1.0)
        du_ref[:, cols] = (slope * back_u).astype(BF16)
    spare = pay_ref.shape[1] - FF
    pay_ref[0, FF:, :] = jnp.zeros((spare, D), BF16)
    pay_ref[1, FF:, :] = jnp.zeros((spare, D), BF16)
    ones = jnp.ones((16, rows), BF16)
    grad = mm(jnp.concatenate([second.T, ones], axis=0), du_ref[...])
    heads = []
    for n in range(4):
        cols = slice(n * D, (n + 1) * D)
        pay_ref[0, cols, :] = grad[:D, cols].astype(BF16)
        heads.append(grad[D : D + 1, cols])
    heads += [jnp.sum(dz.astype(F32), axis=0, keepdims=True), jnp.zeros((11, D), F32)]
    pay_ref[0, FF : FF + 16, :] = jnp.concatenate(heads, axis=0).astype(BF16)
    pay_ref[1, :FF, :] = mm(hidden_ref[...].T, dz).astype(BF16)
    for which in range(2):
        half_copies(scalar_ref[SIDE], pay_ref, keep_ref, send_ref, sems, which)
    for which in range(2):
        pltpu.make_async_copy(pay_ref.at[which], keep_ref, sems.at[which]).wait()


def feed_rest_kernel(
    slots, scalar_ref, o_ref, inverse_ref, x_ref, cot_full_ref, cot_slot_ref, mod_ref, wout_ref, w1_ref,
    w2_ref, line_ref,
    att_ref, hidden_ref, du_ref,
    small_ref, y_full_out, y_slot_out, dm_out, x_out, do_out, go_out, y_ref, dm_ref, do_ref, go_ref, sems,
):
    rows, own = x_ref.shape[0], cot_full_ref.shape[0]
    copies = Copies(sems)
    copies.start(x_ref, x_out)
    gate1, shift2, scale2, gate2 = [mod_ref[n : n + 1, :] for n in range(2, 6)]
    weight, cot = cotangents(scalar_ref, slots, cot_full_ref, cot_slot_ref)
    back = mm_t(du_ref[...], w1_ref[...])
    branch = mm(hidden_ref[...], w2_ref[...]) + line_ref[FC2_LINE : FC2_LINE + 1, :]
    attended = att_ref[...]
    middle = x_ref[...].astype(F32) + gate1 * attended
    normed, inverse = norm_parts(middle)
    y_ref[...] = ((middle + gate2 * branch) * weight).astype(BF16)
    copies.start(y_ref.at[pl.ds(0, own)], y_full_out)
    copies.start(y_ref.at[pl.ds(own, rows - own)], y_slot_out)
    dmid = cot + norm_back(normed, inverse, back * (1.0 + scale2))
    dm_ref[...] = dmid
    copies.start(dm_ref, dm_out)
    datt = (gate1 * dmid).astype(BF16)
    merged_f = jnp.concatenate([o_ref[n] for n in range(HEADS // 2)], axis=1)
    dout = mm_t(datt, wout_ref[...]) * jnp.concatenate([inverse_ref[n] for n in range(HEADS // 2)], axis=1)
    dout = dout.astype(BF16).astype(F32)
    product = dout * merged_f
    high = product.astype(BF16)
    low = (product - high.astype(F32)).astype(BF16)
    row = lax.broadcasted_iota(jnp.int32, (D, 128), 0)
    lane = lax.broadcasted_iota(jnp.int32, (D, 128), 1)
    heads = jnp.where(row // HDIM == lane // 2, -1.0, 0.0).astype(BF16)
    less = mm(high, heads) + mm(low, heads)
    lane = lax.broadcasted_iota(jnp.int32, (rows, 128), 1)
    kept = less.astype(BF16).astype(F32)
    pair = jnp.where(lane % 2 == 0, kept, less - kept)
    for head in range(HEADS):
        tile = dout[:, head // 2 * 128 : (head // 2 + 1) * 128]
        if head % 2:
            tile = pltpu.roll(tile, HDIM, 1)
        more = pltpu.roll(pair, HDIM - 2 * head, 1)
        more = jnp.where(lane < HDIM + 2, more, 0.0)
        do_ref[head] = jnp.where(lane < HDIM, tile, more).astype(BF16)
    copies.start(do_ref, do_out)
    go_ref[...] = mm(merged_f.astype(BF16).T, datt).astype(BF16)
    copies.start(go_ref, go_out)
    column = lambda value: jnp.sum(value.astype(F32), axis=0, keepdims=True)
    sums = [dmid * attended, back, back * normed, cot * branch, datt]
    small_ref[...] = jnp.concatenate([column(value) for value in sums] + [jnp.zeros((3, D), F32)], axis=0)
    copies.wait()


def attend_back(own, e_ref, q_ref, k_ref, v_ref, do_ref, place_ref, outs, sums):
    dq_ref, dk_ref, dv_ref, tab_ref = outs
    dkt_ref, dvt_ref, part_ref = sums
    rows = q_ref.shape[1]
    spans = blocks_of(0, own, 256) + blocks_of(own, rows - own, 256)
    items = [(side, *span) for side in range(2) for span in spans]
    grads, found = {}, {}
    for n in range(len(items) + 2):
        if n < len(items):
            side, at, size = items[n]
            grads[n] = mm_t(do_ref[side, at : at + size, :], v_ref[side])
        if 0 <= n - 1 < len(items):
            side, at, size = items[n - 1]
            found[n - 1] = (e_ref[side, at : at + size, :].astype(F32) * grads.pop(n - 1)).astype(BF16)
        if 0 <= n - 2:
            side, at, size = items[n - 2]
            lanes = slice(side * HDIM, (side + 1) * HDIM)
            ds = found.pop(n - 2)
            dq = mm(ds, k_ref[side])
            dq_ref[at : at + size, lanes] = (dq[:, :HDIM] * (1.0 / math.sqrt(HDIM))).astype(BF16)
            part_ref[at : at + size, lanes] = dq[:, HDIM:].astype(BF16)
            dkt = mm(q_ref[side, at : at + size, :HDIM].T, ds)
            dvt = mm(do_ref[side, at : at + size, :HDIM].T, e_ref[side, at : at + size, :])
            if at == 0:
                dkt_ref[lanes, :] = dkt
                dvt_ref[lanes, :] = dvt
            else:
                dkt_ref[lanes, :] += dkt
                dvt_ref[lanes, :] += dvt
    tab_ref[...] = mm(place_ref[...], part_ref[...])
    dk_ref[...] = dkt_ref[...].astype(BF16).T
    dv_ref[...] = dvt_ref[...].astype(BF16).T


def back_kernel(own, everyone, scalar_ref, kept_ref, mod_ref, prior_ref, *refs):
    group_sources, refs = refs[:5], refs[5:]
    sources, refs = refs[:7], refs[7:]
    keep_ref, send_ref, dx_ref, dx_own_ref, refs = *refs[:4], refs[4:]
    group_local, refs = refs[:5], refs[5:]
    local, refs = refs[:7], refs[7:]
    dq_ref, dk_ref, dv_ref, tab_ref, normed_ref, inverse_ref, dxs_ref, dkt_ref, dvt_ref, pay_ref = refs[:10]
    place_ref, part_ref, group_sems, sems, pay_sems = refs[10:]
    tok_ref, a_ref, x_ref, slot_ref, weight_ref, dm_ref, go_ref = local
    step = pl.program_id(0)
    last = pl.num_programs(0) - 1
    slot = step % 2

    def fetches(group, place):
        return [
            pltpu.make_async_copy(source.at[pl.ds(2 * group, 2)], target.at[place], group_sems.at[place, n])
            for n, (source, target) in enumerate(zip(group_sources, group_local))
        ]

    def copies():
        return [
            pltpu.make_async_copy(source, target, sems.at[n])
            for n, (source, target) in enumerate(zip(sources, local))
        ]

    @pl.when(step == 0)
    def first():
        whole = copies()
        whole[0].start()
        for copy in fetches(0, 0):
            copy.start()
        for copy in whole[1:]:
            copy.start()
        for copy in fetches(1, 1):
            copy.start()
        slots = x_ref.shape[0] - own
        place_ref[...] = place_onehot(row_places(scalar_ref, kept_ref, own, slots), turned=True).T
        whole[0].wait()
        normed, inverse = norm_parts(tok_ref[...].astype(F32))
        normed_ref[...] = normed
        inverse_ref[...] = jnp.broadcast_to(inverse, inverse_ref.shape)

    @pl.when((step > 0) & (step + 1 < last))
    def following():
        for copy in fetches(step + 1, 1 - slot):
            copy.start()

    @pl.when(step < last)
    def attention():
        for copy in fetches(step, slot):
            copy.wait()
        outs = dq_ref.at[step], dk_ref.at[step], dv_ref.at[step], tab_ref.at[step]
        attend_back(own, *[ref.at[slot] for ref in group_local], place_ref, outs, (dkt_ref, dvt_ref, part_ref))

    @pl.when(step == last)
    def projections():
        for copy in copies()[1:]:
            copy.wait()
        groups = dq_ref.shape[0]
        total = tok_ref.shape[0]
        rows = x_ref.shape[0]
        slots = rows - own
        scale = mod_ref[1:2, :]
        here = row_span(scalar_ref, STARTS, own)

        def joined(ref, span):
            return jnp.concatenate([ref[n, span, :] for n in range(groups)], axis=1)

        every = slice(0, total)
        dk, dv = joined(dk_ref, every), joined(dv_ref, every)
        dq_own, dq_slot = joined(dq_ref, slice(0, own)), joined(dq_ref, slice(own, rows))
        column = lambda value: jnp.sum(value.astype(F32), axis=0, keepdims=True)
        lowered_t = a_ref[...].T
        pay_ref[0:D, :] = (mm(a_ref[here, :].T, dq_own) + mm(slot_ref[...].T, dq_slot)).astype(BF16)
        pay_ref[D : 2 * D, :] = mm(lowered_t, dk).astype(BF16)
        pay_ref[2 * D : 3 * D, :] = mm(lowered_t, dv).astype(BF16)
        pay_ref[3 * D : 4 * D, :] = go_ref[...]
        slot_normed, slot_inverse = norm_parts(x_ref[own:, :].astype(F32))
        da = mm_t(dq_slot, weight_ref[:, :D])
        shift_sum, scale_sum = column(da), column(da * slot_normed)
        spread = dm_ref[own:, :] + norm_back(slot_normed, slot_inverse, da * (1.0 + scale))
        chosen = slot_places(scalar_ref, kept_ref, slots) == lax.broadcasted_iota(jnp.int32, (slots, total), 1)
        chosen = chosen.astype(F32)
        moved = mm(chosen.astype(BF16).T, spread.astype(BF16))
        dxs_ref[...] = mm_t(dk, weight_ref[:, D : 2 * D]) + mm_t(dv, weight_ref[:, 2 * D :])
        dxs_ref[here, :] += mm_t(dq_own, weight_ref[:, :D])
        da = dxs_ref[...]
        normed = normed_ref[...]
        shift_sum, scale_sum = shift_sum + column(da), scale_sum + column(da * normed)
        inverse = jnp.concatenate([inverse_ref[...]] * (D // 128), axis=1)
        dxs_ref[...] = moved + norm_back(normed, inverse, da * (1.0 + scale))
        dx_own_ref[...] = dxs_ref[here, :] + dm_ref[:own, :]
        others = dx_ref.shape[0]
        for n in range(others):
            dx_ref[n] = dxs_ref[row_span(scalar_ref, STARTS + 1 + others + n, own), :].astype(BF16)
        rel = table_sums([tab_ref[n] for n in range(groups)])
        first = jnp.where(scalar_ref[SEQ_PLACE] == 0, 1, 0)
        label = scalar_ref[LABEL]
        number = lax.broadcasted_iota(jnp.int32, (1, D), 1)
        digits = jnp.where(number == scalar_ref[PLACE], label // GRID * first, 0)
        digits = jnp.where(number == 128 + scalar_ref[PLACE], label % GRID * first, digits).astype(F32)
        smalls = jnp.concatenate(
            [
                shift_sum, scale_sum, prior_ref[0:4, :], column(dq_own) + column(dq_slot), column(dv),
                *rel, prior_ref[4:5, :], digits, mod_ref[COND_LINE : COND_LINE + 1, :], jnp.zeros((3, D), F32),
            ],
            axis=0,
        ).astype(BF16)
        tail = pay_ref.shape[0] - 4 * D
        row = lax.broadcasted_iota(jnp.int32, (tail, 16), 0)
        lane = lax.broadcasted_iota(jnp.int32, (tail, 16), 1)
        kind = jnp.where(row < 6 * everyone, row // everyone, jnp.where(scalar_ref[SEQ_PLACE] == 0, 12, -1))
        wanted = jnp.where(row % everyone == scalar_ref[PLACE], kind, -1)
        after = row - 7 * everyone
        wanted = jnp.where(after < 0, wanted, jnp.where(after < 6, after + 6, -1))
        pay_ref[4 * D :, :] = mm((lane == wanted).astype(F32).astype(BF16), smalls).astype(BF16)
        halves = Copies(pay_sems)
        split_halves(halves, scalar_ref[SIDE], pay_ref, keep_ref, send_ref)
        halves.wait()


def table_sums(tabs):
    found = ([], [])
    for tab in tabs:
        for side in range(2):
            for part in range(2):
                at = 2 * side * GRID + part * GRID
                square = tab[part * GRID : (part + 1) * GRID, at : at + GRID]
                wide = jnp.concatenate([square, jnp.zeros((GRID, 128 - GRID), F32)], axis=1)
                turned = pltpu.roll(wide, 0, 1, stride=1, stride_axis=0)
                found[part].append(jnp.sum(turned, axis=0, keepdims=True)[:, : 2 * GRID])
    return [jnp.concatenate(parts, axis=1) for parts in found]


def call(kernel, outs, scratch, args, scalars=0, far=0, away=0, copies=0, micros=1, limit=32):
    scratches = [pltpu.VMEM(shape, dtype) for shape, dtype in scratch]
    if copies:
        scratches.append(pltpu.SemaphoreType.DMA((copies,)))
    return pl.pallas_call(
        kernel,
        out_shape=[jax.ShapeDtypeStruct(shape, dtype) for shape, dtype in outs[: len(outs) - away]]
        + [pltpu.HBM(shape, dtype) for shape, dtype in outs[len(outs) - away :]],
        in_specs=[smem] * scalars + [vmem] * (len(args) - scalars - far) + [hbm] * far,
        out_specs=[vmem] * (len(outs) - away) + [hbm] * away,
        scratch_shapes=scratches,
        compiler_params=pltpu.CompilerParams(vmem_limit_bytes=limit * MIB),
        cost_estimate=pl.CostEstimate(flops=micros * 10**9, bytes_accessed=MIB, transcendentals=0),
    )(*args)


def own_call(outs, scalars, sources):
    return pl.pallas_call(
        own_kernel,
        out_shape=[jax.ShapeDtypeStruct(shape, dtype) for shape, dtype in outs],
        in_specs=[smem] * len(scalars) + [hbm] * len(sources),
        out_specs=[smem] + [vmem] * (len(outs) - 1),
        scratch_shapes=[pltpu.VMEM(value.shape, value.dtype) for value in sources]
        + [pltpu.SemaphoreType.DMA((len(sources),))],
        compiler_params=pltpu.CompilerParams(vmem_limit_bytes=16 * MIB),
        cost_estimate=pl.CostEstimate(flops=3 * 10**9, bytes_accessed=MIB, transcendentals=0),
    )(*scalars, *map(in_hbm, sources))


def in_hbm(value):
    return pltpu.with_memory_space_constraint(value, pltpu.HBM)


def add_kernel(pieces, left_ref, right_ref, sum_out, sum_ref, sems):
    copies = Copies(sems)
    rows = sum_ref.shape[0] // pieces
    for n in range(pieces):
        span = pl.ds(n * rows, rows)
        sum_ref[span, :] = (left_ref[span, :].astype(F32) + right_ref[span, :].astype(F32)).astype(BF16)
        copies.start(sum_ref.at[span], sum_out.at[span])
    copies.wait()


def add_call(left, right, micros):
    pieces = 4 if left.shape[0] % 64 == 0 else 1
    out = (left.shape, BF16)
    return call(
        functools.partial(add_kernel, pieces), [out], [out], [left, right], away=1, copies=pieces, micros=micros,
        limit=8,
    )[0]


def spread_kernel(near_ref, far_ref, wide_out, sum_ref, sems):
    sum_ref[...] = (near_ref[...].astype(F32) + far_ref[...].astype(F32)).astype(BF16)
    copies = Copies(sems)
    for n in range(wide_out.shape[0]):
        copies.start(sum_ref, wide_out.at[n])
    copies.wait()


def spread_call(near, far, peers):
    return call(
        spread_kernel, [((peers,) + near.shape, BF16)], [(near.shape, BF16)], [near, far], away=1, copies=peers,
        limit=8,
    )[0]


def back_call(own, everyone, groups_of, sources, scalars, kept, mod, prior, tail_half):
    rows, total = groups_of[1].shape[1], groups_of[2].shape[1]
    groups = HEADS // 2
    others = total // own - 1
    whole = lambda shape: pl.BlockSpec(shape, lambda n: (0,) * len(shape))
    outs = [((tail_half, D), BF16), ((tail_half, D), BF16), ((others, own, D), BF16), ((own, D), F32)]
    scratch = [((2, 2) + value.shape[1:], value.dtype) for value in groups_of]
    scratch += [(value.shape, value.dtype) for value in sources]
    scratch += [
        ((groups, rows, 128), BF16), ((groups, total, 128), BF16), ((groups, total, 128), BF16),
        ((groups, 2 * GRID, 128), F32), ((total, D), F32), ((total, 128), F32), ((total, D), F32),
        ((128, total), F32), ((128, total), F32), ((2 * tail_half, D), BF16),
        ((2 * GRID, rows), BF16), ((rows, 128), BF16),
    ]
    small = [kept, mod, prior]
    return pl.pallas_call(
        functools.partial(back_kernel, own, everyone),
        grid=(groups + 1,),
        out_shape=[jax.ShapeDtypeStruct(shape, dtype) for shape, dtype in outs[:2]]
        + [pltpu.HBM(shape, dtype) for shape, dtype in outs[2:]],
        in_specs=[smem] + [whole(value.shape) for value in small] + [hbm] * (len(groups_of) + len(sources)),
        out_specs=[vmem, vmem] + [whole(shape) for shape, unused in outs[2:]],
        scratch_shapes=[pltpu.VMEM(shape, dtype) for shape, dtype in scratch]
        + [pltpu.SemaphoreType.DMA((2, 5)), pltpu.SemaphoreType.DMA((7,)), pltpu.SemaphoreType.DMA((2,))],
        compiler_params=pltpu.CompilerParams(
            vmem_limit_bytes=48 * MIB, dimension_semantics=("arbitrary",)
        ),
        cost_estimate=pl.CostEstimate(flops=18 * 10**9, bytes_accessed=MIB, transcendentals=0),
    )(scalars, *small, *map(in_hbm, groups_of), *map(in_hbm, sources))


def halves_reader(side_ref, mine_ref, other_ref):
    half = mine_ref.shape[0]

    def get(at, count):
        found = []
        for which in range(2):
            first, last = max(at, which * half), min(at + count, (which + 1) * half)
            if first < last:
                span = slice(first - which * half, last - which * half)
                found.append(jnp.where(side_ref[0] == which, mine_ref[span, :], other_ref[span, :]))
        return found[0] if len(found) == 1 else jnp.concatenate(found, axis=0)

    return get


def layer_kernel(side_ref, mine_ref, other_ref, bias1_ref, bias2_ref, g1_out, g2_out, g1_ref, g2_ref, sems):
    get = halves_reader(side_ref, mine_ref, other_ref)
    copies = Copies(sems)
    half = mine_ref.shape[0]
    for n in range(4):
        cols = pl.ds(n * D, D)
        g1_ref[:, cols] = get(n * D, D).astype(F32)
        copies.start(g1_ref.at[:, cols], g1_out.at[:, cols])
        g2_ref[cols, :] = get(half + n * D, D).astype(F32)
        copies.start(g2_ref.at[cols], g2_out.at[cols])
    small = get(FF, 16).astype(F32)
    for n in range(4):
        bias1_ref[pl.ds(n * D, D)] = small[n]
    bias2_ref[...] = small[4]
    copies.wait()


def last_kernel(
    everyone, side_ref, mine_ref, other_ref, ada_in, qv_ref, rel_ref, out_bias_ref, ada_bias_ref,
    gqkv_out, gada_out, table_out, go_out, gqkv_ref, gada_ref, table_ref, go_ref, ada_ref, sems,
):
    get = halves_reader(side_ref, mine_ref, other_ref)
    copies = Copies(sems)
    copies.start(ada_in, ada_ref)
    for n in range(3):
        cols = pl.ds(n * D, D)
        gqkv_ref[:, cols] = get(n * D, D).astype(F32)
        copies.start(gqkv_ref.at[:, cols], gqkv_out.at[:, cols])
    go_ref[...] = get(3 * D, D).astype(F32)
    copies.start(go_ref, go_out)
    cond = get(4 * D + 6 * everyone, everyone).astype(F32)
    gate = 1.0 / (1.0 + jnp.exp(-cond))
    act_t = (cond * gate).astype(BF16).T
    dmods = [get(4 * D + n * everyone, everyone) for n in range(6)]
    for n in range(6):
        cols = pl.ds(n * D, D)
        gada_ref[:, cols] = mm(act_t, dmods[n])
        copies.start(gada_ref.at[:, cols], gada_out.at[:, cols])
        ada_bias_ref[cols] = jnp.sum(dmods[n].astype(F32), axis=0)
    copies.made.pop(0).wait()
    back = jnp.zeros((everyone, D), F32)
    for n in range(6):
        back = back + mm_t(dmods[n], ada_ref[:, n * D : (n + 1) * D])
    back = gate * (1.0 + cond * (1.0 - gate)) * back
    high = back.astype(BF16)
    low = (back - high.astype(F32)).astype(BF16)
    small = get(4 * D + 7 * everyone, 16).astype(F32)
    label = (small[5:6, :everyone] * GRID + small[5:6, 128 : 128 + everyone]).astype(jnp.int32)
    classes = table_ref.shape[0]
    wide = round_up(classes, 128)
    hot = (label == lax.broadcasted_iota(jnp.int32, (wide, everyone), 0)).astype(F32).astype(BF16)
    table_ref[...] = (mm(hot, high) + mm(hot, low))[:classes]
    copies.start(table_ref, table_out)
    qv_ref[...] = small[:2]
    for part in range(2):
        for head in range(HEADS):
            at = 2 * GRID * head
            rel_ref[head, part : part + 1, :] = small[2 + part : 3 + part, at : at + 2 * GRID - 1]
    out_bias_ref[...] = small[4]
    copies.wait()


def swap_cores(value, dp):
    return lax.ppermute(value, "dp", [(n, n ^ 1) for n in range(dp)])


def exchange(value, dp, seq):
    groups = [
        [(far * (dp // 2) + 2 * pair + core) * seq + at for pair in range(dp // 4) for at in range(seq)]
        for far in range(2)
        for core in range(2)
    ]
    return lax.all_to_all(value, AXES, 0, 0, axis_index_groups=groups)


def near_sum(pieces):
    return jnp.sum(pieces.astype(F32), axis=0).astype(BF16)


def far_half(near, dp):
    return lax.ppermute(near, "dp", [(n, (n + dp // 2) % dp) for n in range(dp)])


def assemble_kernel(cut, place_ref, pair_ref, a1_ref, b1_ref, a2_ref, b2_ref, half_ref):
    rows = pair_ref.shape[1]
    for near in range(2):
        for x in range(2):
            for y in range(2):
                at = (place_ref[0] ^ (4 * near + 2 * x + y)) * rows
                if x:
                    half_ref[pl.ds(pl.multiple_of(at, 16), cut), :] = a2_ref[y, near]
                elif y:
                    half_ref[pl.ds(pl.multiple_of(at, 16), cut), :] = a1_ref[near]
                else:
                    half_ref[pl.ds(pl.multiple_of(at, 16), cut), :] = pair_ref[near, :cut, :]
                rest = pl.ds(pl.multiple_of(at + cut, 16), rows - cut)
                if y:
                    half_ref[rest, :] = b2_ref[x, near]
                elif x:
                    half_ref[rest, :] = b1_ref[near]
                else:
                    half_ref[rest, :] = pair_ref[near, cut:, :]


def after(value, *others):
    return lax.optimization_barrier((value, *others))[0]


def gather_chunks(chunk, last_near, before, finish, dp, seq):
    rows = chunk.shape[0]
    cut = round_up(rows // 2, 16)
    place = lax.axis_index("dp") % (dp // 2) // 2 * seq + lax.axis_index("seq")
    along_x = lambda value: lax.ppermute(value, "dp", [(n, n ^ 2) for n in range(dp)])
    along_y = lambda value: lax.ppermute(value, "seq", [(n, n ^ 1) for n in range(seq)])
    chunk = after(chunk, last_near, before)
    last_wide = finish(last_near)
    pair = jnp.stack([chunk, lax.ppermute(chunk, "dp", [(n, n ^ 4) for n in range(dp)])])
    a, b = pair[:, :cut], pair[:, cut:]
    a1, b1 = along_y(a), along_x(b)
    a, b = jnp.stack([a, a1]), jnp.stack([b, b1])
    a, b, last_wide = lax.optimization_barrier((a, b, last_wide))
    a2, b2 = along_x(a), along_y(b)
    held = (a2, b2)

    def assemble(a2, b2):
        return call(
            functools.partial(assemble_kernel, cut), [((8 * rows, D), BF16)], [],
            [place.astype(jnp.int32).reshape(1), pair, a1, b1, a2, b2], scalars=1, limit=8,
        )[0]

    return (a2, b2), assemble, last_wide, held


def scatter_rows(partial, seq):
    return [
        lax.ppermute(partial[step - 1], "seq", [(n, (n + step) % seq) for n in range(seq)])
        for step in range(1, seq)
    ]


def body(
    dp, seq, image_tokens, kept_index, kept_count, sample_valid, timestep, class_label, class_table,
    ada_weight, ada_bias, qkv_weight, qv_bias, rel_bias, out_weight, out_bias, fc1_weight,
    fc1_bias, fc2_weight, fc2_bias, grad_full, grad_masked,
):
    samples, own, width = image_tokens.shape
    held = kept_index.shape[1]
    slots = grad_masked.shape[1]
    padded = round_up(slots, 16)
    rows = own + padded
    total = own * seq
    everyone = dp * samples
    classes = class_table.shape[0]
    dp_place, seq_place = lax.axis_index("dp"), lax.axis_index("seq")

    half = round_up(FF + 16, dp * seq * 4)
    peers = dp // 4 * seq
    side = dp_place % 2
    sides = side.astype(jnp.int32).reshape(1)
    tail_half = round_up(4 * D + 16 + 7 * everyone, dp * seq * 4) // 2
    kept_of = []
    for s in range(samples):
        tokens = [image_tokens[s]]
        for step in range(1, seq):
            tokens.append(lax.ppermute(tokens[0], "seq", [(n, (n + step) % seq) for n in range(seq)]))
        number = jnp.arange(STARTS + 2 * seq - 1, dtype=jnp.int32)
        block = number - STARTS
        scalars = jnp.where(block < seq, seq_place - block, seq_place + block - seq + 1) % seq * own
        entries = {
            SIDE: side, PLACE: dp_place * samples + s, SLOT_START: seq_place * slots, SEQ_PLACE: seq_place,
        }
        for at, entry in entries.items():
            scalars = jnp.where(number == at, entry, scalars)
        places = scalars.astype(jnp.int32)
        held_rows = held + padded - slots
        cot_slot = jnp.pad(grad_masked[s], ((0, padded - slots), (0, 0)))
        one = slice(s, s + 1)
        scalars, kept, lines, mod, *owned, mask = own_call(
            [
                (places.shape, jnp.int32), ((held_rows, 1), jnp.int32), ((16, D), F32),
                ((8, D), F32), ((own, D), BF16), ((own, D), BF16), ((HEADS, own, 128), BF16),
                ((HEADS, own, 128), BF16), ((HEADS, own, 128), BF16), ((padded, D), BF16), ((8, total), F32),
            ],
            [places, kept_count[one], sample_valid[one], timestep[one], class_label[one]],
            [
                kept_index[one], rel_bias.transpose(1, 0, 2), ada_bias, qv_bias, out_bias, fc1_bias, fc2_bias,
                class_table, ada_weight, tokens[0], qkv_weight,
            ],
        )
        qaug, kaug, vaug, x, lowered, whole, slot = call(
            functools.partial(prep_kernel, seq),
            [
                ((HEADS, rows, 128), BF16), ((HEADS, total, 128), BF16), ((HEADS, total, 128), BF16),
                ((rows, D), BF16), ((total, D), BF16), ((total, D), BF16), ((padded, D), BF16),
            ],
            [((total, D), BF16), ((total, D), BF16), ((total, D), BF16), ((padded, D), BF16)],
            [scalars, *tokens, *owned, kept, mod, qkv_weight, lines],
            scalars=1, away=3, copies=3, micros=3, limit=16,
        )
        mixed, inverse, spread_far, qaug_far, kaug_far, vaug_far = call(
            functools.partial(attend_kernel, own),
            [
                ((HEADS // 2, rows, 128), F32), ((HEADS // 2, rows, 128), F32),
                ((HEADS, rows, total), BF16), (qaug.shape, BF16), (kaug.shape, BF16), (vaug.shape, BF16),
            ],
            [((HEADS, rows, total), BF16)],
            [qaug, kaug, vaug, mask],
            away=4, copies=3 + 8 * HEADS, micros=10, limit=32,
        )
        attended, hidden, du, keep, send = call(
            functools.partial(feed_kernel, slots),
            [((rows, D), F32), ((rows, FF), BF16), ((rows, FF), BF16), ((half, D), BF16), ((half, D), BF16)],
            [((2, half, D), BF16)],
            [
                scalars, mixed, x, grad_full[s], cot_slot, mod, out_weight, fc1_weight, fc2_weight, lines,
            ],
            scalars=1, copies=2, micros=10, limit=24,
        )
        kept_of.append(dict(
            rest=[
                scalars, mixed, inverse, x, grad_full[s], cot_slot, mod, out_weight, fc1_weight, fc2_weight,
                lines, attended, hidden, du,
            ],
            groups=[spread_far, qaug_far, kaug_far, vaug_far], sources=[whole, lowered, slot, qkv_weight],
            small=[scalars, kept, mod], keep=keep, send=send,
        ))

    def added(arrays):
        if len(arrays) == 1:
            return arrays[0]
        return functools.reduce(jnp.add, [a.astype(F32) for a in arrays]).astype(arrays[0].dtype)

    keep, send = added([k["keep"] for k in kept_of]), added([k["send"] for k in kept_of])
    got = swap_cores(send, dp)

    rests = [
        call(
            functools.partial(feed_rest_kernel, slots),
            [
                ((8, D), F32), ((own, D), BF16), ((padded, D), BF16), ((rows, D), F32), ((rows, D), BF16),
                ((HEADS, rows, 128), BF16), ((D, D), BF16),
            ],
            [((rows, D), BF16), ((rows, D), F32), ((HEADS, rows, 128), BF16), ((D, D), BF16)],
            k["rest"],
            scalars=1, away=6, copies=6, micros=6, limit=24,
        )
        for k in kept_of
    ]
    mine = add_call(keep, got, 1)
    mine, rests = lax.optimization_barrier((mine, rests))
    pieces = exchange(mine.reshape(peers, half // peers, D), dp, seq)
    tails = []
    for k, rest in zip(kept_of, rests):
        small, unused_full, unused_slot, dmid, x_far, dout_far, grad_out = rest
        whole, lowered, slot, weights = k["sources"]
        tails.append(
            back_call(
                own, everyone, [*k["groups"], dout_far], [whole, lowered, x_far, slot, weights, dmid, grad_out],
                *k["small"], small, tail_half,
            )
        )

    keep, send = added([t[0] for t in tails]), added([t[1] for t in tails])
    keep, send, pieces = lax.optimization_barrier((keep, send, pieces))
    got = swap_cores(send, dp)
    mine = add_call(keep, got, 1).reshape(peers, tail_half // peers, D)
    pieces, mine = lax.optimization_barrier((pieces, mine))
    near = near_sum(pieces)
    far = far_half(near, dp)
    first_moved = [scatter_rows(t[2][:, : own // 2], seq) for t in tails]
    last_moved = [scatter_rows(t[2][:, own // 2 :], seq) for t in tails]
    last_near = near_sum(exchange(mine, dp, seq))

    def finish(last_near):
        wide = spread_call(last_near, far_half(last_near, dp), peers)
        return wide

    if dp == 16 and seq == 2:
        chunk = (near.astype(F32) + far.astype(F32)).astype(BF16)
        parts, assemble, last_wide, held = gather_chunks(chunk, last_near, first_moved, finish, dp, seq)
    else:
        parts = exchange(spread_call(near, far, peers), dp, seq).reshape(half, D)
        assemble = lambda whole: whole
        parts = (parts,)
        held = parts
        last_wide = finish(last_near)
    last_half = exchange(last_wide, dp, seq).reshape(tail_half, D)
    out_full = jnp.stack([rest[1] for rest in rests])
    out_masked = jnp.stack([rest[2][:slots] for rest in rests])
    layer_half = assemble(*parts)
    last_half = after(last_half, layer_half)
    grad_fc1_bias, grad_fc2_bias, grad_fc1, grad_fc2 = call(
        layer_kernel,
        [((FF,), F32), ((D,), F32), ((D, FF), F32), ((FF, D), F32)],
        [((D, FF), F32), ((FF, D), F32)],
        [sides, layer_half, swap_cores(layer_half, dp)],
        scalars=1, away=2, copies=8, micros=3,
    )
    grad_qv, grad_rel, grad_out_bias, grad_ada_bias, grad_qkv, grad_ada, grad_table, grad_out = call(
        functools.partial(last_kernel, everyone),
        [
            ((2, D), F32), ((HEADS, 2, 2 * GRID - 1), F32), ((D,), F32), ((6 * D,), F32),
            ((D, 3 * D), F32), ((D, 6 * D), F32), ((classes, D), F32), ((D, D), F32),
        ],
        [((D, 3 * D), F32), ((D, 6 * D), F32), ((classes, D), F32), ((D, D), F32), (ada_weight.shape, BF16)],
        [sides, last_half, swap_cores(last_half, dp), in_hbm(ada_weight)],
        scalars=1, far=1, away=4, copies=12, micros=4, limit=16,
    )
    grad_rel = grad_rel.transpose(1, 0, 2)
    grad_qkv, last_moved = lax.optimization_barrier((grad_qkv, last_moved))
    grad_input = []
    for tail, *moved in zip(tails, first_moved, last_moved):
        came = [jnp.concatenate(both).astype(F32) for both in zip(*moved)]
        grad_input.append(functools.reduce(jnp.add, came, tail[3]))
    grad_input = jnp.stack(grad_input)
    return (
        out_full, out_masked, grad_input, grad_table, grad_ada, grad_ada_bias, grad_qkv, grad_qv,
        grad_rel, grad_out, grad_out_bias, grad_fc1, grad_fc1_bias, grad_fc2, grad_fc2_bias,
    )


def solution(mesh):
    split = P("dp", "seq", None)
    placed = (split, P("dp", None)) + (P("dp"),) * 4 + (P(),) * 12 + (split, split)
    return jax.shard_map(
        functools.partial(body, mesh.shape["dp"], mesh.shape["seq"]),
        mesh=mesh,
        in_specs=placed,
        out_specs=(split,) * 3 + (P(),) * 12,
        check_vma=False,
    )
```

```python
import functools
import math

import jax
import jax.numpy as jnp
from jax import lax
from jax.experimental import pallas as pl
from jax.experimental.pallas import tpu as pltpu
from jax.sharding import PartitionSpec as P

D = 384
HEADS = 6
HDIM = 64
GRID = 32
FF = 1536
CHUNK = 256

AXES = ("dp", "seq")
F32 = jnp.float32
BF16 = jnp.bfloat16
MIB = 1024 * 1024
GELU_A = math.sqrt(2.0 / math.pi)
GELU_B = 0.044715

highest = lax.Precision.HIGHEST
big_negative = -1e30
vmem = pl.BlockSpec(memory_space=pltpu.VMEM)
smem = pl.BlockSpec(memory_space=pltpu.SMEM)
hbm = pl.BlockSpec(memory_space=pltpu.HBM)


def round_up(value, step):
    return -(-value // step) * step


def blocks_of(first, count, most):
    pieces = -(-count // most)
    size = round_up(-(-count // pieces), 16)
    found = []
    at = 0
    while at < count:
        found.append((first + at, min(size, count - at)))
        at += size
    return found


def mm(left, right):
    return lax.dot_general(left, right, (((1,), (0,)), ((), ())), preferred_element_type=F32)


def mm_t(left, right):
    return lax.dot_general(left, right, (((1,), (1,)), ((), ())), preferred_element_type=F32)


def norm_parts(value):
    average = jnp.mean(value, axis=-1, keepdims=True)
    centred = value - average
    variance = jnp.mean(centred * centred, axis=-1, keepdims=True)
    inverse = lax.rsqrt(variance + 1e-06)
    return (centred * inverse, inverse)


def norm_back(normed, inverse, grad):
    first = jnp.mean(grad, axis=-1, keepdims=True)
    second = jnp.mean(grad * normed, axis=-1, keepdims=True)
    return inverse * (grad - first - normed * second)


def place_onehot(position, turned=False):
    lane = lax.broadcasted_iota(jnp.int32, (position.shape[0], 2 * GRID), 1)
    if turned:
        lane = jnp.where(lane < GRID, GRID - 1 - lane, 3 * GRID - 1 - lane)
    wanted = jnp.where(lane < GRID, position // GRID, position % GRID + GRID)
    return (lane == wanted).astype(F32).astype(BF16)


class Copies:
    def __init__(self, sems):
        self.sems, self.made, self.count = sems, [], 0

    def start(self, source, target):
        copy = pltpu.make_async_copy(source, target, self.sems.at[self.count])
        copy.start()
        self.made.append(copy)
        self.count += 1

    def wait(self):
        for copy in self.made:
            copy.wait()


def half_copies(side, payload_ref, keep_ref, send_ref, sems, which):
    for target, chosen in ((keep_ref, side == which), (send_ref, side != which)):

        @pl.when(chosen)
        def start():
            pltpu.make_async_copy(payload_ref.at[which], target, sems.at[which]).start()


def split_halves(copies, side, payload_ref, keep_ref, send_ref):
    half = keep_ref.shape[0]
    for which, target in ((side, keep_ref), (1 - side, send_ref)):
        copies.start(payload_ref.at[pl.ds(pl.multiple_of(which * half, 16), half)], target)


SIDE, PLACE, SLOT_START, COUNT, VALID, LABEL, SEQ_PLACE, STARTS = range(8)


def row_span(scalar_ref, number, count):
    return pl.ds(pl.multiple_of(scalar_ref[number], 16), count)


def slot_places(scalar_ref, kept_ref, slots):
    return kept_ref[pl.ds(pl.multiple_of(scalar_ref[SLOT_START], 8), slots), :]


def row_places(scalar_ref, kept_ref, own, slots):
    mine = lax.broadcasted_iota(jnp.int32, (own, 1), 0) + scalar_ref[STARTS]
    return jnp.concatenate([mine, slot_places(scalar_ref, kept_ref, slots)], axis=0)


def row_weights(scalar_ref, own, slots, rows):
    row = lax.broadcasted_iota(jnp.int32, (rows, 1), 0)
    kept = (row < own + slots) & (row - own + scalar_ref[SLOT_START] < scalar_ref[COUNT])
    return jnp.where((row < own) | kept, scalar_ref[VALID], 0).astype(F32)


def project(tokens, mod_ref, weight_ref, line_ref):
    normed, unused = norm_parts(tokens.astype(F32))
    lowered = (normed * (1.0 + mod_ref[1:2, :]) + mod_ref[0:1, :]).astype(BF16)
    query = (mm(lowered, weight_ref[:, :D]) + line_ref[QV_LINE : QV_LINE + 1, :]).astype(BF16)
    scaled = (query.astype(F32) * (1.0 / math.sqrt(HDIM))).astype(BF16)
    keys = mm(lowered, weight_ref[:, D : 2 * D]).astype(BF16)
    values = (mm(lowered, weight_ref[:, 2 * D :]) + line_ref[QV_LINE + 1 : QV_LINE + 2, :]).astype(BF16)
    return lowered, scaled, keys, values


def head_cols(head):
    return slice(head * HDIM, (head + 1) * HDIM)


def ones_lanes(count):
    return (lax.broadcasted_iota(jnp.int32, (count, HDIM), 1) < 2).astype(F32).astype(BF16)


def bias_table(rel_ref):
    lane = lax.broadcasted_iota(jnp.int32, (GRID, 128), 1)
    parts = []
    for part in range(2):
        tiles = []
        for group in range(HEADS // 2):
            tile = jnp.zeros((GRID, 128), F32)
            for side in range(2):
                head = 2 * group + side
                line = rel_ref[head, part : part + 1, :].astype(F32)
                line = jnp.concatenate([line, jnp.zeros((1, 128 - line.shape[1]), F32)], axis=1)
                first = side * HDIM + part * GRID
                turned = pltpu.roll(
                    jnp.broadcast_to(line, (GRID, 128)), (first + 128 - (GRID - 1)) % 128, 1,
                    stride=1, stride_axis=0,
                )
                tile = jnp.where((lane >= first) & (lane < first + GRID), turned, tile)
            tiles.append(tile)
        parts.append(jnp.concatenate(tiles, axis=1))
    return jnp.concatenate(parts, axis=0).astype(BF16)


QV_LINE, OUT_LINE, FC1_LINE, FC2_LINE = 6, 8, 9, 13
COND_LINE = 6


def time_features(moment):
    half = D // 2
    lane = lax.broadcasted_iota(jnp.int32, (1, D), 1)
    number = jnp.where(lane < half, lane, lane - half).astype(F32)
    angle = moment.astype(F32) * jnp.exp(-math.log(10000.0) * number / half)
    return jnp.where(lane < half, jnp.cos(angle), jnp.sin(angle))


def own_kernel(
    start_ref, count_ref, valid_ref, moment_ref, label_ref,
    *refs,
):
    sources, outs, local, sems = refs[:11], refs[11:22], refs[22:33], refs[33]
    scalar_ref, kept_ref, line_ref, mod_ref, a_ref, qs_ref, qaug_ref, kaug_ref, vaug_ref = outs[:9]
    offset_ref, mask_ref = outs[9:]
    kept_in, rel_ref, ada_bias_ref, qv_bias_ref, out_bias_ref, fc1_bias_ref, fc2_bias_ref = local[:7]
    table_ref, ada_ref, tok_ref, weight_ref = local[7:]
    fetched = [pltpu.make_async_copy(*pair, sems.at[n]) for n, pair in enumerate(zip(sources, local))]
    for copy in fetched:
        copy.start()
    for copy in fetched[:7]:
        copy.wait()
    own = tok_ref.shape[0]
    slots = offset_ref.shape[0]
    total = mask_ref.shape[1]
    held = kept_ref.shape[0]
    label = label_ref[0]
    for n in range(scalar_ref.shape[0]):
        scalar_ref[n] = start_ref[n]
    scalar_ref[COUNT] = count_ref[0]
    scalar_ref[VALID] = valid_ref[0]
    scalar_ref[LABEL] = label
    width = round_up(held, 128)
    kept = jnp.concatenate([kept_in[...], jnp.zeros((1, width - kept_in.shape[1]), jnp.int32)], axis=1)
    kept_ref[...] = jnp.broadcast_to(kept, (8, width)).T[:held, :1]
    place = place_onehot(row_places(start_ref, kept_ref, own, slots))
    offsets = mm(place, bias_table(rel_ref)).astype(BF16)
    offset_ref[...] = offsets[own:]
    number = lax.broadcasted_iota(jnp.int32, (held, 1), 0)
    live = jnp.where(number < count_ref[0], kept_ref[...], -1)
    hit = live == lax.broadcasted_iota(jnp.int32, (held, total), 1)
    count = jnp.sum(hit.astype(F32), axis=0, keepdims=True)
    mask_ref[...] = jnp.broadcast_to(jnp.where(count > 0.0, 0.0, big_negative), mask_ref.shape)
    for n in range(6):
        line_ref[n : n + 1, :] = ada_bias_ref[pl.ds(n * D, D)].astype(F32).reshape(1, D)
    line_ref[QV_LINE : QV_LINE + 2, :] = qv_bias_ref[...].astype(F32)
    line_ref[OUT_LINE : OUT_LINE + 1, :] = out_bias_ref[...].astype(F32).reshape(1, D)
    for n in range(4):
        line_ref[FC1_LINE + n : FC1_LINE + n + 1, :] = fc1_bias_ref[pl.ds(n * D, D)].astype(F32).reshape(1, D)
    line_ref[FC2_LINE : FC2_LINE + 1, :] = fc2_bias_ref[...].astype(F32).reshape(1, D)
    line_ref[FC2_LINE + 1 :, :] = jnp.zeros((2, D), F32)
    for copy in fetched[7:]:
        copy.wait()
    hot = lax.broadcasted_iota(jnp.int32, (16, table_ref.shape[0]), 1) == label
    conditioned = mm(hot.astype(F32).astype(BF16), table_ref[...]) + time_features(moment_ref[0])
    gate = 1.0 / (1.0 + jnp.exp(-conditioned))
    activated = (conditioned * gate).astype(BF16)
    for n in range(6):
        mod_ref[n : n + 1, :] = mm(activated, ada_ref[:, n * D : (n + 1) * D])[:1] + line_ref[n : n + 1, :]
    mod_ref[COND_LINE : COND_LINE + 1, :] = conditioned[:1]
    mod_ref[COND_LINE + 1 :, :] = jnp.zeros((1, D), F32)
    lowered, scaled, keys, values = project(tok_ref[...], mod_ref, weight_ref, line_ref)
    a_ref[...] = lowered
    qs_ref[...] = scaled
    for head in range(HEADS):
        cols = head_cols(head)
        qaug_ref[head] = jnp.concatenate([scaled[:, cols], offsets[:own, cols]], axis=1)
        kaug_ref[head] = jnp.concatenate([keys[:, cols], place[:own]], axis=1)
        vaug_ref[head] = jnp.concatenate([values[:, cols], ones_lanes(own)], axis=1)


def prep_kernel(seq, scalar_ref, *refs):
    token_refs, refs = refs[:seq], refs[seq:]
    own_a_ref, own_qs_ref, own_qaug_ref, own_kaug_ref, own_vaug_ref, offset_ref = refs[:6]
    kept_ref, mod_ref, weight_ref, line_ref = refs[6:10]
    qaug_ref, kaug_ref, vaug_ref, x_ref, a_out, tok_out, slot_out = refs[10:17]
    qs_ref, a_ref, tok_ref, slot_ref, sems = refs[17:]
    copies = Copies(sems)
    own = token_refs[0].shape[0]
    slots, total = offset_ref.shape[0], tok_ref.shape[0]
    for n in range(seq):
        tok_ref[row_span(scalar_ref, STARTS + n, own), :] = token_refs[n][...]
    copies.start(tok_ref, tok_out)
    others = [token_refs[n][...] for n in range(1, seq)]
    others = others[0] if seq == 2 else jnp.concatenate(others, axis=0)
    lowered, scaled, keys, values = project(others, mod_ref, weight_ref, line_ref)
    here = row_span(scalar_ref, STARTS, own)
    a_ref[here, :] = own_a_ref[...]
    qs_ref[here, :] = own_qs_ref[...]
    for head in range(HEADS):
        kaug_ref[head, here, :] = own_kaug_ref[head]
        vaug_ref[head, here, :] = own_vaug_ref[head]
        qaug_ref[head, :own, :] = own_qaug_ref[head]
    for n in range(1, seq):
        there = row_span(scalar_ref, STARTS + n, own)
        span = slice((n - 1) * own, n * own)
        a_ref[there, :] = lowered[span]
        qs_ref[there, :] = scaled[span]
        place = place_onehot(lax.broadcasted_iota(jnp.int32, (own, 1), 0) + scalar_ref[STARTS + n])
        for head in range(HEADS):
            cols = head_cols(head)
            kaug_ref[head, there, :] = jnp.concatenate([keys[span, cols], place], axis=1)
            vaug_ref[head, there, :] = jnp.concatenate([values[span, cols], ones_lanes(own)], axis=1)
    copies.start(a_ref, a_out)
    chosen = slot_places(scalar_ref, kept_ref, slots) == lax.broadcasted_iota(jnp.int32, (slots, total), 1)
    chosen = chosen.astype(F32).astype(BF16)
    x_ref[:own, :] = token_refs[0][...]
    x_ref[own:, :] = mm(chosen, tok_ref[...]).astype(BF16)
    slot_ref[...] = mm(chosen, a_ref[...]).astype(BF16)
    copies.start(slot_ref, slot_out)
    query = mm(chosen, qs_ref[...]).astype(BF16)
    for head in range(HEADS):
        cols = head_cols(head)
        qaug_ref[head, own:, :] = jnp.concatenate([query[:, cols], offset_ref[:, cols]], axis=1)
    copies.wait()


def attend_kernel(
    own, qaug_ref, kaug_ref, vaug_ref, mask_ref, o_ref, inverse_ref, e_out, qaug_out, kaug_out, vaug_out, e_ref, sems
):
    rows = qaug_ref.shape[1]
    copies = Copies(sems)
    copies.start(qaug_ref, qaug_out)
    copies.start(kaug_ref, kaug_out)
    copies.start(vaug_ref, vaug_out)
    spans = [(at, size, False) for at, size in blocks_of(0, own, 256)]
    spans += [(at, size, True) for at, size in blocks_of(own, rows - own, 256)]
    items = [(side, *span) for side in range(2) for span in spans]

    def e_copy(head, n):
        side, at, size, masked = items[n]
        span = pl.ds(at, size)
        return pltpu.make_async_copy(
            e_ref.at[head, span], e_out.at[head, span], sems.at[3 + len(spans) * head + n % len(spans)]
        )

    def pair(group, carry):
        scores, spread = {}, {}
        for n in range(len(items) + 2):
            if n < len(items):
                side, at, size, masked = items[n]
                head = 2 * group + side
                scores[n] = mm_t(qaug_ref[head, at : at + size, :], kaug_ref[head])
                if masked:
                    scores[n] = scores[n] + mask_ref[0:1, :]
            if 0 <= n - 1 < len(items):
                side, at, size, masked = items[n - 1]
                found = scores.pop(n - 1)
                spread[n - 1] = jnp.exp(found - jnp.max(found, axis=-1, keepdims=True)).astype(BF16)
                e_ref[2 * group + side, at : at + size, :] = spread[n - 1]
                e_copy(2 * group + side, n - 1).start()
            if 0 <= n - 2:
                side, at, size, masked = items[n - 2]
                mixed = mm(spread.pop(n - 2), vaug_ref[2 * group + side])
                inverse = 1.0 / mixed[:, HDIM : HDIM + 1]
                lanes = slice(side * HDIM, (side + 1) * HDIM)
                o_ref[group, at : at + size, lanes] = mixed[:, :HDIM] * inverse
                inverse_ref[group, at : at + size, lanes] = jnp.broadcast_to(inverse, (size, HDIM))
        return carry

    lax.fori_loop(0, HEADS // 2, pair, 0)
    for head in range(HEADS):
        for n in range(len(spans)):
            e_copy(head, head % 2 * len(spans) + n).wait()
    copies.wait()


def cotangents(scalar_ref, slots, full_ref, slot_ref):
    own = full_ref.shape[0]
    weight = row_weights(scalar_ref, own, slots, own + slot_ref.shape[0])
    return weight, jnp.concatenate([full_ref[...], slot_ref[...]], axis=0).astype(F32) * weight


def feed_kernel(
    slots, scalar_ref, o_ref, x_ref, cot_full_ref, cot_slot_ref, mod_ref, wout_ref, w1_ref,
    w2_ref, line_ref,
    att_ref, hidden_ref, du_ref, bias_ref, keep_ref, send_ref, pay_ref, sems,
):
    rows = x_ref.shape[0]
    gate1, shift2, scale2, gate2 = [mod_ref[n : n + 1, :] for n in range(2, 6)]
    merged = jnp.concatenate([o_ref[n] for n in range(HEADS // 2)], axis=1).astype(BF16)
    attended = mm(merged, wout_ref[...]) + line_ref[OUT_LINE : OUT_LINE + 1, :]
    att_ref[...] = attended
    normed, unused = norm_parts(x_ref[...].astype(F32) + gate1 * attended)
    second = (normed * (1.0 + scale2) + shift2).astype(BF16)
    unused, cot = cotangents(scalar_ref, slots, cot_full_ref, cot_slot_ref)
    dz = (gate2 * cot).astype(BF16)

    bias = jnp.concatenate([line_ref[FC1_LINE + n : FC1_LINE + n + 1, :] for n in range(4)], axis=1)

    def products(c):
        cols = slice(c * CHUNK, (c + 1) * CHUNK)
        return mm(second, w1_ref[:, cols]) + bias[:, cols], mm_t(dz, w2_ref[cols, :])

    chunks = FF // CHUNK
    ready = products(0)
    for c in range(chunks):
        u, back_u = ready
        if c + 1 < chunks:
            ready = products(c + 1)
        cols = slice(c * CHUNK, (c + 1) * CHUNK)
        square = u * u
        t = jnp.tanh(u * (square * (GELU_A * GELU_B) + GELU_A))
        cdf = t * 0.5 + 0.5
        hidden_ref[:, cols] = (u * cdf).astype(BF16)
        slope = cdf * ((1.0 - t) * (u * (square * (3.0 * GELU_A * GELU_B) + GELU_A)) + 1.0)
        du_ref[:, cols] = (slope * back_u).astype(BF16)
    ones = jnp.ones((16, rows), BF16)
    grad = mm(jnp.concatenate([second.T, ones], axis=0), du_ref[...])
    heads = []
    for n in range(4):
        cols = slice(n * D, (n + 1) * D)
        pay_ref[0, cols, :] = grad[:D, cols].astype(BF16)
        heads.append(grad[D : D + 1, cols])
    heads += [jnp.sum(dz.astype(F32), axis=0, keepdims=True), jnp.zeros((3, D), F32)]
    bias_ref[...] = jnp.concatenate(heads, axis=0)
    pay_ref[1, :FF, :] = mm(hidden_ref[...].T, dz).astype(BF16)
    if pay_ref.shape[1] > FF:
        pay_ref[:, FF:, :] = jnp.zeros((2, pay_ref.shape[1] - FF, D), BF16)
    for which in range(2):
        half_copies(scalar_ref[SIDE], pay_ref, keep_ref, send_ref, sems, which)
    for which in range(2):
        pltpu.make_async_copy(pay_ref.at[which], keep_ref, sems.at[which]).wait()


def feed_rest_kernel(
    slots, scalar_ref, o_ref, inverse_ref, x_ref, cot_full_ref, cot_slot_ref, mod_ref, wout_ref, w1_ref,
    w2_ref, line_ref,
    att_ref, hidden_ref, du_ref, bias_ref,
    small_ref, y_full_out, y_slot_out, dm_out, x_out, do_out, go_out, y_ref, dm_ref, do_ref, go_ref, sems,
):
    rows, own = x_ref.shape[0], cot_full_ref.shape[0]
    copies = Copies(sems)
    copies.start(x_ref, x_out)
    gate1, shift2, scale2, gate2 = [mod_ref[n : n + 1, :] for n in range(2, 6)]
    weight, cot = cotangents(scalar_ref, slots, cot_full_ref, cot_slot_ref)
    back = mm_t(du_ref[...], w1_ref[...])
    branch = mm(hidden_ref[...], w2_ref[...]) + line_ref[FC2_LINE : FC2_LINE + 1, :]
    attended = att_ref[...]
    middle = x_ref[...].astype(F32) + gate1 * attended
    normed, inverse = norm_parts(middle)
    y_ref[...] = ((middle + gate2 * branch) * weight).astype(BF16)
    copies.start(y_ref.at[pl.ds(0, own)], y_full_out)
    copies.start(y_ref.at[pl.ds(own, rows - own)], y_slot_out)
    dmid = cot + norm_back(normed, inverse, back * (1.0 + scale2))
    dm_ref[...] = dmid
    copies.start(dm_ref, dm_out)
    datt = (gate1 * dmid).astype(BF16)
    merged_f = jnp.concatenate([o_ref[n] for n in range(HEADS // 2)], axis=1)
    dout = mm_t(datt, wout_ref[...]) * jnp.concatenate([inverse_ref[n] for n in range(HEADS // 2)], axis=1)
    dout = dout.astype(BF16).astype(F32)
    product = dout * merged_f
    high = product.astype(BF16)
    low = (product - high.astype(F32)).astype(BF16)
    row = lax.broadcasted_iota(jnp.int32, (D, 128), 0)
    lane = lax.broadcasted_iota(jnp.int32, (D, 128), 1)
    heads = jnp.where(row // HDIM == lane // 2, -1.0, 0.0).astype(BF16)
    less = mm(high, heads) + mm(low, heads)
    lane = lax.broadcasted_iota(jnp.int32, (rows, 128), 1)
    kept = less.astype(BF16).astype(F32)
    pair = jnp.where(lane % 2 == 0, kept, less - kept)
    for head in range(HEADS):
        tile = dout[:, head // 2 * 128 : (head // 2 + 1) * 128]
        if head % 2:
            tile = pltpu.roll(tile, HDIM, 1)
        more = pltpu.roll(pair, HDIM - 2 * head, 1)
        more = jnp.where(lane < HDIM + 2, more, 0.0)
        do_ref[head] = jnp.where(lane < HDIM, tile, more).astype(BF16)
    copies.start(do_ref, do_out)
    go_ref[...] = mm(merged_f.astype(BF16).T, datt).astype(BF16)
    copies.start(go_ref, go_out)
    column = lambda value: jnp.sum(value.astype(F32), axis=0, keepdims=True)
    sums = [dmid * attended, back, back * normed, cot * branch, datt]
    sums = [column(value) for value in sums] + [bias_ref[:5, :], jnp.zeros((6, D), F32)]
    small_ref[...] = jnp.concatenate(sums, axis=0)
    copies.wait()


def attend_back(own, e_ref, q_ref, k_ref, v_ref, do_ref, place_ref, outs, sums):
    dq_ref, dk_ref, dv_ref, tab_ref = outs
    dkt_ref, dvt_ref, part_ref = sums
    rows = q_ref.shape[1]
    spans = blocks_of(0, own, 256) + blocks_of(own, rows - own, 256)
    items = [(side, *span) for side in range(2) for span in spans]
    grads, found = {}, {}
    for n in range(len(items) + 2):
        if n < len(items):
            side, at, size = items[n]
            grads[n] = mm_t(do_ref[side, at : at + size, :], v_ref[side])
        if 0 <= n - 1 < len(items):
            side, at, size = items[n - 1]
            found[n - 1] = (e_ref[side, at : at + size, :].astype(F32) * grads.pop(n - 1)).astype(BF16)
        if 0 <= n - 2:
            side, at, size = items[n - 2]
            lanes = slice(side * HDIM, (side + 1) * HDIM)
            ds = found.pop(n - 2)
            dq = mm(ds, k_ref[side])
            dq_ref[at : at + size, lanes] = (dq[:, :HDIM] * (1.0 / math.sqrt(HDIM))).astype(BF16)
            part_ref[at : at + size, lanes] = dq[:, HDIM:].astype(BF16)
            dkt = mm(q_ref[side, at : at + size, :HDIM].T, ds)
            dvt = mm(do_ref[side, at : at + size, :HDIM].T, e_ref[side, at : at + size, :])
            if at == 0:
                dkt_ref[lanes, :] = dkt
                dvt_ref[lanes, :] = dvt
            else:
                dkt_ref[lanes, :] += dkt
                dvt_ref[lanes, :] += dvt
    tab_ref[...] = mm(place_ref[...], part_ref[...])
    dk_ref[...] = dkt_ref[...].astype(BF16).T
    dv_ref[...] = dvt_ref[...].astype(BF16).T


def back_kernel(own, everyone, scalar_ref, kept_ref, mod_ref, prior_ref, *refs):
    group_sources, refs = refs[:5], refs[5:]
    sources, refs = refs[:7], refs[7:]
    keep_ref, send_ref, dx_ref, dx_own_ref, refs = *refs[:4], refs[4:]
    group_local, refs = refs[:5], refs[5:]
    local, refs = refs[:7], refs[7:]
    dq_ref, dk_ref, dv_ref, tab_ref, normed_ref, inverse_ref, dxs_ref, dkt_ref, dvt_ref, pay_ref = refs[:10]
    place_ref, part_ref, group_sems, sems, pay_sems = refs[10:]
    tok_ref, a_ref, x_ref, slot_ref, weight_ref, dm_ref, go_ref = local
    step = pl.program_id(0)
    last = pl.num_programs(0) - 1
    slot = step % 2

    def fetches(group, place):
        return [
            pltpu.make_async_copy(source.at[pl.ds(2 * group, 2)], target.at[place], group_sems.at[place, n])
            for n, (source, target) in enumerate(zip(group_sources, group_local))
        ]

    def copies():
        return [
            pltpu.make_async_copy(source, target, sems.at[n])
            for n, (source, target) in enumerate(zip(sources, local))
        ]

    @pl.when(step == 0)
    def first():
        whole = copies()
        whole[0].start()
        for copy in fetches(0, 0):
            copy.start()
        for copy in whole[1:]:
            copy.start()
        for copy in fetches(1, 1):
            copy.start()
        slots = x_ref.shape[0] - own
        place_ref[...] = place_onehot(row_places(scalar_ref, kept_ref, own, slots), turned=True).T
        whole[0].wait()
        normed, inverse = norm_parts(tok_ref[...].astype(F32))
        normed_ref[...] = normed
        inverse_ref[...] = jnp.broadcast_to(inverse, inverse_ref.shape)

    @pl.when((step > 0) & (step + 1 < last))
    def following():
        for copy in fetches(step + 1, 1 - slot):
            copy.start()

    @pl.when(step < last)
    def attention():
        for copy in fetches(step, slot):
            copy.wait()
        outs = dq_ref.at[step], dk_ref.at[step], dv_ref.at[step], tab_ref.at[step]
        attend_back(own, *[ref.at[slot] for ref in group_local], place_ref, outs, (dkt_ref, dvt_ref, part_ref))

    @pl.when(step == last)
    def projections():
        for copy in copies()[1:]:
            copy.wait()
        groups = dq_ref.shape[0]
        total = tok_ref.shape[0]
        rows = x_ref.shape[0]
        slots = rows - own
        scale = mod_ref[1:2, :]
        here = row_span(scalar_ref, STARTS, own)

        def joined(ref, span):
            return jnp.concatenate([ref[n, span, :] for n in range(groups)], axis=1)

        every = slice(0, total)
        dk, dv = joined(dk_ref, every), joined(dv_ref, every)
        dq_own, dq_slot = joined(dq_ref, slice(0, own)), joined(dq_ref, slice(own, rows))
        column = lambda value: jnp.sum(value.astype(F32), axis=0, keepdims=True)
        lowered_t = a_ref[...].T
        pay_ref[0:D, :] = (mm(a_ref[here, :].T, dq_own) + mm(slot_ref[...].T, dq_slot)).astype(BF16)
        pay_ref[D : 2 * D, :] = mm(lowered_t, dk).astype(BF16)
        pay_ref[2 * D : 3 * D, :] = mm(lowered_t, dv).astype(BF16)
        pay_ref[3 * D : 4 * D, :] = go_ref[...]
        slot_normed, slot_inverse = norm_parts(x_ref[own:, :].astype(F32))
        da = mm_t(dq_slot, weight_ref[:, :D])
        shift_sum, scale_sum = column(da), column(da * slot_normed)
        spread = dm_ref[own:, :] + norm_back(slot_normed, slot_inverse, da * (1.0 + scale))
        chosen = slot_places(scalar_ref, kept_ref, slots) == lax.broadcasted_iota(jnp.int32, (slots, total), 1)
        chosen = chosen.astype(F32)
        moved = mm(chosen.astype(BF16).T, spread.astype(BF16))
        dxs_ref[...] = mm_t(dk, weight_ref[:, D : 2 * D]) + mm_t(dv, weight_ref[:, 2 * D :])
        dxs_ref[here, :] += mm_t(dq_own, weight_ref[:, :D])
        da = dxs_ref[...]
        normed = normed_ref[...]
        shift_sum, scale_sum = shift_sum + column(da), scale_sum + column(da * normed)
        inverse = jnp.concatenate([inverse_ref[...]] * (D // 128), axis=1)
        dxs_ref[...] = moved + norm_back(normed, inverse, da * (1.0 + scale))
        dx_own_ref[...] = dxs_ref[here, :] + dm_ref[:own, :]
        others = dx_ref.shape[0]
        for n in range(others):
            dx_ref[n] = dxs_ref[row_span(scalar_ref, STARTS + 1 + others + n, own), :].astype(BF16)
        rel = table_sums([tab_ref[n] for n in range(groups)])
        first = jnp.where(scalar_ref[SEQ_PLACE] == 0, 1, 0)
        label = scalar_ref[LABEL]
        number = lax.broadcasted_iota(jnp.int32, (1, D), 1)
        digits = jnp.where(number == scalar_ref[PLACE], label // GRID * first, 0)
        digits = jnp.where(number == 128 + scalar_ref[PLACE], label % GRID * first, digits).astype(F32)
        smalls = jnp.concatenate(
            [
                shift_sum, scale_sum, prior_ref[0:4, :], column(dq_own) + column(dq_slot), column(dv),
                *rel, prior_ref[4:5, :], digits, prior_ref[5:10, :], mod_ref[COND_LINE : COND_LINE + 1, :],
                jnp.zeros((14, D), F32),
            ],
            axis=0,
        ).astype(BF16)
        tail = pay_ref.shape[0] - 4 * D
        row = lax.broadcasted_iota(jnp.int32, (tail, 32), 0)
        lane = lax.broadcasted_iota(jnp.int32, (tail, 32), 1)
        kind = jnp.where(row < 6 * everyone, row // everyone, jnp.where(scalar_ref[SEQ_PLACE] == 0, 17, -1))
        wanted = jnp.where(row % everyone == scalar_ref[PLACE], kind, -1)
        after = row - 7 * everyone
        wanted = jnp.where(after < 0, wanted, jnp.where(after < 11, after + 6, -1))
        pay_ref[4 * D :, :] = mm((lane == wanted).astype(F32).astype(BF16), smalls).astype(BF16)
        halves = Copies(pay_sems)
        split_halves(halves, scalar_ref[SIDE], pay_ref, keep_ref, send_ref)
        halves.wait()


def table_sums(tabs):
    found = ([], [])
    for tab in tabs:
        for side in range(2):
            for part in range(2):
                at = 2 * side * GRID + part * GRID
                square = tab[part * GRID : (part + 1) * GRID, at : at + GRID]
                wide = jnp.concatenate([square, jnp.zeros((GRID, 128 - GRID), F32)], axis=1)
                turned = pltpu.roll(wide, 0, 1, stride=1, stride_axis=0)
                found[part].append(jnp.sum(turned, axis=0, keepdims=True)[:, : 2 * GRID])
    return [jnp.concatenate(parts, axis=1) for parts in found]


def call(kernel, outs, scratch, args, scalars=0, far=0, away=0, copies=0, micros=1, limit=32):
    scratches = [pltpu.VMEM(shape, dtype) for shape, dtype in scratch]
    if copies:
        scratches.append(pltpu.SemaphoreType.DMA((copies,)))
    return pl.pallas_call(
        kernel,
        out_shape=[jax.ShapeDtypeStruct(shape, dtype) for shape, dtype in outs[: len(outs) - away]]
        + [pltpu.HBM(shape, dtype) for shape, dtype in outs[len(outs) - away :]],
        in_specs=[smem] * scalars + [vmem] * (len(args) - scalars - far) + [hbm] * far,
        out_specs=[vmem] * (len(outs) - away) + [hbm] * away,
        scratch_shapes=scratches,
        compiler_params=pltpu.CompilerParams(vmem_limit_bytes=limit * MIB),
        cost_estimate=pl.CostEstimate(flops=micros * 10**9, bytes_accessed=MIB, transcendentals=0),
    )(*args)


def own_call(outs, scalars, sources):
    return pl.pallas_call(
        own_kernel,
        out_shape=[jax.ShapeDtypeStruct(shape, dtype) for shape, dtype in outs],
        in_specs=[smem] * len(scalars) + [hbm] * len(sources),
        out_specs=[smem] + [vmem] * (len(outs) - 1),
        scratch_shapes=[pltpu.VMEM(value.shape, value.dtype) for value in sources]
        + [pltpu.SemaphoreType.DMA((len(sources),))],
        compiler_params=pltpu.CompilerParams(vmem_limit_bytes=16 * MIB),
        cost_estimate=pl.CostEstimate(flops=3 * 10**9, bytes_accessed=MIB, transcendentals=0),
    )(*scalars, *map(in_hbm, sources))


def in_hbm(value):
    return pltpu.with_memory_space_constraint(value, pltpu.HBM)


def add_kernel(pieces, left_ref, right_ref, sum_out, sum_ref, sems):
    copies = Copies(sems)
    rows = sum_ref.shape[0] // pieces
    for n in range(pieces):
        span = pl.ds(n * rows, rows)
        sum_ref[span, :] = (left_ref[span, :].astype(F32) + right_ref[span, :].astype(F32)).astype(BF16)
        copies.start(sum_ref.at[span], sum_out.at[span])
    copies.wait()


def add_call(left, right, micros):
    pieces = 4 if left.shape[0] % 64 == 0 else 1
    out = (left.shape, BF16)
    return call(
        functools.partial(add_kernel, pieces), [out], [out], [left, right], away=1, copies=pieces, micros=micros,
        limit=8,
    )[0]


def spread_kernel(near_ref, far_ref, wide_out, sum_ref, sems):
    sum_ref[...] = (near_ref[...].astype(F32) + far_ref[...].astype(F32)).astype(BF16)
    copies = Copies(sems)
    for n in range(wide_out.shape[0]):
        copies.start(sum_ref, wide_out.at[n])
    copies.wait()


def spread_call(near, far, peers):
    return call(
        spread_kernel, [((peers,) + near.shape, BF16)], [(near.shape, BF16)], [near, far], away=1, copies=peers,
        limit=8,
    )[0]


def back_call(own, everyone, groups_of, sources, scalars, kept, mod, prior, tail_half):
    rows, total = groups_of[1].shape[1], groups_of[2].shape[1]
    groups = HEADS // 2
    others = total // own - 1
    whole = lambda shape: pl.BlockSpec(shape, lambda n: (0,) * len(shape))
    outs = [((tail_half, D), BF16), ((tail_half, D), BF16), ((others, own, D), BF16), ((own, D), F32)]
    scratch = [((2, 2) + value.shape[1:], value.dtype) for value in groups_of]
    scratch += [(value.shape, value.dtype) for value in sources]
    scratch += [
        ((groups, rows, 128), BF16), ((groups, total, 128), BF16), ((groups, total, 128), BF16),
        ((groups, 2 * GRID, 128), F32), ((total, D), F32), ((total, 128), F32), ((total, D), F32),
        ((128, total), F32), ((128, total), F32), ((2 * tail_half, D), BF16),
        ((2 * GRID, rows), BF16), ((rows, 128), BF16),
    ]
    small = [kept, mod, prior]
    return pl.pallas_call(
        functools.partial(back_kernel, own, everyone),
        grid=(groups + 1,),
        out_shape=[jax.ShapeDtypeStruct(shape, dtype) for shape, dtype in outs[:2]]
        + [pltpu.HBM(shape, dtype) for shape, dtype in outs[2:]],
        in_specs=[smem] + [whole(value.shape) for value in small] + [hbm] * (len(groups_of) + len(sources)),
        out_specs=[vmem, vmem] + [whole(shape) for shape, unused in outs[2:]],
        scratch_shapes=[pltpu.VMEM(shape, dtype) for shape, dtype in scratch]
        + [pltpu.SemaphoreType.DMA((2, 5)), pltpu.SemaphoreType.DMA((7,)), pltpu.SemaphoreType.DMA((2,))],
        compiler_params=pltpu.CompilerParams(
            vmem_limit_bytes=48 * MIB, dimension_semantics=("arbitrary",)
        ),
        cost_estimate=pl.CostEstimate(flops=18 * 10**9, bytes_accessed=MIB, transcendentals=0),
    )(scalars, *small, *map(in_hbm, groups_of), *map(in_hbm, sources))


def halves_reader(side_ref, mine_ref, other_ref):
    half = mine_ref.shape[0]

    def get(at, count):
        found = []
        for which in range(2):
            first, last = max(at, which * half), min(at + count, (which + 1) * half)
            if first < last:
                span = slice(first - which * half, last - which * half)
                found.append(jnp.where(side_ref[0] == which, mine_ref[span, :], other_ref[span, :]))
        return found[0] if len(found) == 1 else jnp.concatenate(found, axis=0)

    return get


def widen_half(core, half_ref, g1_out, g2_out, wide_ref, sems):
    for which in range(2):

        @pl.when(core == which)
        def widen():
            copies = Copies(sems)
            for n in range(4):
                rows = pl.ds(n * D, D)
                wide_ref[rows, :] = half_ref[rows, :].astype(F32)
                copies.start(wide_ref.at[rows], g2_out.at[rows] if which else g1_out.at[:, rows])
            copies.wait()


def near_half_kernel(side_ref, half_ref, g1_out, g2_out, wide_ref, sems):
    widen_half(side_ref[0], half_ref, g1_out, g2_out, wide_ref, sems)


def far_half_kernel(side_ref, half_ref, g1_in, g2_in, g1_out, g2_out, wide_ref, sems):
    widen_half(1 - side_ref[0], half_ref, g1_out, g2_out, wide_ref, sems)


def widen_near(sides, layer_half):
    return pl.pallas_call(
        near_half_kernel,
        out_shape=[pltpu.HBM((D, FF), F32), pltpu.HBM((FF, D), F32)],
        in_specs=[smem, vmem],
        out_specs=[hbm, hbm],
        scratch_shapes=[pltpu.VMEM((FF, D), F32), pltpu.SemaphoreType.DMA((4,))],
        compiler_params=pltpu.CompilerParams(vmem_limit_bytes=8 * MIB),
        cost_estimate=pl.CostEstimate(flops=10**9, bytes_accessed=MIB, transcendentals=0),
    )(sides, layer_half)


def widen_far(sides, other, first):
    return pl.pallas_call(
        far_half_kernel,
        out_shape=[pltpu.HBM((D, FF), F32), pltpu.HBM((FF, D), F32)],
        in_specs=[smem, vmem, hbm, hbm],
        out_specs=[hbm, hbm],
        input_output_aliases={2: 0, 3: 1},
        scratch_shapes=[pltpu.VMEM((FF, D), F32), pltpu.SemaphoreType.DMA((4,))],
        compiler_params=pltpu.CompilerParams(vmem_limit_bytes=8 * MIB),
        cost_estimate=pl.CostEstimate(flops=10**9, bytes_accessed=MIB, transcendentals=0),
    )(sides, other, *map(in_hbm, first))


def last_kernel(
    everyone, side_ref, mine_ref, other_ref, ada_in, qv_ref, rel_ref, out_bias_ref, ada_bias_ref, bias1_ref,
    bias2_ref, gqkv_out, gada_out, table_out, go_out, gqkv_ref, gada_ref, table_ref, go_ref, ada_ref, sems,
):
    get = halves_reader(side_ref, mine_ref, other_ref)
    copies = Copies(sems)
    copies.start(ada_in, ada_ref)
    for n in range(3):
        cols = pl.ds(n * D, D)
        gqkv_ref[:, cols] = get(n * D, D).astype(F32)
        copies.start(gqkv_ref.at[:, cols], gqkv_out.at[:, cols])
    go_ref[...] = get(3 * D, D).astype(F32)
    copies.start(go_ref, go_out)
    cond = get(4 * D + 6 * everyone, everyone).astype(F32)
    gate = 1.0 / (1.0 + jnp.exp(-cond))
    act_t = (cond * gate).astype(BF16).T
    dmods = [get(4 * D + n * everyone, everyone) for n in range(6)]
    small = get(4 * D + 7 * everyone, 16).astype(F32)

    def ada():
        for n in range(6):
            cols = pl.ds(n * D, D)
            gada_ref[:, cols] = mm(act_t, dmods[n])
            copies.start(gada_ref.at[:, cols], gada_out.at[:, cols])
            ada_bias_ref[cols] = jnp.sum(dmods[n].astype(F32), axis=0)

    def table():
        copies.made.pop(0).wait()
        back = jnp.zeros((everyone, D), F32)
        for n in range(6):
            back = back + mm_t(dmods[n], ada_ref[:, n * D : (n + 1) * D])
        back = gate * (1.0 + cond * (1.0 - gate)) * back
        high = back.astype(BF16)
        low = (back - high.astype(F32)).astype(BF16)
        label = (small[5:6, :everyone] * GRID + small[5:6, 128 : 128 + everyone]).astype(jnp.int32)
        classes = table_ref.shape[0]
        wide = round_up(classes, 128)
        hot = (label == lax.broadcasted_iota(jnp.int32, (wide, everyone), 0)).astype(F32).astype(BF16)
        table_ref[...] = (mm(hot, high) + mm(hot, low))[:classes]
        copies.start(table_ref, table_out)

    ada()
    table()
    qv_ref[...] = small[:2]
    for part in range(2):
        for head in range(HEADS):
            at = 2 * GRID * head
            rel_ref[head, part : part + 1, :] = small[2 + part : 3 + part, at : at + 2 * GRID - 1]
    out_bias_ref[...] = small[4]
    for n in range(4):
        bias1_ref[pl.ds(n * D, D)] = small[6 + n]
    bias2_ref[...] = small[10]
    copies.wait()


def swap_cores(value, dp):
    return lax.ppermute(value, "dp", [(n, n ^ 1) for n in range(dp)])


def exchange(value, dp, seq):
    groups = [
        [(far * (dp // 2) + 2 * pair + core) * seq + at for pair in range(dp // 4) for at in range(seq)]
        for far in range(2)
        for core in range(2)
    ]
    return lax.all_to_all(value, AXES, 0, 0, axis_index_groups=groups)


def near_sum(pieces):
    return jnp.sum(pieces.astype(F32), axis=0).astype(BF16)


def far_half(near, dp):
    return lax.ppermute(near, "dp", [(n, (n + dp // 2) % dp) for n in range(dp)])


def assemble_kernel(cut, place_ref, pair_ref, a1_ref, b1_ref, a2_ref, b2_ref, half_ref):
    rows = pair_ref.shape[1]
    for near in range(2):
        for x in range(2):
            for y in range(2):
                at = (place_ref[0] ^ (4 * near + 2 * x + y)) * rows
                if x:
                    half_ref[pl.ds(pl.multiple_of(at, 16), cut), :] = a2_ref[y, near]
                elif y:
                    half_ref[pl.ds(pl.multiple_of(at, 16), cut), :] = a1_ref[near]
                else:
                    half_ref[pl.ds(pl.multiple_of(at, 16), cut), :] = pair_ref[near, :cut, :]
                rest = pl.ds(pl.multiple_of(at + cut, 16), rows - cut)
                if y:
                    half_ref[rest, :] = b2_ref[x, near]
                elif x:
                    half_ref[rest, :] = b1_ref[near]
                else:
                    half_ref[rest, :] = pair_ref[near, cut:, :]


def after(value, *others):
    return lax.optimization_barrier((value, *others))[0]


def gather_chunks(chunk, last_near, before, finish, dp, seq):
    rows = chunk.shape[0]
    cut = round_up(rows // 2, 16)
    place = lax.axis_index("dp") % (dp // 2) // 2 * seq + lax.axis_index("seq")
    along_x = lambda value: lax.ppermute(value, "dp", [(n, n ^ 2) for n in range(dp)])
    along_y = lambda value: lax.ppermute(value, "seq", [(n, n ^ 1) for n in range(seq)])
    chunk = after(chunk, last_near, before)
    last_wide = finish(last_near)
    pair = jnp.stack([chunk, lax.ppermute(chunk, "dp", [(n, n ^ 4) for n in range(dp)])])
    a, b = pair[:, :cut], pair[:, cut:]
    a1, b1 = along_y(a), along_x(b)
    a, b = jnp.stack([a, a1]), jnp.stack([b, b1])
    a, b = after((a, b), last_wide)
    a2, b2 = along_x(a), along_y(b)
    held = (a2, b2)

    def assemble(a2, b2):
        return call(
            functools.partial(assemble_kernel, cut), [((8 * rows, D), BF16)], [],
            [place.astype(jnp.int32).reshape(1), pair, a1, b1, a2, b2], scalars=1, limit=8,
        )[0]

    return (a2, b2), assemble, last_wide, held


def scatter_rows(partial, seq):
    return [
        lax.ppermute(partial[step - 1], "seq", [(n, (n + step) % seq) for n in range(seq)])
        for step in range(1, seq)
    ]


def body(
    dp, seq, image_tokens, kept_index, kept_count, sample_valid, timestep, class_label, class_table,
    ada_weight, ada_bias, qkv_weight, qv_bias, rel_bias, out_weight, out_bias, fc1_weight,
    fc1_bias, fc2_weight, fc2_bias, grad_full, grad_masked,
):
    samples, own, width = image_tokens.shape
    held = kept_index.shape[1]
    slots = grad_masked.shape[1]
    padded = round_up(slots, 16)
    rows = own + padded
    total = own * seq
    everyone = dp * samples
    classes = class_table.shape[0]
    dp_place, seq_place = lax.axis_index("dp"), lax.axis_index("seq")

    half = round_up(FF, dp * seq * 4)
    peers = dp // 4 * seq
    side = dp_place % 2
    sides = side.astype(jnp.int32).reshape(1)
    tail_half = round_up(4 * D + 16 + 7 * everyone, dp * seq * 4) // 2
    kept_of = []
    for s in range(samples):
        tokens = [image_tokens[s]]
        for step in range(1, seq):
            tokens.append(lax.ppermute(tokens[0], "seq", [(n, (n + step) % seq) for n in range(seq)]))
        number = jnp.arange(STARTS + 2 * seq - 1, dtype=jnp.int32)
        block = number - STARTS
        scalars = jnp.where(block < seq, seq_place - block, seq_place + block - seq + 1) % seq * own
        entries = {
            SIDE: side, PLACE: dp_place * samples + s, SLOT_START: seq_place * slots, SEQ_PLACE: seq_place,
        }
        for at, entry in entries.items():
            scalars = jnp.where(number == at, entry, scalars)
        places = scalars.astype(jnp.int32)
        held_rows = held + padded - slots
        cot_slot = jnp.pad(grad_masked[s], ((0, padded - slots), (0, 0)))
        one = slice(s, s + 1)
        scalars, kept, lines, mod, *owned, mask = own_call(
            [
                (places.shape, jnp.int32), ((held_rows, 1), jnp.int32), ((16, D), F32),
                ((8, D), F32), ((own, D), BF16), ((own, D), BF16), ((HEADS, own, 128), BF16),
                ((HEADS, own, 128), BF16), ((HEADS, own, 128), BF16), ((padded, D), BF16), ((8, total), F32),
            ],
            [places, kept_count[one], sample_valid[one], timestep[one], class_label[one]],
            [
                kept_index[one], rel_bias.transpose(1, 0, 2), ada_bias, qv_bias, out_bias, fc1_bias, fc2_bias,
                class_table, ada_weight, tokens[0], qkv_weight,
            ],
        )
        qaug, kaug, vaug, x, lowered, whole, slot = call(
            functools.partial(prep_kernel, seq),
            [
                ((HEADS, rows, 128), BF16), ((HEADS, total, 128), BF16), ((HEADS, total, 128), BF16),
                ((rows, D), BF16), ((total, D), BF16), ((total, D), BF16), ((padded, D), BF16),
            ],
            [((total, D), BF16), ((total, D), BF16), ((total, D), BF16), ((padded, D), BF16)],
            [scalars, *tokens, *owned, kept, mod, qkv_weight, lines],
            scalars=1, away=3, copies=3, micros=3, limit=16,
        )
        mixed, inverse, spread_far, qaug_far, kaug_far, vaug_far = call(
            functools.partial(attend_kernel, own),
            [
                ((HEADS // 2, rows, 128), F32), ((HEADS // 2, rows, 128), F32),
                ((HEADS, rows, total), BF16), (qaug.shape, BF16), (kaug.shape, BF16), (vaug.shape, BF16),
            ],
            [((HEADS, rows, total), BF16)],
            [qaug, kaug, vaug, mask],
            away=4, copies=3 + 8 * HEADS, micros=10, limit=32,
        )
        attended, hidden, du, biases, keep, send = call(
            functools.partial(feed_kernel, slots),
            [
                ((rows, D), F32), ((rows, FF), BF16), ((rows, FF), BF16), ((8, D), F32), ((half, D), BF16),
                ((half, D), BF16),
            ],
            [((2, half, D), BF16)],
            [
                scalars, mixed, x, grad_full[s], cot_slot, mod, out_weight, fc1_weight, fc2_weight, lines,
            ],
            scalars=1, copies=2, micros=10, limit=24,
        )
        kept_of.append(dict(
            rest=[
                scalars, mixed, inverse, x, grad_full[s], cot_slot, mod, out_weight, fc1_weight, fc2_weight,
                lines, attended, hidden, du, biases,
            ],
            groups=[spread_far, qaug_far, kaug_far, vaug_far], sources=[whole, lowered, slot, qkv_weight],
            small=[scalars, kept, mod], keep=keep, send=send,
        ))

    def added(arrays):
        if len(arrays) == 1:
            return arrays[0]
        return functools.reduce(jnp.add, [a.astype(F32) for a in arrays]).astype(arrays[0].dtype)

    keep, send = added([k["keep"] for k in kept_of]), added([k["send"] for k in kept_of])
    got = swap_cores(send, dp)

    rests = [
        call(
            functools.partial(feed_rest_kernel, slots),
            [
                ((16, D), F32), ((own, D), BF16), ((padded, D), BF16), ((rows, D), F32), ((rows, D), BF16),
                ((HEADS, rows, 128), BF16), ((D, D), BF16),
            ],
            [((rows, D), BF16), ((rows, D), F32), ((HEADS, rows, 128), BF16), ((D, D), BF16)],
            k["rest"],
            scalars=1, away=6, copies=6, micros=6, limit=24,
        )
        for k in kept_of
    ]
    mine = add_call(keep, got, 1)
    mine, rests = lax.optimization_barrier((mine, rests))
    pieces = exchange(mine.reshape(peers, half // peers, D), dp, seq)
    tails = []
    for k, rest in zip(kept_of, rests):
        small, unused_full, unused_slot, dmid, x_far, dout_far, grad_out = rest
        whole, lowered, slot, weights = k["sources"]
        tails.append(
            back_call(
                own, everyone, [*k["groups"], dout_far], [whole, lowered, x_far, slot, weights, dmid, grad_out],
                *k["small"], small, tail_half,
            )
        )

    keep, send = added([t[0] for t in tails]), added([t[1] for t in tails])
    keep, send, pieces = lax.optimization_barrier((keep, send, pieces))
    got = swap_cores(send, dp)
    mine = add_call(keep, got, 1).reshape(peers, tail_half // peers, D)
    pieces, mine = lax.optimization_barrier((pieces, mine))
    near = near_sum(pieces)
    far = far_half(near, dp)
    first_moved = [scatter_rows(t[2][:, : own // 2], seq) for t in tails]
    last_moved = [scatter_rows(t[2][:, own // 2 :], seq) for t in tails]
    last_near = near_sum(exchange(mine, dp, seq))

    def finish(last_near):
        wide = spread_call(last_near, far_half(last_near, dp), peers)
        return wide

    if dp == 16 and seq == 2:
        chunk = (near.astype(F32) + far.astype(F32)).astype(BF16)
        parts, assemble, last_wide, held = gather_chunks(chunk, last_near, first_moved, finish, dp, seq)
    else:
        parts = exchange(spread_call(near, far, peers), dp, seq).reshape(half, D)
        assemble = lambda whole: whole
        parts = (parts,)
        held = parts
        last_wide = finish(last_near)
    last_half = exchange(last_wide, dp, seq).reshape(tail_half, D)
    out_full = jnp.stack([rest[1] for rest in rests])
    out_masked = jnp.stack([rest[2][:slots] for rest in rests])
    layer_half = assemble(*parts)
    other = swap_cores(layer_half, dp)
    first = widen_near(sides, layer_half)
    last_half = after(last_half, layer_half)
    grad_fc1, grad_fc2 = widen_far(sides, other, first)
    found = call(
        functools.partial(last_kernel, everyone),
        [
            ((2, D), F32), ((HEADS, 2, 2 * GRID - 1), F32), ((D,), F32), ((6 * D,), F32), ((FF,), F32), ((D,), F32),
            ((D, 3 * D), F32), ((D, 6 * D), F32), ((classes, D), F32), ((D, D), F32),
        ],
        [((D, 3 * D), F32), ((D, 6 * D), F32), ((classes, D), F32), ((D, D), F32), (ada_weight.shape, BF16)],
        [sides, last_half, swap_cores(last_half, dp), in_hbm(ada_weight)],
        scalars=1, far=1, away=4, copies=12, micros=4, limit=16,
    )
    grad_qv, grad_rel, grad_out_bias, grad_ada_bias, grad_fc1_bias, grad_fc2_bias = found[:6]
    grad_qkv, grad_ada, grad_table, grad_out = found[6:]
    grad_rel = grad_rel.transpose(1, 0, 2)
    grad_qkv, last_moved = lax.optimization_barrier((grad_qkv, last_moved))
    grad_input = []
    for tail, *moved in zip(tails, first_moved, last_moved):
        came = [jnp.concatenate(both).astype(F32) for both in zip(*moved)]
        grad_input.append(functools.reduce(jnp.add, came, tail[3]))
    grad_input = jnp.stack(grad_input)
    return (
        out_full, out_masked, grad_input, grad_table, grad_ada, grad_ada_bias, grad_qkv, grad_qv,
        grad_rel, grad_out, grad_out_bias, grad_fc1, grad_fc1_bias, grad_fc2, grad_fc2_bias,
    )


def solution(mesh):
    split = P("dp", "seq", None)
    placed = (split, P("dp", None)) + (P("dp"),) * 4 + (P(),) * 12 + (split, split)
    return jax.shard_map(
        functools.partial(body, mesh.shape["dp"], mesh.shape["seq"]),
        mesh=mesh,
        in_specs=placed,
        out_specs=(split,) * 3 + (P(),) * 12,
        check_vma=False,
    )
```

```python
import functools
import math

import jax
import jax.numpy as jnp
from jax import lax
from jax.experimental import pallas as pl
from jax.experimental.pallas import tpu as pltpu
from jax.sharding import PartitionSpec as P

D = 384
HEADS = 6
HDIM = 64
GRID = 32
FF = 1536
CHUNK = 256

AXES = ("dp", "seq")
F32 = jnp.float32
BF16 = jnp.bfloat16
MIB = 1024 * 1024
GELU_A = math.sqrt(2.0 / math.pi)
GELU_B = 0.044715

highest = lax.Precision.HIGHEST
big_negative = -1e30
vmem = pl.BlockSpec(memory_space=pltpu.VMEM)
smem = pl.BlockSpec(memory_space=pltpu.SMEM)
hbm = pl.BlockSpec(memory_space=pltpu.HBM)


def round_up(value, step):
    return -(-value // step) * step


def blocks_of(first, count, most):
    pieces = -(-count // most)
    size = round_up(-(-count // pieces), 16)
    found = []
    at = 0
    while at < count:
        found.append((first + at, min(size, count - at)))
        at += size
    return found


def mm(left, right):
    return lax.dot_general(left, right, (((1,), (0,)), ((), ())), preferred_element_type=F32)


def mm_t(left, right):
    return lax.dot_general(left, right, (((1,), (1,)), ((), ())), preferred_element_type=F32)


def norm_parts(value):
    average = jnp.mean(value, axis=-1, keepdims=True)
    centred = value - average
    variance = jnp.mean(centred * centred, axis=-1, keepdims=True)
    inverse = lax.rsqrt(variance + 1e-06)
    return (centred * inverse, inverse)


def norm_back(normed, inverse, grad):
    first = jnp.mean(grad, axis=-1, keepdims=True)
    second = jnp.mean(grad * normed, axis=-1, keepdims=True)
    return inverse * (grad - first - normed * second)


def place_onehot(position, turned=False):
    lane = lax.broadcasted_iota(jnp.int32, (position.shape[0], 2 * GRID), 1)
    if turned:
        lane = jnp.where(lane < GRID, GRID - 1 - lane, 3 * GRID - 1 - lane)
    wanted = jnp.where(lane < GRID, position // GRID, position % GRID + GRID)
    return (lane == wanted).astype(F32).astype(BF16)


class Copies:
    def __init__(self, sems):
        self.sems, self.made, self.count = sems, [], 0

    def start(self, source, target):
        copy = pltpu.make_async_copy(source, target, self.sems.at[self.count])
        copy.start()
        self.made.append(copy)
        self.count += 1

    def wait(self):
        for copy in self.made:
            copy.wait()


def half_copies(side, payload_ref, keep_ref, send_ref, sems, which):
    for target, chosen in ((keep_ref, side == which), (send_ref, side != which)):

        @pl.when(chosen)
        def start():
            pltpu.make_async_copy(payload_ref.at[which], target, sems.at[which]).start()


def split_halves(copies, side, payload_ref, keep_ref, send_ref):
    half = keep_ref.shape[0]
    for which, target in ((side, keep_ref), (1 - side, send_ref)):
        copies.start(payload_ref.at[pl.ds(pl.multiple_of(which * half, 16), half)], target)


SIDE, PLACE, SLOT_START, COUNT, VALID, LABEL, SEQ_PLACE, STARTS = range(8)


def row_span(scalar_ref, number, count):
    return pl.ds(pl.multiple_of(scalar_ref[number], 16), count)


def slot_places(scalar_ref, kept_ref, slots):
    return kept_ref[pl.ds(pl.multiple_of(scalar_ref[SLOT_START], 8), slots), :]


def row_places(scalar_ref, kept_ref, own, slots):
    mine = lax.broadcasted_iota(jnp.int32, (own, 1), 0) + scalar_ref[STARTS]
    return jnp.concatenate([mine, slot_places(scalar_ref, kept_ref, slots)], axis=0)


def row_weights(scalar_ref, own, slots, rows):
    row = lax.broadcasted_iota(jnp.int32, (rows, 1), 0)
    kept = (row < own + slots) & (row - own + scalar_ref[SLOT_START] < scalar_ref[COUNT])
    return jnp.where((row < own) | kept, scalar_ref[VALID], 0).astype(F32)


def project(tokens, mod_ref, weight_ref, line_ref):
    normed, unused = norm_parts(tokens.astype(F32))
    lowered = (normed * (1.0 + mod_ref[1:2, :]) + mod_ref[0:1, :]).astype(BF16)
    query = (mm(lowered, weight_ref[:, :D]) + line_ref[QV_LINE : QV_LINE + 1, :]).astype(BF16)
    scaled = (query.astype(F32) * (1.0 / math.sqrt(HDIM))).astype(BF16)
    keys = mm(lowered, weight_ref[:, D : 2 * D]).astype(BF16)
    values = (mm(lowered, weight_ref[:, 2 * D :]) + line_ref[QV_LINE + 1 : QV_LINE + 2, :]).astype(BF16)
    return lowered, scaled, keys, values


def head_cols(head):
    return slice(head * HDIM, (head + 1) * HDIM)


def ones_lanes(count):
    return (lax.broadcasted_iota(jnp.int32, (count, HDIM), 1) < 2).astype(F32).astype(BF16)


def bias_table(rel_ref):
    lane = lax.broadcasted_iota(jnp.int32, (GRID, 128), 1)
    parts = []
    for part in range(2):
        tiles = []
        for group in range(HEADS // 2):
            tile = jnp.zeros((GRID, 128), F32)
            for side in range(2):
                head = 2 * group + side
                line = rel_ref[head, part : part + 1, :].astype(F32)
                line = jnp.concatenate([line, jnp.zeros((1, 128 - line.shape[1]), F32)], axis=1)
                first = side * HDIM + part * GRID
                turned = pltpu.roll(
                    jnp.broadcast_to(line, (GRID, 128)), (first + 128 - (GRID - 1)) % 128, 1,
                    stride=1, stride_axis=0,
                )
                tile = jnp.where((lane >= first) & (lane < first + GRID), turned, tile)
            tiles.append(tile)
        parts.append(jnp.concatenate(tiles, axis=1))
    return jnp.concatenate(parts, axis=0).astype(BF16)


QV_LINE, OUT_LINE, FC1_LINE, FC2_LINE = 6, 8, 9, 13
COND_LINE = 6


def time_features(moment):
    half = D // 2
    lane = lax.broadcasted_iota(jnp.int32, (1, D), 1)
    number = jnp.where(lane < half, lane, lane - half).astype(F32)
    angle = moment.astype(F32) * jnp.exp(-math.log(10000.0) * number / half)
    return jnp.where(lane < half, jnp.cos(angle), jnp.sin(angle))


def own_kernel(
    start_ref, count_ref, valid_ref, moment_ref, label_ref,
    *refs,
):
    sources, outs, local, sems = refs[:11], refs[11:22], refs[22:33], refs[33]
    scalar_ref, kept_ref, line_ref, mod_ref, a_ref, qs_ref, qaug_ref, kaug_ref, vaug_ref = outs[:9]
    offset_ref, mask_ref = outs[9:]
    kept_in, rel_ref, ada_bias_ref, qv_bias_ref, out_bias_ref, fc1_bias_ref, fc2_bias_ref = local[:7]
    table_ref, ada_ref, tok_ref, weight_ref = local[7:]
    fetched = [pltpu.make_async_copy(*pair, sems.at[n]) for n, pair in enumerate(zip(sources, local))]
    for copy in fetched:
        copy.start()
    for copy in fetched[:7]:
        copy.wait()
    own = tok_ref.shape[0]
    slots = offset_ref.shape[0]
    total = mask_ref.shape[1]
    held = kept_ref.shape[0]
    label = label_ref[0]
    for n in range(scalar_ref.shape[0]):
        scalar_ref[n] = start_ref[n]
    scalar_ref[COUNT] = count_ref[0]
    scalar_ref[VALID] = valid_ref[0]
    scalar_ref[LABEL] = label
    width = round_up(held, 128)
    kept = jnp.concatenate([kept_in[...], jnp.zeros((1, width - kept_in.shape[1]), jnp.int32)], axis=1)
    kept_ref[...] = jnp.broadcast_to(kept, (8, width)).T[:held, :1]
    place = place_onehot(row_places(start_ref, kept_ref, own, slots))
    offsets = mm(place, bias_table(rel_ref)).astype(BF16)
    offset_ref[...] = offsets[own:]
    number = lax.broadcasted_iota(jnp.int32, (held, 1), 0)
    live = jnp.where(number < count_ref[0], kept_ref[...], -1)
    hit = live == lax.broadcasted_iota(jnp.int32, (held, total), 1)
    count = jnp.sum(hit.astype(F32), axis=0, keepdims=True)
    mask_ref[...] = jnp.broadcast_to(jnp.where(count > 0.0, 0.0, big_negative), mask_ref.shape)
    for n in range(6):
        line_ref[n : n + 1, :] = ada_bias_ref[pl.ds(n * D, D)].astype(F32).reshape(1, D)
    line_ref[QV_LINE : QV_LINE + 2, :] = qv_bias_ref[...].astype(F32)
    line_ref[OUT_LINE : OUT_LINE + 1, :] = out_bias_ref[...].astype(F32).reshape(1, D)
    for n in range(4):
        line_ref[FC1_LINE + n : FC1_LINE + n + 1, :] = fc1_bias_ref[pl.ds(n * D, D)].astype(F32).reshape(1, D)
    line_ref[FC2_LINE : FC2_LINE + 1, :] = fc2_bias_ref[...].astype(F32).reshape(1, D)
    line_ref[FC2_LINE + 1 :, :] = jnp.zeros((2, D), F32)
    for copy in fetched[7:]:
        copy.wait()
    hot = lax.broadcasted_iota(jnp.int32, (16, table_ref.shape[0]), 1) == label
    conditioned = mm(hot.astype(F32).astype(BF16), table_ref[...]) + time_features(moment_ref[0])
    gate = 1.0 / (1.0 + jnp.exp(-conditioned))
    activated = (conditioned * gate).astype(BF16)
    for n in range(6):
        mod_ref[n : n + 1, :] = mm(activated, ada_ref[:, n * D : (n + 1) * D])[:1] + line_ref[n : n + 1, :]
    mod_ref[COND_LINE : COND_LINE + 1, :] = conditioned[:1]
    mod_ref[COND_LINE + 1 :, :] = jnp.zeros((1, D), F32)
    lowered, scaled, keys, values = project(tok_ref[...], mod_ref, weight_ref, line_ref)
    a_ref[...] = lowered
    qs_ref[...] = scaled
    for head in range(HEADS):
        cols = head_cols(head)
        qaug_ref[head] = jnp.concatenate([scaled[:, cols], offsets[:own, cols]], axis=1)
        kaug_ref[head] = jnp.concatenate([keys[:, cols], place[:own]], axis=1)
        vaug_ref[head] = jnp.concatenate([values[:, cols], ones_lanes(own)], axis=1)


def prep_kernel(seq, scalar_ref, *refs):
    token_refs, refs = refs[:seq], refs[seq:]
    own_a_ref, own_qs_ref, own_qaug_ref, own_kaug_ref, own_vaug_ref, offset_ref = refs[:6]
    kept_ref, mod_ref, weight_ref, line_ref = refs[6:10]
    qaug_ref, kaug_ref, vaug_ref, x_ref, a_out, tok_out, slot_out = refs[10:17]
    qs_ref, a_ref, tok_ref, slot_ref, sems = refs[17:]
    copies = Copies(sems)
    own = token_refs[0].shape[0]
    slots, total = offset_ref.shape[0], tok_ref.shape[0]
    for n in range(seq):
        tok_ref[row_span(scalar_ref, STARTS + n, own), :] = token_refs[n][...]
    copies.start(tok_ref, tok_out)
    others = [token_refs[n][...] for n in range(1, seq)]
    others = others[0] if seq == 2 else jnp.concatenate(others, axis=0)
    lowered, scaled, keys, values = project(others, mod_ref, weight_ref, line_ref)
    here = row_span(scalar_ref, STARTS, own)
    a_ref[here, :] = own_a_ref[...]
    qs_ref[here, :] = own_qs_ref[...]
    for head in range(HEADS):
        kaug_ref[head, here, :] = own_kaug_ref[head]
        vaug_ref[head, here, :] = own_vaug_ref[head]
        qaug_ref[head, :own, :] = own_qaug_ref[head]
    for n in range(1, seq):
        there = row_span(scalar_ref, STARTS + n, own)
        span = slice((n - 1) * own, n * own)
        a_ref[there, :] = lowered[span]
        qs_ref[there, :] = scaled[span]
        place = place_onehot(lax.broadcasted_iota(jnp.int32, (own, 1), 0) + scalar_ref[STARTS + n])
        for head in range(HEADS):
            cols = head_cols(head)
            kaug_ref[head, there, :] = jnp.concatenate([keys[span, cols], place], axis=1)
            vaug_ref[head, there, :] = jnp.concatenate([values[span, cols], ones_lanes(own)], axis=1)
    copies.start(a_ref, a_out)
    chosen = slot_places(scalar_ref, kept_ref, slots) == lax.broadcasted_iota(jnp.int32, (slots, total), 1)
    chosen = chosen.astype(F32).astype(BF16)
    x_ref[:own, :] = token_refs[0][...]
    x_ref[own:, :] = mm(chosen, tok_ref[...]).astype(BF16)
    slot_ref[...] = mm(chosen, a_ref[...]).astype(BF16)
    copies.start(slot_ref, slot_out)
    query = mm(chosen, qs_ref[...]).astype(BF16)
    for head in range(HEADS):
        cols = head_cols(head)
        qaug_ref[head, own:, :] = jnp.concatenate([query[:, cols], offset_ref[:, cols]], axis=1)
    copies.wait()


def attend_kernel(
    own, qaug_ref, kaug_ref, vaug_ref, mask_ref, o_ref, inverse_ref, e_out, qaug_out, kaug_out, vaug_out, e_ref, sems
):
    rows = qaug_ref.shape[1]
    copies = Copies(sems)
    copies.start(qaug_ref, qaug_out)
    copies.start(kaug_ref, kaug_out)
    copies.start(vaug_ref, vaug_out)
    spans = [(at, size, False) for at, size in blocks_of(0, own, 512)]
    spans += [(at, size, True) for at, size in blocks_of(own, rows - own, 512)]
    items = [(side, *span) for side in range(2) for span in spans]

    def e_copy(head, n):
        side, at, size, masked = items[n]
        span = pl.ds(at, size)
        return pltpu.make_async_copy(
            e_ref.at[head, span], e_out.at[head, span], sems.at[3 + len(spans) * head + n % len(spans)]
        )

    def pair(group, carry):
        scores, spread = {}, {}
        for n in range(len(items) + 2):
            if n < len(items):
                side, at, size, masked = items[n]
                head = 2 * group + side
                scores[n] = mm_t(qaug_ref[head, at : at + size, :], kaug_ref[head])
                if masked:
                    scores[n] = scores[n] + mask_ref[0:1, :]
            if 0 <= n - 1 < len(items):
                side, at, size, masked = items[n - 1]
                found = scores.pop(n - 1)
                spread[n - 1] = jnp.exp(found - jnp.max(found, axis=-1, keepdims=True)).astype(BF16)
                e_ref[2 * group + side, at : at + size, :] = spread[n - 1]
                e_copy(2 * group + side, n - 1).start()
            if 0 <= n - 2:
                side, at, size, masked = items[n - 2]
                mixed = mm(spread.pop(n - 2), vaug_ref[2 * group + side])
                inverse = 1.0 / mixed[:, HDIM : HDIM + 1]
                lanes = slice(side * HDIM, (side + 1) * HDIM)
                o_ref[group, at : at + size, lanes] = mixed[:, :HDIM] * inverse
                inverse_ref[group, at : at + size, lanes] = jnp.broadcast_to(inverse, (size, HDIM))
        return carry

    lax.fori_loop(0, HEADS // 2, pair, 0)
    for head in range(HEADS):
        for n in range(len(spans)):
            e_copy(head, head % 2 * len(spans) + n).wait()
    copies.wait()


def cotangents(scalar_ref, slots, full_ref, slot_ref):
    own = full_ref.shape[0]
    weight = row_weights(scalar_ref, own, slots, own + slot_ref.shape[0])
    return weight, jnp.concatenate([full_ref[...], slot_ref[...]], axis=0).astype(F32) * weight


def feed_kernel(
    slots, scalar_ref, o_ref, x_ref, cot_full_ref, cot_slot_ref, mod_ref, wout_ref, w1_ref,
    w2_ref, line_ref,
    att_ref, hidden_ref, du_ref, bias_ref, keep_ref, send_ref, pay_ref, sems,
):
    rows = x_ref.shape[0]
    gate1, shift2, scale2, gate2 = [mod_ref[n : n + 1, :] for n in range(2, 6)]
    merged = jnp.concatenate([o_ref[n] for n in range(HEADS // 2)], axis=1).astype(BF16)
    attended = mm(merged, wout_ref[...]) + line_ref[OUT_LINE : OUT_LINE + 1, :]
    att_ref[...] = attended
    normed, unused = norm_parts(x_ref[...].astype(F32) + gate1 * attended)
    second = (normed * (1.0 + scale2) + shift2).astype(BF16)
    unused, cot = cotangents(scalar_ref, slots, cot_full_ref, cot_slot_ref)
    dz = (gate2 * cot).astype(BF16)

    bias = jnp.concatenate([line_ref[FC1_LINE + n : FC1_LINE + n + 1, :] for n in range(4)], axis=1)

    def products(c):
        cols = slice(c * CHUNK, (c + 1) * CHUNK)
        return mm(second, w1_ref[:, cols]) + bias[:, cols], mm_t(dz, w2_ref[cols, :])

    chunks = FF // CHUNK
    ready = products(0)
    for c in range(chunks):
        u, back_u = ready
        if c + 1 < chunks:
            ready = products(c + 1)
        cols = slice(c * CHUNK, (c + 1) * CHUNK)
        square = u * u
        t = jnp.tanh(u * (square * (GELU_A * GELU_B) + GELU_A))
        cdf = t * 0.5 + 0.5
        hidden_ref[:, cols] = (u * cdf).astype(BF16)
        slope = cdf * ((1.0 - t) * (u * (square * (3.0 * GELU_A * GELU_B) + GELU_A)) + 1.0)
        du_ref[:, cols] = (slope * back_u).astype(BF16)
    ones = jnp.ones((16, rows), BF16)
    grad = mm(jnp.concatenate([second.T, ones], axis=0), du_ref[...])
    heads = []
    for n in range(4):
        cols = slice(n * D, (n + 1) * D)
        pay_ref[0, cols, :] = grad[:D, cols].astype(BF16)
        heads.append(grad[D : D + 1, cols])
    heads += [jnp.sum(dz.astype(F32), axis=0, keepdims=True), jnp.zeros((3, D), F32)]
    bias_ref[...] = jnp.concatenate(heads, axis=0)
    pay_ref[1, :FF, :] = mm(hidden_ref[...].T, dz).astype(BF16)
    if pay_ref.shape[1] > FF:
        pay_ref[:, FF:, :] = jnp.zeros((2, pay_ref.shape[1] - FF, D), BF16)
    for which in range(2):
        half_copies(scalar_ref[SIDE], pay_ref, keep_ref, send_ref, sems, which)
    for which in range(2):
        pltpu.make_async_copy(pay_ref.at[which], keep_ref, sems.at[which]).wait()


def feed_rest_kernel(
    slots, scalar_ref, o_ref, inverse_ref, x_ref, cot_full_ref, cot_slot_ref, mod_ref, wout_ref, w1_ref,
    w2_ref, line_ref,
    att_ref, hidden_ref, du_ref, bias_ref,
    small_ref, y_full_out, y_slot_out, dm_out, x_out, do_out, go_out, y_ref, dm_ref, do_ref, go_ref, sems,
):
    rows, own = x_ref.shape[0], cot_full_ref.shape[0]
    copies = Copies(sems)
    copies.start(x_ref, x_out)
    gate1, shift2, scale2, gate2 = [mod_ref[n : n + 1, :] for n in range(2, 6)]
    weight, cot = cotangents(scalar_ref, slots, cot_full_ref, cot_slot_ref)
    back = mm_t(du_ref[...], w1_ref[...])
    branch = mm(hidden_ref[...], w2_ref[...]) + line_ref[FC2_LINE : FC2_LINE + 1, :]
    attended = att_ref[...]
    middle = x_ref[...].astype(F32) + gate1 * attended
    normed, inverse = norm_parts(middle)
    y_ref[...] = ((middle + gate2 * branch) * weight).astype(BF16)
    copies.start(y_ref.at[pl.ds(0, own)], y_full_out)
    copies.start(y_ref.at[pl.ds(own, rows - own)], y_slot_out)
    dmid = cot + norm_back(normed, inverse, back * (1.0 + scale2))
    dm_ref[...] = dmid
    copies.start(dm_ref, dm_out)
    datt = (gate1 * dmid).astype(BF16)
    merged_f = jnp.concatenate([o_ref[n] for n in range(HEADS // 2)], axis=1)
    dout = mm_t(datt, wout_ref[...]) * jnp.concatenate([inverse_ref[n] for n in range(HEADS // 2)], axis=1)
    dout = dout.astype(BF16).astype(F32)
    product = dout * merged_f
    high = product.astype(BF16)
    low = (product - high.astype(F32)).astype(BF16)
    row = lax.broadcasted_iota(jnp.int32, (D, 128), 0)
    lane = lax.broadcasted_iota(jnp.int32, (D, 128), 1)
    heads = jnp.where(row // HDIM == lane // 2, -1.0, 0.0).astype(BF16)
    less = mm(high, heads) + mm(low, heads)
    lane = lax.broadcasted_iota(jnp.int32, (rows, 128), 1)
    kept = less.astype(BF16).astype(F32)
    pair = jnp.where(lane % 2 == 0, kept, less - kept)
    for head in range(HEADS):
        tile = dout[:, head // 2 * 128 : (head // 2 + 1) * 128]
        if head % 2:
            tile = pltpu.roll(tile, HDIM, 1)
        more = pltpu.roll(pair, HDIM - 2 * head, 1)
        more = jnp.where(lane < HDIM + 2, more, 0.0)
        do_ref[head] = jnp.where(lane < HDIM, tile, more).astype(BF16)
    copies.start(do_ref, do_out)
    go_ref[...] = mm(merged_f.astype(BF16).T, datt).astype(BF16)
    copies.start(go_ref, go_out)
    column = lambda value: jnp.sum(value.astype(F32), axis=0, keepdims=True)
    sums = [dmid * attended, back, back * normed, cot * branch, datt]
    sums = [column(value) for value in sums] + [bias_ref[:5, :], jnp.zeros((6, D), F32)]
    small_ref[...] = jnp.concatenate(sums, axis=0)
    copies.wait()


def attend_back(own, e_ref, q_ref, k_ref, v_ref, do_ref, place_ref, outs, sums):
    dq_ref, dk_ref, dv_ref, tab_ref = outs
    dkt_ref, dvt_ref, part_ref = sums
    rows = q_ref.shape[1]
    spans = blocks_of(0, own, 256) + blocks_of(own, rows - own, 256)
    items = [(side, *span) for side in range(2) for span in spans]
    grads, found = {}, {}
    for n in range(len(items) + 2):
        if n < len(items):
            side, at, size = items[n]
            grads[n] = mm_t(do_ref[side, at : at + size, :], v_ref[side])
        if 0 <= n - 1 < len(items):
            side, at, size = items[n - 1]
            found[n - 1] = (e_ref[side, at : at + size, :].astype(F32) * grads.pop(n - 1)).astype(BF16)
        if 0 <= n - 2:
            side, at, size = items[n - 2]
            lanes = slice(side * HDIM, (side + 1) * HDIM)
            ds = found.pop(n - 2)
            dq = mm(ds, k_ref[side])
            dq_ref[at : at + size, lanes] = (dq[:, :HDIM] * (1.0 / math.sqrt(HDIM))).astype(BF16)
            part_ref[at : at + size, lanes] = dq[:, HDIM:].astype(BF16)
            dkt = mm(q_ref[side, at : at + size, :HDIM].T, ds)
            dvt = mm(do_ref[side, at : at + size, :HDIM].T, e_ref[side, at : at + size, :])
            if at == 0:
                dkt_ref[lanes, :] = dkt
                dvt_ref[lanes, :] = dvt
            else:
                dkt_ref[lanes, :] += dkt
                dvt_ref[lanes, :] += dvt
    tab_ref[...] = mm(place_ref[...], part_ref[...])
    dk_ref[...] = dkt_ref[...].astype(BF16).T
    dv_ref[...] = dvt_ref[...].astype(BF16).T


def back_kernel(own, everyone, scalar_ref, kept_ref, mod_ref, prior_ref, *refs):
    group_sources, refs = refs[:5], refs[5:]
    sources, refs = refs[:7], refs[7:]
    keep_ref, send_ref, dx_out, dx_own_out, refs = *refs[:4], refs[4:]
    group_local, refs = refs[:5], refs[5:]
    local, refs = refs[:7], refs[7:]
    dq_ref, dk_ref, dv_ref, tab_ref, normed_ref, inverse_ref, dxs_ref, dkt_ref, dvt_ref, pay_ref = refs[:10]
    place_ref, part_ref, dx_ref, dx_own_ref, group_sems, sems, pay_sems = refs[10:]
    tok_ref, a_ref, x_ref, slot_ref, weight_ref, dm_ref, go_ref = local
    step = pl.program_id(0)
    last = pl.num_programs(0) - 1
    slot = step % 2

    def fetches(group, place):
        return [
            pltpu.make_async_copy(source.at[pl.ds(2 * group, 2)], target.at[place], group_sems.at[place, n])
            for n, (source, target) in enumerate(zip(group_sources, group_local))
        ]

    def copies():
        return [
            pltpu.make_async_copy(source, target, sems.at[n])
            for n, (source, target) in enumerate(zip(sources, local))
        ]

    @pl.when(step == 0)
    def first():
        whole = copies()
        whole[0].start()
        for copy in fetches(0, 0):
            copy.start()
        for copy in whole[1:]:
            copy.start()
        for copy in fetches(1, 1):
            copy.start()
        slots = x_ref.shape[0] - own
        place_ref[...] = place_onehot(row_places(scalar_ref, kept_ref, own, slots), turned=True).T
        whole[0].wait()
        normed, inverse = norm_parts(tok_ref[...].astype(F32))
        normed_ref[...] = normed
        inverse_ref[...] = jnp.broadcast_to(inverse, inverse_ref.shape)

    @pl.when((step > 0) & (step + 1 < last))
    def following():
        for copy in fetches(step + 1, 1 - slot):
            copy.start()

    @pl.when(step < last)
    def attention():
        for copy in fetches(step, slot):
            copy.wait()
        outs = dq_ref.at[step], dk_ref.at[step], dv_ref.at[step], tab_ref.at[step]
        attend_back(own, *[ref.at[slot] for ref in group_local], place_ref, outs, (dkt_ref, dvt_ref, part_ref))

    @pl.when(step == last)
    def projections():
        for copy in copies()[1:]:
            copy.wait()
        groups = dq_ref.shape[0]
        total = tok_ref.shape[0]
        rows = x_ref.shape[0]
        slots = rows - own
        scale = mod_ref[1:2, :]
        here = row_span(scalar_ref, STARTS, own)

        def joined(ref, span):
            return jnp.concatenate([ref[n, span, :] for n in range(groups)], axis=1)

        every = slice(0, total)
        dk, dv = joined(dk_ref, every), joined(dv_ref, every)
        dq_own, dq_slot = joined(dq_ref, slice(0, own)), joined(dq_ref, slice(own, rows))
        column = lambda value: jnp.sum(value.astype(F32), axis=0, keepdims=True)
        lowered_t = a_ref[...].T
        pay_ref[0:D, :] = (mm(a_ref[here, :].T, dq_own) + mm(slot_ref[...].T, dq_slot)).astype(BF16)
        pay_ref[D : 2 * D, :] = mm(lowered_t, dk).astype(BF16)
        pay_ref[2 * D : 3 * D, :] = mm(lowered_t, dv).astype(BF16)
        pay_ref[3 * D : 4 * D, :] = go_ref[...]
        slot_normed, slot_inverse = norm_parts(x_ref[own:, :].astype(F32))
        da = mm_t(dq_slot, weight_ref[:, :D])
        shift_sum, scale_sum = column(da), column(da * slot_normed)
        spread = dm_ref[own:, :] + norm_back(slot_normed, slot_inverse, da * (1.0 + scale))
        chosen = slot_places(scalar_ref, kept_ref, slots) == lax.broadcasted_iota(jnp.int32, (slots, total), 1)
        chosen = chosen.astype(F32)
        moved = mm(chosen.astype(BF16).T, spread.astype(BF16))
        dxs_ref[...] = mm_t(dk, weight_ref[:, D : 2 * D]) + mm_t(dv, weight_ref[:, 2 * D :])
        dxs_ref[here, :] += mm_t(dq_own, weight_ref[:, :D])
        da = dxs_ref[...]
        normed = normed_ref[...]
        shift_sum, scale_sum = shift_sum + column(da), scale_sum + column(da * normed)
        inverse = jnp.concatenate([inverse_ref[...]] * (D // 128), axis=1)
        dxs_ref[...] = moved + norm_back(normed, inverse, da * (1.0 + scale))
        dx_own_ref[...] = dxs_ref[here, :] + dm_ref[:own, :]
        others = dx_ref.shape[0]
        for n in range(others):
            dx_ref[n] = dxs_ref[row_span(scalar_ref, STARTS + 1 + others + n, own), :].astype(BF16)
        halves = Copies(pay_sems)
        halves.start(dx_own_ref, dx_own_out)
        halves.start(dx_ref, dx_out)
        rel = table_sums([tab_ref[n] for n in range(groups)])
        first = jnp.where(scalar_ref[SEQ_PLACE] == 0, 1, 0)
        label = scalar_ref[LABEL]
        number = lax.broadcasted_iota(jnp.int32, (1, D), 1)
        digits = jnp.where(number == scalar_ref[PLACE], label // GRID * first, 0)
        digits = jnp.where(number == 128 + scalar_ref[PLACE], label % GRID * first, digits).astype(F32)
        smalls = jnp.concatenate(
            [
                shift_sum, scale_sum, prior_ref[0:4, :], column(dq_own) + column(dq_slot), column(dv),
                *rel, prior_ref[4:5, :], digits, prior_ref[5:10, :], mod_ref[COND_LINE : COND_LINE + 1, :],
                jnp.zeros((14, D), F32),
            ],
            axis=0,
        ).astype(BF16)
        tail = pay_ref.shape[0] - 4 * D
        row = lax.broadcasted_iota(jnp.int32, (tail, 32), 0)
        lane = lax.broadcasted_iota(jnp.int32, (tail, 32), 1)
        kind = jnp.where(row < 6 * everyone, row // everyone, jnp.where(scalar_ref[SEQ_PLACE] == 0, 17, -1))
        wanted = jnp.where(row % everyone == scalar_ref[PLACE], kind, -1)
        after = row - 7 * everyone
        wanted = jnp.where(after < 0, wanted, jnp.where(after < 11, after + 6, -1))
        pay_ref[4 * D :, :] = mm((lane == wanted).astype(F32).astype(BF16), smalls).astype(BF16)
        split_halves(halves, scalar_ref[SIDE], pay_ref, keep_ref, send_ref)
        halves.wait()


def table_sums(tabs):
    found = ([], [])
    for tab in tabs:
        for side in range(2):
            for part in range(2):
                at = 2 * side * GRID + part * GRID
                square = tab[part * GRID : (part + 1) * GRID, at : at + GRID]
                wide = jnp.concatenate([square, jnp.zeros((GRID, 128 - GRID), F32)], axis=1)
                turned = pltpu.roll(wide, 0, 1, stride=1, stride_axis=0)
                found[part].append(jnp.sum(turned, axis=0, keepdims=True)[:, : 2 * GRID])
    return [jnp.concatenate(parts, axis=1) for parts in found]


def call(kernel, outs, scratch, args, scalars=0, far=0, away=0, copies=0, micros=1, limit=32):
    scratches = [pltpu.VMEM(shape, dtype) for shape, dtype in scratch]
    if copies:
        scratches.append(pltpu.SemaphoreType.DMA((copies,)))
    return pl.pallas_call(
        kernel,
        out_shape=[jax.ShapeDtypeStruct(shape, dtype) for shape, dtype in outs[: len(outs) - away]]
        + [pltpu.HBM(shape, dtype) for shape, dtype in outs[len(outs) - away :]],
        in_specs=[smem] * scalars + [vmem] * (len(args) - scalars - far) + [hbm] * far,
        out_specs=[vmem] * (len(outs) - away) + [hbm] * away,
        scratch_shapes=scratches,
        compiler_params=pltpu.CompilerParams(vmem_limit_bytes=limit * MIB),
        cost_estimate=pl.CostEstimate(flops=micros * 10**9, bytes_accessed=MIB, transcendentals=0),
    )(*args)


def own_call(outs, scalars, sources):
    return pl.pallas_call(
        own_kernel,
        out_shape=[jax.ShapeDtypeStruct(shape, dtype) for shape, dtype in outs],
        in_specs=[smem] * len(scalars) + [hbm] * len(sources),
        out_specs=[smem] + [vmem] * (len(outs) - 1),
        scratch_shapes=[pltpu.VMEM(value.shape, value.dtype) for value in sources]
        + [pltpu.SemaphoreType.DMA((len(sources),))],
        compiler_params=pltpu.CompilerParams(vmem_limit_bytes=16 * MIB),
        cost_estimate=pl.CostEstimate(flops=3 * 10**9, bytes_accessed=MIB, transcendentals=0),
    )(*scalars, *map(in_hbm, sources))


def in_hbm(value):
    return pltpu.with_memory_space_constraint(value, pltpu.HBM)


def add_kernel(pieces, left_ref, right_ref, sum_out, sum_ref, sems):
    copies = Copies(sems)
    rows = sum_ref.shape[0] // pieces
    for n in range(pieces):
        span = pl.ds(n * rows, rows)
        sum_ref[span, :] = (left_ref[span, :].astype(F32) + right_ref[span, :].astype(F32)).astype(BF16)
        copies.start(sum_ref.at[span], sum_out.at[span])
    copies.wait()


def add_call(left, right, micros):
    pieces = 4 if left.shape[0] % 64 == 0 else 1
    out = (left.shape, BF16)
    return call(
        functools.partial(add_kernel, pieces), [out], [out], [left, right], away=1, copies=pieces, micros=micros,
        limit=8,
    )[0]


def spread_kernel(near_ref, far_ref, wide_out, sum_ref, sems):
    sum_ref[...] = (near_ref[...].astype(F32) + far_ref[...].astype(F32)).astype(BF16)
    copies = Copies(sems)
    for n in range(wide_out.shape[0]):
        copies.start(sum_ref, wide_out.at[n])
    copies.wait()


def spread_call(near, far, peers):
    return call(
        spread_kernel, [((peers,) + near.shape, BF16)], [(near.shape, BF16)], [near, far], away=1, copies=peers,
        limit=8,
    )[0]


def back_call(own, everyone, groups_of, sources, scalars, kept, mod, prior, tail_half):
    rows, total = groups_of[1].shape[1], groups_of[2].shape[1]
    groups = HEADS // 2
    others = total // own - 1
    whole = lambda shape: pl.BlockSpec(shape, lambda n: (0,) * len(shape))
    outs = [((tail_half, D), BF16), ((tail_half, D), BF16), ((others, own, D), BF16), ((own, D), F32)]
    scratch = [((2, 2) + value.shape[1:], value.dtype) for value in groups_of]
    scratch += [(value.shape, value.dtype) for value in sources]
    scratch += [
        ((groups, rows, 128), BF16), ((groups, total, 128), BF16), ((groups, total, 128), BF16),
        ((groups, 2 * GRID, 128), F32), ((total, D), F32), ((total, 128), F32), ((total, D), F32),
        ((128, total), F32), ((128, total), F32), ((2 * tail_half, D), BF16),
        ((2 * GRID, rows), BF16), ((rows, 128), BF16), outs[2], outs[3],
    ]
    small = [kept, mod, prior]
    return pl.pallas_call(
        functools.partial(back_kernel, own, everyone),
        grid=(groups + 1,),
        out_shape=[jax.ShapeDtypeStruct(shape, dtype) for shape, dtype in outs[:2]]
        + [pltpu.HBM(shape, dtype) for shape, dtype in outs[2:]],
        in_specs=[smem] + [whole(value.shape) for value in small] + [hbm] * (len(groups_of) + len(sources)),
        out_specs=[vmem, vmem, hbm, hbm],
        scratch_shapes=[pltpu.VMEM(shape, dtype) for shape, dtype in scratch]
        + [pltpu.SemaphoreType.DMA((2, 5)), pltpu.SemaphoreType.DMA((7,)), pltpu.SemaphoreType.DMA((4,))],
        compiler_params=pltpu.CompilerParams(
            vmem_limit_bytes=48 * MIB, dimension_semantics=("arbitrary",)
        ),
        cost_estimate=pl.CostEstimate(flops=18 * 10**9, bytes_accessed=MIB, transcendentals=0),
    )(scalars, *small, *map(in_hbm, groups_of), *map(in_hbm, sources))


def halves_reader(side_ref, mine_ref, other_ref):
    half = mine_ref.shape[0]

    def get(at, count):
        found = []
        for which in range(2):
            first, last = max(at, which * half), min(at + count, (which + 1) * half)
            if first < last:
                span = slice(first - which * half, last - which * half)
                found.append(jnp.where(side_ref[0] == which, mine_ref[span, :], other_ref[span, :]))
        return found[0] if len(found) == 1 else jnp.concatenate(found, axis=0)

    return get


def widen_half(core, half_ref, g1_out, g2_out, wide_ref, sems):
    for which in range(2):

        @pl.when(core == which)
        def widen():
            copies = Copies(sems)
            for n in range(4):
                rows = pl.ds(n * D, D)
                wide_ref[rows, :] = half_ref[rows, :].astype(F32)
                copies.start(wide_ref.at[rows], g2_out.at[rows] if which else g1_out.at[:, rows])
            copies.wait()


def near_half_kernel(side_ref, half_ref, g1_out, g2_out, wide_ref, sems):
    widen_half(side_ref[0], half_ref, g1_out, g2_out, wide_ref, sems)


def far_half_kernel(side_ref, half_ref, g1_in, g2_in, g1_out, g2_out, wide_ref, sems):
    widen_half(1 - side_ref[0], half_ref, g1_out, g2_out, wide_ref, sems)


def widen_near(sides, layer_half):
    return pl.pallas_call(
        near_half_kernel,
        out_shape=[pltpu.HBM((D, FF), F32), pltpu.HBM((FF, D), F32)],
        in_specs=[smem, vmem],
        out_specs=[hbm, hbm],
        scratch_shapes=[pltpu.VMEM((FF, D), F32), pltpu.SemaphoreType.DMA((4,))],
        compiler_params=pltpu.CompilerParams(vmem_limit_bytes=8 * MIB),
        cost_estimate=pl.CostEstimate(flops=10**9, bytes_accessed=MIB, transcendentals=0),
    )(sides, layer_half)


def widen_far(sides, other, first):
    return pl.pallas_call(
        far_half_kernel,
        out_shape=[pltpu.HBM((D, FF), F32), pltpu.HBM((FF, D), F32)],
        in_specs=[smem, vmem, hbm, hbm],
        out_specs=[hbm, hbm],
        input_output_aliases={2: 0, 3: 1},
        scratch_shapes=[pltpu.VMEM((FF, D), F32), pltpu.SemaphoreType.DMA((4,))],
        compiler_params=pltpu.CompilerParams(vmem_limit_bytes=8 * MIB),
        cost_estimate=pl.CostEstimate(flops=10**9, bytes_accessed=MIB, transcendentals=0),
    )(sides, other, *map(in_hbm, first))


def last_kernel(
    everyone, side_ref, mine_ref, other_ref, ada_in, qv_ref, rel_ref, out_bias_ref, ada_bias_ref, bias1_ref,
    bias2_ref, gqkv_out, gada_out, table_out, go_out, gqkv_ref, gada_ref, table_ref, go_ref, ada_ref, sems,
):
    get = halves_reader(side_ref, mine_ref, other_ref)
    copies = Copies(sems)
    copies.start(ada_in, ada_ref)
    for n in range(3):
        cols = pl.ds(n * D, D)
        gqkv_ref[:, cols] = get(n * D, D).astype(F32)
        copies.start(gqkv_ref.at[:, cols], gqkv_out.at[:, cols])
    go_ref[...] = get(3 * D, D).astype(F32)
    copies.start(go_ref, go_out)
    cond = get(4 * D + 6 * everyone, everyone).astype(F32)
    gate = 1.0 / (1.0 + jnp.exp(-cond))
    act_t = (cond * gate).astype(BF16).T
    dmods = [get(4 * D + n * everyone, everyone) for n in range(6)]
    small = get(4 * D + 7 * everyone, 16).astype(F32)

    def ada():
        for n in range(6):
            cols = pl.ds(n * D, D)
            gada_ref[:, cols] = mm(act_t, dmods[n])
            copies.start(gada_ref.at[:, cols], gada_out.at[:, cols])
            ada_bias_ref[cols] = jnp.sum(dmods[n].astype(F32), axis=0)

    def table():
        copies.made.pop(0).wait()
        back = jnp.zeros((everyone, D), F32)
        for n in range(6):
            back = back + mm_t(dmods[n], ada_ref[:, n * D : (n + 1) * D])
        back = gate * (1.0 + cond * (1.0 - gate)) * back
        high = back.astype(BF16)
        low = (back - high.astype(F32)).astype(BF16)
        label = (small[5:6, :everyone] * GRID + small[5:6, 128 : 128 + everyone]).astype(jnp.int32)
        classes = table_ref.shape[0]
        wide = round_up(classes, 128)
        hot = (label == lax.broadcasted_iota(jnp.int32, (wide, everyone), 0)).astype(F32).astype(BF16)
        table_ref[...] = (mm(hot, high) + mm(hot, low))[:classes]
        copies.start(table_ref, table_out)

    ada()
    table()
    qv_ref[...] = small[:2]
    for part in range(2):
        for head in range(HEADS):
            at = 2 * GRID * head
            rel_ref[head, part : part + 1, :] = small[2 + part : 3 + part, at : at + 2 * GRID - 1]
    out_bias_ref[...] = small[4]
    for n in range(4):
        bias1_ref[pl.ds(n * D, D)] = small[6 + n]
    bias2_ref[...] = small[10]
    copies.wait()


def swap_cores(value, dp):
    return lax.ppermute(value, "dp", [(n, n ^ 1) for n in range(dp)])


def exchange(value, dp, seq):
    groups = [
        [(far * (dp // 2) + 2 * pair + core) * seq + at for pair in range(dp // 4) for at in range(seq)]
        for far in range(2)
        for core in range(2)
    ]
    return lax.all_to_all(value, AXES, 0, 0, axis_index_groups=groups)


def near_sum(pieces):
    return jnp.sum(pieces.astype(F32), axis=0).astype(BF16)


def far_half(near, dp):
    return lax.ppermute(near, "dp", [(n, (n + dp // 2) % dp) for n in range(dp)])


def assemble_kernel(cut, place_ref, pair_ref, a1_ref, b1_ref, a2_ref, b2_ref, half_ref):
    rows = pair_ref.shape[1]
    for near in range(2):
        for x in range(2):
            for y in range(2):
                at = (place_ref[0] ^ (4 * near + 2 * x + y)) * rows
                if x:
                    half_ref[pl.ds(pl.multiple_of(at, 16), cut), :] = a2_ref[y, near]
                elif y:
                    half_ref[pl.ds(pl.multiple_of(at, 16), cut), :] = a1_ref[near]
                else:
                    half_ref[pl.ds(pl.multiple_of(at, 16), cut), :] = pair_ref[near, :cut, :]
                rest = pl.ds(pl.multiple_of(at + cut, 16), rows - cut)
                if y:
                    half_ref[rest, :] = b2_ref[x, near]
                elif x:
                    half_ref[rest, :] = b1_ref[near]
                else:
                    half_ref[rest, :] = pair_ref[near, cut:, :]


def after(value, *others):
    return lax.optimization_barrier((value, *others))[0]


def gather_chunks(chunk, last_near, before, between, finish, dp, seq):
    rows = chunk.shape[0]
    cut = round_up(rows // 2, 16)
    place = lax.axis_index("dp") % (dp // 2) // 2 * seq + lax.axis_index("seq")
    along_x = lambda value: lax.ppermute(value, "dp", [(n, n ^ 2) for n in range(dp)])
    along_y = lambda value: lax.ppermute(value, "seq", [(n, n ^ 1) for n in range(seq)])
    chunk = after(chunk, last_near, before)
    last_wide = finish(last_near)
    pair = jnp.stack([chunk, lax.ppermute(chunk, "dp", [(n, n ^ 4) for n in range(dp)])])
    pair = after(pair, between)
    a, b = pair[:, :cut], pair[:, cut:]
    a1, b1 = along_y(a), along_x(b)
    a, b = jnp.stack([a, a1]), jnp.stack([b, b1])
    a, b = after((a, b), last_wide)
    a2, b2 = along_x(a), along_y(b)
    held = (a2, b2)

    def assemble(a2, b2):
        return call(
            functools.partial(assemble_kernel, cut), [((8 * rows, D), BF16)], [],
            [place.astype(jnp.int32).reshape(1), pair, a1, b1, a2, b2], scalars=1, limit=8,
        )[0]

    return (a2, b2), assemble, last_wide, held


def scatter_rows(partial, seq):
    return [
        lax.ppermute(partial[step - 1], "seq", [(n, (n + step) % seq) for n in range(seq)])
        for step in range(1, seq)
    ]


def body(
    dp, seq, image_tokens, kept_index, kept_count, sample_valid, timestep, class_label, class_table,
    ada_weight, ada_bias, qkv_weight, qv_bias, rel_bias, out_weight, out_bias, fc1_weight,
    fc1_bias, fc2_weight, fc2_bias, grad_full, grad_masked,
):
    samples, own, width = image_tokens.shape
    held = kept_index.shape[1]
    slots = grad_masked.shape[1]
    padded = round_up(slots, 16)
    rows = own + padded
    total = own * seq
    everyone = dp * samples
    classes = class_table.shape[0]
    dp_place, seq_place = lax.axis_index("dp"), lax.axis_index("seq")

    half = round_up(FF, dp * seq * 4)
    peers = dp // 4 * seq
    side = dp_place % 2
    sides = side.astype(jnp.int32).reshape(1)
    tail_half = round_up(4 * D + 16 + 7 * everyone, dp * seq * 4) // 2
    kept_of = []
    for s in range(samples):
        tokens = [image_tokens[s]]
        for step in range(1, seq):
            tokens.append(lax.ppermute(tokens[0], "seq", [(n, (n + step) % seq) for n in range(seq)]))
        number = jnp.arange(STARTS + 2 * seq - 1, dtype=jnp.int32)
        block = number - STARTS
        scalars = jnp.where(block < seq, seq_place - block, seq_place + block - seq + 1) % seq * own
        entries = {
            SIDE: side, PLACE: dp_place * samples + s, SLOT_START: seq_place * slots, SEQ_PLACE: seq_place,
        }
        for at, entry in entries.items():
            scalars = jnp.where(number == at, entry, scalars)
        places = scalars.astype(jnp.int32)
        held_rows = held + padded - slots
        cot_slot = jnp.pad(grad_masked[s], ((0, padded - slots), (0, 0)))
        one = slice(s, s + 1)
        scalars, kept, lines, mod, *owned, mask = own_call(
            [
                (places.shape, jnp.int32), ((held_rows, 1), jnp.int32), ((16, D), F32),
                ((8, D), F32), ((own, D), BF16), ((own, D), BF16), ((HEADS, own, 128), BF16),
                ((HEADS, own, 128), BF16), ((HEADS, own, 128), BF16), ((padded, D), BF16), ((8, total), F32),
            ],
            [places, kept_count[one], sample_valid[one], timestep[one], class_label[one]],
            [
                kept_index[one], rel_bias.transpose(1, 0, 2), ada_bias, qv_bias, out_bias, fc1_bias, fc2_bias,
                class_table, ada_weight, tokens[0], qkv_weight,
            ],
        )
        qaug, kaug, vaug, x, lowered, whole, slot = call(
            functools.partial(prep_kernel, seq),
            [
                ((HEADS, rows, 128), BF16), ((HEADS, total, 128), BF16), ((HEADS, total, 128), BF16),
                ((rows, D), BF16), ((total, D), BF16), ((total, D), BF16), ((padded, D), BF16),
            ],
            [((total, D), BF16), ((total, D), BF16), ((total, D), BF16), ((padded, D), BF16)],
            [scalars, *tokens, *owned, kept, mod, qkv_weight, lines],
            scalars=1, away=3, copies=3, micros=3, limit=16,
        )
        mixed, inverse, spread_far, qaug_far, kaug_far, vaug_far = call(
            functools.partial(attend_kernel, own),
            [
                ((HEADS // 2, rows, 128), F32), ((HEADS // 2, rows, 128), F32),
                ((HEADS, rows, total), BF16), (qaug.shape, BF16), (kaug.shape, BF16), (vaug.shape, BF16),
            ],
            [((HEADS, rows, total), BF16)],
            [qaug, kaug, vaug, mask],
            away=4, copies=3 + 8 * HEADS, micros=10, limit=32,
        )
        attended, hidden, du, biases, keep, send = call(
            functools.partial(feed_kernel, slots),
            [
                ((rows, D), F32), ((rows, FF), BF16), ((rows, FF), BF16), ((8, D), F32), ((half, D), BF16),
                ((half, D), BF16),
            ],
            [((2, half, D), BF16)],
            [
                scalars, mixed, x, grad_full[s], cot_slot, mod, out_weight, fc1_weight, fc2_weight, lines,
            ],
            scalars=1, copies=2, micros=10, limit=24,
        )
        kept_of.append(dict(
            rest=[
                scalars, mixed, inverse, x, grad_full[s], cot_slot, mod, out_weight, fc1_weight, fc2_weight,
                lines, attended, hidden, du, biases,
            ],
            groups=[spread_far, qaug_far, kaug_far, vaug_far], sources=[whole, lowered, slot, qkv_weight],
            small=[scalars, kept, mod], keep=keep, send=send,
        ))

    def added(arrays):
        if len(arrays) == 1:
            return arrays[0]
        return functools.reduce(jnp.add, [a.astype(F32) for a in arrays]).astype(arrays[0].dtype)

    keep, send = added([k["keep"] for k in kept_of]), added([k["send"] for k in kept_of])
    got = swap_cores(send, dp)

    rests = [
        call(
            functools.partial(feed_rest_kernel, slots),
            [
                ((16, D), F32), ((own, D), BF16), ((padded, D), BF16), ((rows, D), F32), ((rows, D), BF16),
                ((HEADS, rows, 128), BF16), ((D, D), BF16),
            ],
            [((rows, D), BF16), ((rows, D), F32), ((HEADS, rows, 128), BF16), ((D, D), BF16)],
            k["rest"],
            scalars=1, away=6, copies=6, micros=6, limit=24,
        )
        for k in kept_of
    ]
    mine = add_call(keep, got, 1)
    mine, rests = lax.optimization_barrier((mine, rests))
    pieces = exchange(mine.reshape(peers, half // peers, D), dp, seq)
    tails = []
    for k, rest in zip(kept_of, rests):
        small, unused_full, unused_slot, dmid, x_far, dout_far, grad_out = rest
        whole, lowered, slot, weights = k["sources"]
        tails.append(
            back_call(
                own, everyone, [*k["groups"], dout_far], [whole, lowered, x_far, slot, weights, dmid, grad_out],
                *k["small"], small, tail_half,
            )
        )

    keep, send = added([t[0] for t in tails]), added([t[1] for t in tails])
    keep, send, pieces = lax.optimization_barrier((keep, send, pieces))
    got = swap_cores(send, dp)
    mine = add_call(keep, got, 1).reshape(peers, tail_half // peers, D)
    pieces, mine = lax.optimization_barrier((pieces, mine))
    near = near_sum(pieces)
    far = far_half(near, dp)
    first_moved = [scatter_rows(t[2][:, : own // 2], seq) for t in tails]
    last_near = near_sum(exchange(mine, dp, seq))
    last_moved = [scatter_rows(after(t[2][:, own // 2 :], last_near), seq) for t in tails]

    def finish(last_near):
        wide = spread_call(last_near, far_half(last_near, dp), peers)
        return wide

    if dp == 16 and seq == 2:
        chunk = (near.astype(F32) + far.astype(F32)).astype(BF16)
        parts, assemble, last_wide, held = gather_chunks(chunk, last_near, first_moved, last_moved, finish, dp, seq)
    else:
        parts = exchange(spread_call(near, far, peers), dp, seq).reshape(half, D)
        assemble = lambda whole: whole
        parts = (parts,)
        held = parts
        last_wide = finish(last_near)
    last_half = exchange(last_wide, dp, seq).reshape(tail_half, D)
    out_full = jnp.stack([rest[1] for rest in rests])
    out_masked = jnp.stack([rest[2][:slots] for rest in rests])
    layer_half = assemble(*parts)
    other = swap_cores(layer_half, dp)
    first = widen_near(sides, layer_half)
    grad_input = []
    for tail, *moved in zip(tails, first_moved, last_moved):
        came = [jnp.concatenate(both).astype(F32) for both in zip(*moved)]
        grad_input.append(functools.reduce(jnp.add, came, tail[3]))
    grad_input = jnp.stack(grad_input)
    last_half = after(last_half, layer_half, grad_input)
    grad_fc1, grad_fc2 = widen_far(sides, other, first)
    found = call(
        functools.partial(last_kernel, everyone),
        [
            ((2, D), F32), ((HEADS, 2, 2 * GRID - 1), F32), ((D,), F32), ((6 * D,), F32), ((FF,), F32), ((D,), F32),
            ((D, 3 * D), F32), ((D, 6 * D), F32), ((classes, D), F32), ((D, D), F32),
        ],
        [((D, 3 * D), F32), ((D, 6 * D), F32), ((classes, D), F32), ((D, D), F32), (ada_weight.shape, BF16)],
        [sides, last_half, swap_cores(last_half, dp), in_hbm(ada_weight)],
        scalars=1, far=1, away=4, copies=12, micros=4, limit=16,
    )
    grad_qv, grad_rel, grad_out_bias, grad_ada_bias, grad_fc1_bias, grad_fc2_bias = found[:6]
    grad_qkv, grad_ada, grad_table, grad_out = found[6:]
    grad_rel = grad_rel.transpose(1, 0, 2)
    return (
        out_full, out_masked, grad_input, grad_table, grad_ada, grad_ada_bias, grad_qkv, grad_qv,
        grad_rel, grad_out, grad_out_bias, grad_fc1, grad_fc1_bias, grad_fc2, grad_fc2_bias,
    )


def solution(mesh):
    split = P("dp", "seq", None)
    placed = (split, P("dp", None)) + (P("dp"),) * 4 + (P(),) * 12 + (split, split)
    return jax.shard_map(
        functools.partial(body, mesh.shape["dp"], mesh.shape["seq"]),
        mesh=mesh,
        in_specs=placed,
        out_specs=(split,) * 3 + (P(),) * 12,
        check_vma=False,
    )
```

```python
import functools
import math

import jax
import jax.numpy as jnp
from jax import lax
from jax.experimental import pallas as pl
from jax.experimental.pallas import tpu as pltpu
from jax.sharding import PartitionSpec as P

D = 384
HEADS = 6
HDIM = 64
GRID = 32
FF = 1536
CHUNK = 256

AXES = ("dp", "seq")
F32 = jnp.float32
BF16 = jnp.bfloat16
MIB = 1024 * 1024
GELU_A = math.sqrt(2.0 / math.pi)
GELU_B = 0.044715

highest = lax.Precision.HIGHEST
big_negative = -1e30
vmem = pl.BlockSpec(memory_space=pltpu.VMEM)
smem = pl.BlockSpec(memory_space=pltpu.SMEM)
hbm = pl.BlockSpec(memory_space=pltpu.HBM)


def round_up(value, step):
    return -(-value // step) * step


def blocks_of(first, count, most):
    pieces = -(-count // most)
    size = round_up(-(-count // pieces), 16)
    found = []
    at = 0
    while at < count:
        found.append((first + at, min(size, count - at)))
        at += size
    return found


def mm(left, right):
    return lax.dot_general(left, right, (((1,), (0,)), ((), ())), preferred_element_type=F32)


def mm_t(left, right):
    return lax.dot_general(left, right, (((1,), (1,)), ((), ())), preferred_element_type=F32)


def norm_parts(value):
    average = jnp.mean(value, axis=-1, keepdims=True)
    centred = value - average
    variance = jnp.mean(centred * centred, axis=-1, keepdims=True)
    inverse = lax.rsqrt(variance + 1e-06)
    return (centred * inverse, inverse)


def norm_back(normed, inverse, grad):
    first = jnp.mean(grad, axis=-1, keepdims=True)
    second = jnp.mean(grad * normed, axis=-1, keepdims=True)
    return inverse * (grad - first - normed * second)


def place_onehot(position, turned=False):
    lane = lax.broadcasted_iota(jnp.int32, (position.shape[0], 2 * GRID), 1)
    if turned:
        lane = jnp.where(lane < GRID, GRID - 1 - lane, 3 * GRID - 1 - lane)
    wanted = jnp.where(lane < GRID, position // GRID, position % GRID + GRID)
    return (lane == wanted).astype(F32).astype(BF16)


class Copies:
    def __init__(self, sems):
        self.sems, self.made, self.count = sems, [], 0

    def start(self, source, target):
        copy = pltpu.make_async_copy(source, target, self.sems.at[self.count])
        copy.start()
        self.made.append(copy)
        self.count += 1

    def wait(self):
        for copy in self.made:
            copy.wait()


def half_copies(side, payload_ref, keep_ref, send_ref, sems, which):
    for target, chosen in ((keep_ref, side == which), (send_ref, side != which)):

        @pl.when(chosen)
        def start():
            pltpu.make_async_copy(payload_ref.at[which], target, sems.at[which]).start()


def split_halves(copies, side, payload_ref, keep_ref, send_ref):
    half = keep_ref.shape[0]
    for which, target in ((side, keep_ref), (1 - side, send_ref)):
        copies.start(payload_ref.at[pl.ds(pl.multiple_of(which * half, 16), half)], target)


SIDE, PLACE, SLOT_START, COUNT, VALID, LABEL, SEQ_PLACE, STARTS = range(8)


def row_span(scalar_ref, number, count):
    return pl.ds(pl.multiple_of(scalar_ref[number], 16), count)


def slot_places(scalar_ref, kept_ref, slots):
    return kept_ref[pl.ds(pl.multiple_of(scalar_ref[SLOT_START], 8), slots), :]


def row_places(scalar_ref, kept_ref, own, slots):
    mine = lax.broadcasted_iota(jnp.int32, (own, 1), 0) + scalar_ref[STARTS]
    return jnp.concatenate([mine, slot_places(scalar_ref, kept_ref, slots)], axis=0)


def row_weights(scalar_ref, own, slots, rows):
    row = lax.broadcasted_iota(jnp.int32, (rows, 1), 0)
    kept = (row < own + slots) & (row - own + scalar_ref[SLOT_START] < scalar_ref[COUNT])
    return jnp.where((row < own) | kept, scalar_ref[VALID], 0).astype(F32)


def project(tokens, mod_ref, weight_ref, line_ref):
    normed, unused = norm_parts(tokens.astype(F32))
    lowered = (normed * (1.0 + mod_ref[1:2, :]) + mod_ref[0:1, :]).astype(BF16)
    query = (mm(lowered, weight_ref[:, :D]) + line_ref[QV_LINE : QV_LINE + 1, :]).astype(BF16)
    scaled = (query.astype(F32) * (1.0 / math.sqrt(HDIM))).astype(BF16)
    keys = mm(lowered, weight_ref[:, D : 2 * D]).astype(BF16)
    values = (mm(lowered, weight_ref[:, 2 * D :]) + line_ref[QV_LINE + 1 : QV_LINE + 2, :]).astype(BF16)
    return lowered, scaled, keys, values


def head_cols(head):
    return slice(head * HDIM, (head + 1) * HDIM)


def ones_lanes(count):
    return (lax.broadcasted_iota(jnp.int32, (count, HDIM), 1) < 2).astype(F32).astype(BF16)


def bias_table(rel_ref):
    lane = lax.broadcasted_iota(jnp.int32, (GRID, 128), 1)
    parts = []
    for part in range(2):
        tiles = []
        for group in range(HEADS // 2):
            tile = jnp.zeros((GRID, 128), F32)
            for side in range(2):
                head = 2 * group + side
                line = rel_ref[head, part : part + 1, :].astype(F32)
                line = jnp.concatenate([line, jnp.zeros((1, 128 - line.shape[1]), F32)], axis=1)
                first = side * HDIM + part * GRID
                turned = pltpu.roll(
                    jnp.broadcast_to(line, (GRID, 128)), (first + 128 - (GRID - 1)) % 128, 1,
                    stride=1, stride_axis=0,
                )
                tile = jnp.where((lane >= first) & (lane < first + GRID), turned, tile)
            tiles.append(tile)
        parts.append(jnp.concatenate(tiles, axis=1))
    return jnp.concatenate(parts, axis=0).astype(BF16)


QV_LINE, OUT_LINE, FC1_LINE, FC2_LINE = 6, 8, 9, 13
COND_LINE = 6


def time_features(moment):
    half = D // 2
    lane = lax.broadcasted_iota(jnp.int32, (1, D), 1)
    number = jnp.where(lane < half, lane, lane - half).astype(F32)
    angle = moment.astype(F32) * jnp.exp(-math.log(10000.0) * number / half)
    return jnp.where(lane < half, jnp.cos(angle), jnp.sin(angle))


def own_kernel(
    start_ref, count_ref, valid_ref, moment_ref, label_ref,
    *refs,
):
    sources, outs, local, sems = refs[:11], refs[11:22], refs[22:33], refs[33]
    scalar_ref, kept_ref, line_ref, mod_ref, a_ref, qs_ref, qaug_ref, kaug_ref, vaug_ref = outs[:9]
    offset_ref, mask_ref = outs[9:]
    kept_in, rel_ref, ada_bias_ref, qv_bias_ref, out_bias_ref, fc1_bias_ref, fc2_bias_ref = local[:7]
    table_ref, ada_ref, tok_ref, weight_ref = local[7:]
    fetched = [pltpu.make_async_copy(*pair, sems.at[n]) for n, pair in enumerate(zip(sources, local))]
    for copy in fetched:
        copy.start()
    for copy in fetched[:7]:
        copy.wait()
    own = tok_ref.shape[0]
    slots = offset_ref.shape[0]
    total = mask_ref.shape[1]
    held = kept_ref.shape[0]
    label = label_ref[0]
    for n in range(scalar_ref.shape[0]):
        scalar_ref[n] = start_ref[n]
    scalar_ref[COUNT] = count_ref[0]
    scalar_ref[VALID] = valid_ref[0]
    scalar_ref[LABEL] = label
    width = round_up(held, 128)
    kept = jnp.concatenate([kept_in[...], jnp.zeros((1, width - kept_in.shape[1]), jnp.int32)], axis=1)
    kept_ref[...] = jnp.broadcast_to(kept, (8, width)).T[:held, :1]
    place = place_onehot(row_places(start_ref, kept_ref, own, slots))
    offsets = mm(place, bias_table(rel_ref)).astype(BF16)
    offset_ref[...] = offsets[own:]
    number = lax.broadcasted_iota(jnp.int32, (held, 1), 0)
    live = jnp.where(number < count_ref[0], kept_ref[...], -1)
    hit = live == lax.broadcasted_iota(jnp.int32, (held, total), 1)
    count = jnp.sum(hit.astype(F32), axis=0, keepdims=True)
    mask_ref[...] = jnp.broadcast_to(jnp.where(count > 0.0, 0.0, big_negative), mask_ref.shape)
    for n in range(6):
        line_ref[n : n + 1, :] = ada_bias_ref[pl.ds(n * D, D)].astype(F32).reshape(1, D)
    line_ref[QV_LINE : QV_LINE + 2, :] = qv_bias_ref[...].astype(F32)
    line_ref[OUT_LINE : OUT_LINE + 1, :] = out_bias_ref[...].astype(F32).reshape(1, D)
    for n in range(4):
        line_ref[FC1_LINE + n : FC1_LINE + n + 1, :] = fc1_bias_ref[pl.ds(n * D, D)].astype(F32).reshape(1, D)
    line_ref[FC2_LINE : FC2_LINE + 1, :] = fc2_bias_ref[...].astype(F32).reshape(1, D)
    line_ref[FC2_LINE + 1 :, :] = jnp.zeros((2, D), F32)
    for copy in fetched[7:]:
        copy.wait()
    hot = lax.broadcasted_iota(jnp.int32, (16, table_ref.shape[0]), 1) == label
    conditioned = mm(hot.astype(F32).astype(BF16), table_ref[...]) + time_features(moment_ref[0])
    gate = 1.0 / (1.0 + jnp.exp(-conditioned))
    activated = (conditioned * gate).astype(BF16)
    for n in range(6):
        mod_ref[n : n + 1, :] = mm(activated, ada_ref[:, n * D : (n + 1) * D])[:1] + line_ref[n : n + 1, :]
    mod_ref[COND_LINE : COND_LINE + 1, :] = conditioned[:1]
    mod_ref[COND_LINE + 1 :, :] = jnp.zeros((1, D), F32)
    lowered, scaled, keys, values = project(tok_ref[...], mod_ref, weight_ref, line_ref)
    a_ref[...] = lowered
    qs_ref[...] = scaled
    for head in range(HEADS):
        cols = head_cols(head)
        qaug_ref[head] = jnp.concatenate([scaled[:, cols], offsets[:own, cols]], axis=1)
        kaug_ref[head] = jnp.concatenate([keys[:, cols], place[:own]], axis=1)
        vaug_ref[head] = jnp.concatenate([values[:, cols], ones_lanes(own)], axis=1)


def prep_kernel(seq, scalar_ref, *refs):
    token_refs, refs = refs[:seq], refs[seq:]
    own_a_ref, own_qs_ref, own_qaug_ref, own_kaug_ref, own_vaug_ref, offset_ref = refs[:6]
    kept_ref, mod_ref, weight_ref, line_ref = refs[6:10]
    qaug_ref, kaug_ref, vaug_ref, x_ref, a_out, tok_out, slot_out = refs[10:17]
    qs_ref, a_ref, tok_ref, slot_ref, sems = refs[17:]
    copies = Copies(sems)
    own = token_refs[0].shape[0]
    slots, total = offset_ref.shape[0], tok_ref.shape[0]
    for n in range(seq):
        tok_ref[row_span(scalar_ref, STARTS + n, own), :] = token_refs[n][...]
    copies.start(tok_ref, tok_out)
    others = [token_refs[n][...] for n in range(1, seq)]
    others = others[0] if seq == 2 else jnp.concatenate(others, axis=0)
    lowered, scaled, keys, values = project(others, mod_ref, weight_ref, line_ref)
    here = row_span(scalar_ref, STARTS, own)
    a_ref[here, :] = own_a_ref[...]
    qs_ref[here, :] = own_qs_ref[...]
    for head in range(HEADS):
        kaug_ref[head, here, :] = own_kaug_ref[head]
        vaug_ref[head, here, :] = own_vaug_ref[head]
        qaug_ref[head, :own, :] = own_qaug_ref[head]
    for n in range(1, seq):
        there = row_span(scalar_ref, STARTS + n, own)
        span = slice((n - 1) * own, n * own)
        a_ref[there, :] = lowered[span]
        qs_ref[there, :] = scaled[span]
        place = place_onehot(lax.broadcasted_iota(jnp.int32, (own, 1), 0) + scalar_ref[STARTS + n])
        for head in range(HEADS):
            cols = head_cols(head)
            kaug_ref[head, there, :] = jnp.concatenate([keys[span, cols], place], axis=1)
            vaug_ref[head, there, :] = jnp.concatenate([values[span, cols], ones_lanes(own)], axis=1)
    copies.start(a_ref, a_out)
    chosen = slot_places(scalar_ref, kept_ref, slots) == lax.broadcasted_iota(jnp.int32, (slots, total), 1)
    chosen = chosen.astype(F32).astype(BF16)
    x_ref[:own, :] = token_refs[0][...]
    x_ref[own:, :] = mm(chosen, tok_ref[...]).astype(BF16)
    slot_ref[...] = mm(chosen, a_ref[...]).astype(BF16)
    copies.start(slot_ref, slot_out)
    query = mm(chosen, qs_ref[...]).astype(BF16)
    for head in range(HEADS):
        cols = head_cols(head)
        qaug_ref[head, own:, :] = jnp.concatenate([query[:, cols], offset_ref[:, cols]], axis=1)
    copies.wait()


def attend_kernel(
    own, qaug_ref, kaug_ref, vaug_ref, mask_ref, o_ref, inverse_ref, e_out, qaug_out, kaug_out, vaug_out, e_ref, sems
):
    rows = qaug_ref.shape[1]
    copies = Copies(sems)
    copies.start(qaug_ref, qaug_out)
    copies.start(kaug_ref, kaug_out)
    copies.start(vaug_ref, vaug_out)
    spans = [(at, size, False) for at, size in blocks_of(0, own, 512)]
    spans += [(at, size, True) for at, size in blocks_of(own, rows - own, 512)]
    items = [(side, *span) for side in range(2) for span in spans]

    def e_copy(head, n):
        side, at, size, masked = items[n]
        span = pl.ds(at, size)
        return pltpu.make_async_copy(
            e_ref.at[head, span], e_out.at[head, span], sems.at[3 + len(spans) * head + n % len(spans)]
        )

    def pair(group, carry):
        scores, spread = {}, {}
        for n in range(len(items) + 2):
            if n < len(items):
                side, at, size, masked = items[n]
                head = 2 * group + side
                scores[n] = mm_t(qaug_ref[head, at : at + size, :], kaug_ref[head])
                if masked:
                    scores[n] = scores[n] + mask_ref[0:1, :]
            if 0 <= n - 1 < len(items):
                side, at, size, masked = items[n - 1]
                found = scores.pop(n - 1)
                spread[n - 1] = jnp.exp(found - jnp.max(found, axis=-1, keepdims=True)).astype(BF16)
                e_ref[2 * group + side, at : at + size, :] = spread[n - 1]
                e_copy(2 * group + side, n - 1).start()
            if 0 <= n - 2:
                side, at, size, masked = items[n - 2]
                mixed = mm(spread.pop(n - 2), vaug_ref[2 * group + side])
                inverse = 1.0 / mixed[:, HDIM : HDIM + 1]
                lanes = slice(side * HDIM, (side + 1) * HDIM)
                o_ref[group, at : at + size, lanes] = mixed[:, :HDIM] * inverse
                inverse_ref[group, at : at + size, lanes] = jnp.broadcast_to(inverse, (size, HDIM))
        return carry

    lax.fori_loop(0, HEADS // 2, pair, 0)
    for head in range(HEADS):
        for n in range(len(spans)):
            e_copy(head, head % 2 * len(spans) + n).wait()
    copies.wait()


def cotangents(scalar_ref, slots, full_ref, slot_ref):
    own = full_ref.shape[0]
    weight = row_weights(scalar_ref, own, slots, own + slot_ref.shape[0])
    return weight, jnp.concatenate([full_ref[...], slot_ref[...]], axis=0).astype(F32) * weight


def feed_kernel(
    slots, scalar_ref, o_ref, x_ref, cot_full_ref, cot_slot_ref, mod_ref, wout_ref, w1_ref,
    w2_ref, line_ref,
    att_ref, hidden_ref, du_ref, bias_ref, keep_ref, send_ref, pay_ref, sems,
):
    rows = x_ref.shape[0]
    gate1, shift2, scale2, gate2 = [mod_ref[n : n + 1, :] for n in range(2, 6)]
    merged = jnp.concatenate([o_ref[n] for n in range(HEADS // 2)], axis=1).astype(BF16)
    attended = mm(merged, wout_ref[...]) + line_ref[OUT_LINE : OUT_LINE + 1, :]
    att_ref[...] = attended
    normed, unused = norm_parts(x_ref[...].astype(F32) + gate1 * attended)
    second = (normed * (1.0 + scale2) + shift2).astype(BF16)
    unused, cot = cotangents(scalar_ref, slots, cot_full_ref, cot_slot_ref)
    dz = (gate2 * cot).astype(BF16)

    bias = jnp.concatenate([line_ref[FC1_LINE + n : FC1_LINE + n + 1, :] for n in range(4)], axis=1)

    def products(c):
        cols = slice(c * CHUNK, (c + 1) * CHUNK)
        return mm(second, w1_ref[:, cols]) + bias[:, cols], mm_t(dz, w2_ref[cols, :])

    chunks = FF // CHUNK
    ready = products(0)
    for c in range(chunks):
        u, back_u = ready
        if c + 1 < chunks:
            ready = products(c + 1)
        cols = slice(c * CHUNK, (c + 1) * CHUNK)
        square = u * u
        t = jnp.tanh(u * (square * (GELU_A * GELU_B) + GELU_A))
        cdf = t * 0.5 + 0.5
        hidden_ref[:, cols] = (u * cdf).astype(BF16)
        slope = cdf * ((1.0 - t) * (u * (square * (3.0 * GELU_A * GELU_B) + GELU_A)) + 1.0)
        du_ref[:, cols] = (slope * back_u).astype(BF16)
    ones = jnp.ones((16, rows), BF16)
    grad = mm(jnp.concatenate([second.T, ones], axis=0), du_ref[...])
    heads = []
    for n in range(4):
        cols = slice(n * D, (n + 1) * D)
        pay_ref[0, cols, :] = grad[:D, cols].astype(BF16)
        heads.append(grad[D : D + 1, cols])
    heads += [jnp.sum(dz.astype(F32), axis=0, keepdims=True), jnp.zeros((3, D), F32)]
    bias_ref[...] = jnp.concatenate(heads, axis=0)
    pay_ref[1, :FF, :] = mm(hidden_ref[...].T, dz).astype(BF16)
    if pay_ref.shape[1] > FF:
        pay_ref[:, FF:, :] = jnp.zeros((2, pay_ref.shape[1] - FF, D), BF16)
    for which in range(2):
        half_copies(scalar_ref[SIDE], pay_ref, keep_ref, send_ref, sems, which)
    for which in range(2):
        pltpu.make_async_copy(pay_ref.at[which], keep_ref, sems.at[which]).wait()


def feed_rest_kernel(
    slots, scalar_ref, o_ref, inverse_ref, x_ref, cot_full_ref, cot_slot_ref, mod_ref, wout_ref, w1_ref,
    w2_ref, line_ref,
    att_ref, hidden_ref, du_ref, bias_ref,
    small_ref, y_full_out, y_slot_out, dm_out, x_out, do_out, go_out, y_ref, dm_ref, do_ref, go_ref, sems,
):
    rows, own = x_ref.shape[0], cot_full_ref.shape[0]
    copies = Copies(sems)
    copies.start(x_ref, x_out)
    gate1, shift2, scale2, gate2 = [mod_ref[n : n + 1, :] for n in range(2, 6)]
    weight, cot = cotangents(scalar_ref, slots, cot_full_ref, cot_slot_ref)
    back = mm_t(du_ref[...], w1_ref[...])
    branch = mm(hidden_ref[...], w2_ref[...]) + line_ref[FC2_LINE : FC2_LINE + 1, :]
    attended = att_ref[...]
    middle = x_ref[...].astype(F32) + gate1 * attended
    normed, inverse = norm_parts(middle)
    y_ref[...] = ((middle + gate2 * branch) * weight).astype(BF16)
    copies.start(y_ref.at[pl.ds(0, own)], y_full_out)
    copies.start(y_ref.at[pl.ds(own, rows - own)], y_slot_out)
    dmid = cot + norm_back(normed, inverse, back * (1.0 + scale2))
    dm_ref[...] = dmid
    copies.start(dm_ref, dm_out)
    datt = (gate1 * dmid).astype(BF16)
    merged_f = jnp.concatenate([o_ref[n] for n in range(HEADS // 2)], axis=1)
    dout = mm_t(datt, wout_ref[...]) * jnp.concatenate([inverse_ref[n] for n in range(HEADS // 2)], axis=1)
    dout = dout.astype(BF16).astype(F32)
    product = dout * merged_f
    high = product.astype(BF16)
    low = (product - high.astype(F32)).astype(BF16)
    row = lax.broadcasted_iota(jnp.int32, (D, 128), 0)
    lane = lax.broadcasted_iota(jnp.int32, (D, 128), 1)
    heads = jnp.where(row // HDIM == lane // 2, -1.0, 0.0).astype(BF16)
    less = mm(high, heads) + mm(low, heads)
    lane = lax.broadcasted_iota(jnp.int32, (rows, 128), 1)
    kept = less.astype(BF16).astype(F32)
    pair = jnp.where(lane % 2 == 0, kept, less - kept)
    for head in range(HEADS):
        tile = dout[:, head // 2 * 128 : (head // 2 + 1) * 128]
        if head % 2:
            tile = pltpu.roll(tile, HDIM, 1)
        more = pltpu.roll(pair, HDIM - 2 * head, 1)
        more = jnp.where(lane < HDIM + 2, more, 0.0)
        do_ref[head] = jnp.where(lane < HDIM, tile, more).astype(BF16)
    copies.start(do_ref, do_out)
    go_ref[...] = mm(merged_f.astype(BF16).T, datt).astype(BF16)
    copies.start(go_ref, go_out)
    column = lambda value: jnp.sum(value.astype(F32), axis=0, keepdims=True)
    sums = [dmid * attended, back, back * normed, cot * branch, datt]
    sums = [column(value) for value in sums] + [bias_ref[:5, :], jnp.zeros((6, D), F32)]
    small_ref[...] = jnp.concatenate(sums, axis=0)
    copies.wait()


def attend_back(own, e_ref, q_ref, k_ref, v_ref, do_ref, place_ref, outs, sums):
    dq_ref, dk_ref, dv_ref, tab_ref = outs
    dkt_ref, dvt_ref, part_ref = sums
    rows = q_ref.shape[1]
    spans = blocks_of(0, own, 256) + blocks_of(own, rows - own, 256)
    items = [(side, *span) for side in range(2) for span in spans]
    grads, found = {}, {}
    for n in range(len(items) + 2):
        if n < len(items):
            side, at, size = items[n]
            grads[n] = mm_t(do_ref[side, at : at + size, :], v_ref[side])
        if 0 <= n - 1 < len(items):
            side, at, size = items[n - 1]
            found[n - 1] = (e_ref[side, at : at + size, :].astype(F32) * grads.pop(n - 1)).astype(BF16)
        if 0 <= n - 2:
            side, at, size = items[n - 2]
            lanes = slice(side * HDIM, (side + 1) * HDIM)
            ds = found.pop(n - 2)
            dq = mm(ds, k_ref[side])
            dq_ref[at : at + size, lanes] = (dq[:, :HDIM] * (1.0 / math.sqrt(HDIM))).astype(BF16)
            part_ref[at : at + size, lanes] = dq[:, HDIM:].astype(BF16)
            dkt = mm(q_ref[side, at : at + size, :HDIM].T, ds)
            dvt = mm(do_ref[side, at : at + size, :HDIM].T, e_ref[side, at : at + size, :])
            if at == 0:
                dkt_ref[lanes, :] = dkt
                dvt_ref[lanes, :] = dvt
            else:
                dkt_ref[lanes, :] += dkt
                dvt_ref[lanes, :] += dvt
    tab_ref[...] = mm(place_ref[...], part_ref[...])
    dk_ref[...] = dkt_ref[...].astype(BF16).T
    dv_ref[...] = dvt_ref[...].astype(BF16).T


def back_kernel(own, everyone, scalar_ref, kept_ref, mod_ref, prior_ref, *refs):
    group_sources, refs = refs[:5], refs[5:]
    sources, refs = refs[:7], refs[7:]
    keep_ref, send_ref, dx_out, dx_own_out, refs = *refs[:4], refs[4:]
    group_local, refs = refs[:5], refs[5:]
    local, refs = refs[:7], refs[7:]
    dq_ref, dk_ref, dv_ref, tab_ref, normed_ref, inverse_ref, dxs_ref, dkt_ref, dvt_ref, pay_ref = refs[:10]
    place_ref, part_ref, dx_ref, dx_own_ref, group_sems, sems, pay_sems = refs[10:]
    tok_ref, a_ref, x_ref, slot_ref, weight_ref, dm_ref, go_ref = local
    step = pl.program_id(0)
    last = pl.num_programs(0) - 1
    slot = step % 2

    def fetches(group, place):
        return [
            pltpu.make_async_copy(source.at[pl.ds(2 * group, 2)], target.at[place], group_sems.at[place, n])
            for n, (source, target) in enumerate(zip(group_sources, group_local))
        ]

    def copies():
        return [
            pltpu.make_async_copy(source, target, sems.at[n])
            for n, (source, target) in enumerate(zip(sources, local))
        ]

    @pl.when(step == 0)
    def first():
        whole = copies()
        whole[0].start()
        for copy in fetches(0, 0):
            copy.start()
        for copy in whole[1:]:
            copy.start()
        for copy in fetches(1, 1):
            copy.start()
        slots = x_ref.shape[0] - own
        place_ref[...] = place_onehot(row_places(scalar_ref, kept_ref, own, slots), turned=True).T
        whole[0].wait()
        normed, inverse = norm_parts(tok_ref[...].astype(F32))
        normed_ref[...] = normed
        inverse_ref[...] = jnp.broadcast_to(inverse, inverse_ref.shape)

    @pl.when((step > 0) & (step + 1 < last))
    def following():
        for copy in fetches(step + 1, 1 - slot):
            copy.start()

    @pl.when(step < last)
    def attention():
        for copy in fetches(step, slot):
            copy.wait()
        outs = dq_ref.at[step], dk_ref.at[step], dv_ref.at[step], tab_ref.at[step]
        attend_back(own, *[ref.at[slot] for ref in group_local], place_ref, outs, (dkt_ref, dvt_ref, part_ref))

    @pl.when(step == last)
    def projections():
        for copy in copies()[1:]:
            copy.wait()
        groups = dq_ref.shape[0]
        total = tok_ref.shape[0]
        rows = x_ref.shape[0]
        slots = rows - own
        scale = mod_ref[1:2, :]
        here = row_span(scalar_ref, STARTS, own)

        def joined(ref, span):
            return jnp.concatenate([ref[n, span, :] for n in range(groups)], axis=1)

        every = slice(0, total)
        dk, dv = joined(dk_ref, every), joined(dv_ref, every)
        dq_own, dq_slot = joined(dq_ref, slice(0, own)), joined(dq_ref, slice(own, rows))
        column = lambda value: jnp.sum(value.astype(F32), axis=0, keepdims=True)
        lowered_t = a_ref[...].T
        pay_ref[0:D, :] = (mm(a_ref[here, :].T, dq_own) + mm(slot_ref[...].T, dq_slot)).astype(BF16)
        pay_ref[D : 2 * D, :] = mm(lowered_t, dk).astype(BF16)
        pay_ref[2 * D : 3 * D, :] = mm(lowered_t, dv).astype(BF16)
        pay_ref[3 * D : 4 * D, :] = go_ref[...]
        slot_normed, slot_inverse = norm_parts(x_ref[own:, :].astype(F32))
        da = mm_t(dq_slot, weight_ref[:, :D])
        shift_sum, scale_sum = column(da), column(da * slot_normed)
        spread = dm_ref[own:, :] + norm_back(slot_normed, slot_inverse, da * (1.0 + scale))
        chosen = slot_places(scalar_ref, kept_ref, slots) == lax.broadcasted_iota(jnp.int32, (slots, total), 1)
        chosen = chosen.astype(F32)
        moved = mm(chosen.astype(BF16).T, spread.astype(BF16))
        dxs_ref[...] = mm_t(dk, weight_ref[:, D : 2 * D]) + mm_t(dv, weight_ref[:, 2 * D :])
        dxs_ref[here, :] += mm_t(dq_own, weight_ref[:, :D])
        da = dxs_ref[...]
        normed = normed_ref[...]
        shift_sum, scale_sum = shift_sum + column(da), scale_sum + column(da * normed)
        inverse = jnp.concatenate([inverse_ref[...]] * (D // 128), axis=1)
        dxs_ref[...] = moved + norm_back(normed, inverse, da * (1.0 + scale))
        dx_own_ref[...] = dxs_ref[here, :] + dm_ref[:own, :]
        others = dx_ref.shape[0]
        for n in range(others):
            dx_ref[n] = dxs_ref[row_span(scalar_ref, STARTS + 1 + others + n, own), :].astype(BF16)
        halves = Copies(pay_sems)
        halves.start(dx_own_ref, dx_own_out)
        halves.start(dx_ref, dx_out)
        half = keep_ref.shape[0]

        def part(which):
            return pay_ref.at[pl.ds(which * half, half)]

        def hand_over(which):
            for target, chosen in ((keep_ref, scalar_ref[SIDE] == which), (send_ref, scalar_ref[SIDE] != which)):

                @pl.when(chosen)
                def start():
                    pltpu.make_async_copy(part(which), target, pay_sems.at[2 + which]).start()

        if half <= 4 * D:
            hand_over(0)
        rel = table_sums([tab_ref[n] for n in range(groups)])
        first = jnp.where(scalar_ref[SEQ_PLACE] == 0, 1, 0)
        label = scalar_ref[LABEL]
        number = lax.broadcasted_iota(jnp.int32, (1, D), 1)
        digits = jnp.where(number == scalar_ref[PLACE], label // GRID * first, 0)
        digits = jnp.where(number == 128 + scalar_ref[PLACE], label % GRID * first, digits).astype(F32)
        smalls = jnp.concatenate(
            [
                shift_sum, scale_sum, prior_ref[0:4, :], column(dq_own) + column(dq_slot), column(dv),
                *rel, prior_ref[4:5, :], digits, prior_ref[5:10, :], mod_ref[COND_LINE : COND_LINE + 1, :],
                jnp.zeros((14, D), F32),
            ],
            axis=0,
        ).astype(BF16)
        tail = pay_ref.shape[0] - 4 * D
        row = lax.broadcasted_iota(jnp.int32, (tail, 32), 0)
        lane = lax.broadcasted_iota(jnp.int32, (tail, 32), 1)
        kind = jnp.where(row < 6 * everyone, row // everyone, jnp.where(scalar_ref[SEQ_PLACE] == 0, 17, -1))
        wanted = jnp.where(row % everyone == scalar_ref[PLACE], kind, -1)
        after = row - 7 * everyone
        wanted = jnp.where(after < 0, wanted, jnp.where(after < 11, after + 6, -1))
        pay_ref[4 * D :, :] = mm((lane == wanted).astype(F32).astype(BF16), smalls).astype(BF16)
        if half > 4 * D:
            hand_over(0)
        hand_over(1)
        for which in range(2):
            pltpu.make_async_copy(part(which), keep_ref, pay_sems.at[2 + which]).wait()
        halves.wait()


def table_sums(tabs):
    found = ([], [])
    for tab in tabs:
        for side in range(2):
            for part in range(2):
                at = 2 * side * GRID + part * GRID
                square = tab[part * GRID : (part + 1) * GRID, at : at + GRID]
                wide = jnp.concatenate([square, jnp.zeros((GRID, 128 - GRID), F32)], axis=1)
                turned = pltpu.roll(wide, 0, 1, stride=1, stride_axis=0)
                found[part].append(jnp.sum(turned, axis=0, keepdims=True)[:, : 2 * GRID])
    return [jnp.concatenate(parts, axis=1) for parts in found]


def call(kernel, outs, scratch, args, scalars=0, far=0, away=0, copies=0, micros=1, limit=32):
    scratches = [pltpu.VMEM(shape, dtype) for shape, dtype in scratch]
    if copies:
        scratches.append(pltpu.SemaphoreType.DMA((copies,)))
    return pl.pallas_call(
        kernel,
        out_shape=[jax.ShapeDtypeStruct(shape, dtype) for shape, dtype in outs[: len(outs) - away]]
        + [pltpu.HBM(shape, dtype) for shape, dtype in outs[len(outs) - away :]],
        in_specs=[smem] * scalars + [vmem] * (len(args) - scalars - far) + [hbm] * far,
        out_specs=[vmem] * (len(outs) - away) + [hbm] * away,
        scratch_shapes=scratches,
        compiler_params=pltpu.CompilerParams(vmem_limit_bytes=limit * MIB),
        cost_estimate=pl.CostEstimate(flops=micros * 10**9, bytes_accessed=MIB, transcendentals=0),
    )(*args)


def own_call(outs, scalars, sources):
    return pl.pallas_call(
        own_kernel,
        out_shape=[jax.ShapeDtypeStruct(shape, dtype) for shape, dtype in outs],
        in_specs=[smem] * len(scalars) + [hbm] * len(sources),
        out_specs=[smem] + [vmem] * (len(outs) - 1),
        scratch_shapes=[pltpu.VMEM(value.shape, value.dtype) for value in sources]
        + [pltpu.SemaphoreType.DMA((len(sources),))],
        compiler_params=pltpu.CompilerParams(vmem_limit_bytes=16 * MIB),
        cost_estimate=pl.CostEstimate(flops=3 * 10**9, bytes_accessed=MIB, transcendentals=0),
    )(*scalars, *map(in_hbm, sources))


def in_hbm(value):
    return pltpu.with_memory_space_constraint(value, pltpu.HBM)


def add_kernel(pieces, left_ref, right_ref, sum_out, sum_ref, sems):
    copies = Copies(sems)
    rows = sum_ref.shape[0] // pieces
    for n in range(pieces):
        span = pl.ds(n * rows, rows)
        sum_ref[span, :] = (left_ref[span, :].astype(F32) + right_ref[span, :].astype(F32)).astype(BF16)
        copies.start(sum_ref.at[span], sum_out.at[span])
    copies.wait()


def add_call(left, right, micros):
    pieces = 4 if left.shape[0] % 64 == 0 else 1
    out = (left.shape, BF16)
    return call(
        functools.partial(add_kernel, pieces), [out], [out], [left, right], away=1, copies=pieces, micros=micros,
        limit=8,
    )[0]


def spread_kernel(near_ref, far_ref, wide_out, sum_ref, sems):
    sum_ref[...] = (near_ref[...].astype(F32) + far_ref[...].astype(F32)).astype(BF16)
    copies = Copies(sems)
    for n in range(wide_out.shape[0]):
        copies.start(sum_ref, wide_out.at[n])
    copies.wait()


def spread_call(near, far, peers):
    return call(
        spread_kernel, [((peers,) + near.shape, BF16)], [(near.shape, BF16)], [near, far], away=1, copies=peers,
        limit=8,
    )[0]


def back_call(own, everyone, groups_of, sources, scalars, kept, mod, prior, tail_half):
    rows, total = groups_of[1].shape[1], groups_of[2].shape[1]
    groups = HEADS // 2
    others = total // own - 1
    whole = lambda shape: pl.BlockSpec(shape, lambda n: (0,) * len(shape))
    outs = [((tail_half, D), BF16), ((tail_half, D), BF16), ((others, own, D), BF16), ((own, D), F32)]
    scratch = [((2, 2) + value.shape[1:], value.dtype) for value in groups_of]
    scratch += [(value.shape, value.dtype) for value in sources]
    scratch += [
        ((groups, rows, 128), BF16), ((groups, total, 128), BF16), ((groups, total, 128), BF16),
        ((groups, 2 * GRID, 128), F32), ((total, D), F32), ((total, 128), F32), ((total, D), F32),
        ((128, total), F32), ((128, total), F32), ((2 * tail_half, D), BF16),
        ((2 * GRID, rows), BF16), ((rows, 128), BF16), outs[2], outs[3],
    ]
    small = [kept, mod, prior]
    return pl.pallas_call(
        functools.partial(back_kernel, own, everyone),
        grid=(groups + 1,),
        out_shape=[jax.ShapeDtypeStruct(shape, dtype) for shape, dtype in outs[:2]]
        + [pltpu.HBM(shape, dtype) for shape, dtype in outs[2:]],
        in_specs=[smem] + [whole(value.shape) for value in small] + [hbm] * (len(groups_of) + len(sources)),
        out_specs=[vmem, vmem, hbm, hbm],
        scratch_shapes=[pltpu.VMEM(shape, dtype) for shape, dtype in scratch]
        + [pltpu.SemaphoreType.DMA((2, 5)), pltpu.SemaphoreType.DMA((7,)), pltpu.SemaphoreType.DMA((4,))],
        compiler_params=pltpu.CompilerParams(
            vmem_limit_bytes=48 * MIB, dimension_semantics=("arbitrary",)
        ),
        cost_estimate=pl.CostEstimate(flops=18 * 10**9, bytes_accessed=MIB, transcendentals=0),
    )(scalars, *small, *map(in_hbm, groups_of), *map(in_hbm, sources))


def halves_reader(side_ref, mine_ref, other_ref):
    half = mine_ref.shape[0]

    def get(at, count):
        found = []
        for which in range(2):
            first, last = max(at, which * half), min(at + count, (which + 1) * half)
            if first < last:
                span = slice(first - which * half, last - which * half)
                found.append(jnp.where(side_ref[0] == which, mine_ref[span, :], other_ref[span, :]))
        return found[0] if len(found) == 1 else jnp.concatenate(found, axis=0)

    return get


def widen_half(core, half_ref, g1_out, g2_out, wide_ref, sems):
    for which in range(2):

        @pl.when(core == which)
        def widen():
            copies = Copies(sems)
            for n in range(4):
                rows = pl.ds(n * D, D)
                wide_ref[rows, :] = half_ref[rows, :].astype(F32)
                copies.start(wide_ref.at[rows], g2_out.at[rows] if which else g1_out.at[:, rows])
            copies.wait()


def near_half_kernel(side_ref, half_ref, g1_out, g2_out, wide_ref, sems):
    widen_half(side_ref[0], half_ref, g1_out, g2_out, wide_ref, sems)


def far_half_kernel(side_ref, half_ref, g1_in, g2_in, g1_out, g2_out, wide_ref, sems):
    widen_half(1 - side_ref[0], half_ref, g1_out, g2_out, wide_ref, sems)


def widen_near(sides, layer_half):
    return pl.pallas_call(
        near_half_kernel,
        out_shape=[pltpu.HBM((D, FF), F32), pltpu.HBM((FF, D), F32)],
        in_specs=[smem, vmem],
        out_specs=[hbm, hbm],
        scratch_shapes=[pltpu.VMEM((FF, D), F32), pltpu.SemaphoreType.DMA((4,))],
        compiler_params=pltpu.CompilerParams(vmem_limit_bytes=8 * MIB),
        cost_estimate=pl.CostEstimate(flops=10**9, bytes_accessed=MIB, transcendentals=0),
    )(sides, layer_half)


def widen_far(sides, other, first):
    return pl.pallas_call(
        far_half_kernel,
        out_shape=[pltpu.HBM((D, FF), F32), pltpu.HBM((FF, D), F32)],
        in_specs=[smem, vmem, hbm, hbm],
        out_specs=[hbm, hbm],
        input_output_aliases={2: 0, 3: 1},
        scratch_shapes=[pltpu.VMEM((FF, D), F32), pltpu.SemaphoreType.DMA((4,))],
        compiler_params=pltpu.CompilerParams(vmem_limit_bytes=8 * MIB),
        cost_estimate=pl.CostEstimate(flops=10**9, bytes_accessed=MIB, transcendentals=0),
    )(sides, other, *map(in_hbm, first))


def last_kernel(
    everyone, side_ref, mine_ref, other_ref, ada_in, qv_ref, rel_ref, out_bias_ref, ada_bias_ref, bias1_ref,
    bias2_ref, gqkv_out, gada_out, table_out, go_out, gqkv_ref, gada_ref, table_ref, go_ref, ada_ref, sems,
):
    get = halves_reader(side_ref, mine_ref, other_ref)
    copies = Copies(sems)
    copies.start(ada_in, ada_ref)
    for n in range(3):
        cols = pl.ds(n * D, D)
        gqkv_ref[:, cols] = get(n * D, D).astype(F32)
        copies.start(gqkv_ref.at[:, cols], gqkv_out.at[:, cols])
    go_ref[...] = get(3 * D, D).astype(F32)
    copies.start(go_ref, go_out)
    cond = get(4 * D + 6 * everyone, everyone).astype(F32)
    gate = 1.0 / (1.0 + jnp.exp(-cond))
    act_t = (cond * gate).astype(BF16).T
    dmods = [get(4 * D + n * everyone, everyone) for n in range(6)]
    small = get(4 * D + 7 * everyone, 16).astype(F32)

    def ada():
        for n in range(6):
            cols = pl.ds(n * D, D)
            gada_ref[:, cols] = mm(act_t, dmods[n])
            copies.start(gada_ref.at[:, cols], gada_out.at[:, cols])
            ada_bias_ref[cols] = jnp.sum(dmods[n].astype(F32), axis=0)

    def table():
        copies.made.pop(0).wait()
        back = jnp.zeros((everyone, D), F32)
        for n in range(6):
            back = back + mm_t(dmods[n], ada_ref[:, n * D : (n + 1) * D])
        back = gate * (1.0 + cond * (1.0 - gate)) * back
        high = back.astype(BF16)
        low = (back - high.astype(F32)).astype(BF16)
        label = (small[5:6, :everyone] * GRID + small[5:6, 128 : 128 + everyone]).astype(jnp.int32)
        classes = table_ref.shape[0]
        wide = round_up(classes, 128)
        hot = (label == lax.broadcasted_iota(jnp.int32, (wide, everyone), 0)).astype(F32).astype(BF16)
        table_ref[...] = (mm(hot, high) + mm(hot, low))[:classes]
        copies.start(table_ref, table_out)

    ada()
    table()
    qv_ref[...] = small[:2]
    for part in range(2):
        for head in range(HEADS):
            at = 2 * GRID * head
            rel_ref[head, part : part + 1, :] = small[2 + part : 3 + part, at : at + 2 * GRID - 1]
    out_bias_ref[...] = small[4]
    for n in range(4):
        bias1_ref[pl.ds(n * D, D)] = small[6 + n]
    bias2_ref[...] = small[10]
    copies.wait()


def swap_cores(value, dp):
    return lax.ppermute(value, "dp", [(n, n ^ 1) for n in range(dp)])


def exchange(value, dp, seq):
    groups = [
        [(far * (dp // 2) + 2 * pair + core) * seq + at for pair in range(dp // 4) for at in range(seq)]
        for far in range(2)
        for core in range(2)
    ]
    return lax.all_to_all(value, AXES, 0, 0, axis_index_groups=groups)


def near_sum(pieces):
    return jnp.sum(pieces.astype(F32), axis=0).astype(BF16)


def far_half(near, dp):
    return lax.ppermute(near, "dp", [(n, (n + dp // 2) % dp) for n in range(dp)])


def assemble_kernel(cut, place_ref, pair_ref, a1_ref, b1_ref, a2_ref, b2_ref, half_ref):
    rows = pair_ref.shape[1]
    for near in range(2):
        for x in range(2):
            for y in range(2):
                at = (place_ref[0] ^ (4 * near + 2 * x + y)) * rows
                if x:
                    half_ref[pl.ds(pl.multiple_of(at, 16), cut), :] = a2_ref[y, near]
                elif y:
                    half_ref[pl.ds(pl.multiple_of(at, 16), cut), :] = a1_ref[near]
                else:
                    half_ref[pl.ds(pl.multiple_of(at, 16), cut), :] = pair_ref[near, :cut, :]
                rest = pl.ds(pl.multiple_of(at + cut, 16), rows - cut)
                if y:
                    half_ref[rest, :] = b2_ref[x, near]
                elif x:
                    half_ref[rest, :] = b1_ref[near]
                else:
                    half_ref[rest, :] = pair_ref[near, cut:, :]


def after(value, *others):
    return lax.optimization_barrier((value, *others))[0]


def gather_chunks(chunk, last_near, before, between, finish, dp, seq):
    rows = chunk.shape[0]
    cut = round_up(rows // 2, 16)
    place = lax.axis_index("dp") % (dp // 2) // 2 * seq + lax.axis_index("seq")
    along_x = lambda value: lax.ppermute(value, "dp", [(n, n ^ 2) for n in range(dp)])
    along_y = lambda value: lax.ppermute(value, "seq", [(n, n ^ 1) for n in range(seq)])
    chunk = after(chunk, last_near, before)
    last_wide = finish(last_near)
    pair = jnp.stack([chunk, lax.ppermute(chunk, "dp", [(n, n ^ 4) for n in range(dp)])])
    pair = after(pair, between)
    a, b = pair[:, :cut], pair[:, cut:]
    a1, b1 = along_y(a), along_x(b)
    a, b = jnp.stack([a, a1]), jnp.stack([b, b1])
    a, b = after((a, b), last_wide)
    a2, b2 = along_x(a), along_y(b)
    held = (a2, b2)

    def assemble(a2, b2):
        return call(
            functools.partial(assemble_kernel, cut), [((8 * rows, D), BF16)], [],
            [place.astype(jnp.int32).reshape(1), pair, a1, b1, a2, b2], scalars=1, limit=8,
        )[0]

    return (a2, b2), assemble, last_wide, held


def scatter_rows(partial, seq):
    return [
        lax.ppermute(partial[step - 1], "seq", [(n, (n + step) % seq) for n in range(seq)])
        for step in range(1, seq)
    ]


def body(
    dp, seq, image_tokens, kept_index, kept_count, sample_valid, timestep, class_label, class_table,
    ada_weight, ada_bias, qkv_weight, qv_bias, rel_bias, out_weight, out_bias, fc1_weight,
    fc1_bias, fc2_weight, fc2_bias, grad_full, grad_masked,
):
    samples, own, width = image_tokens.shape
    held = kept_index.shape[1]
    slots = grad_masked.shape[1]
    padded = round_up(slots, 16)
    rows = own + padded
    total = own * seq
    everyone = dp * samples
    classes = class_table.shape[0]
    dp_place, seq_place = lax.axis_index("dp"), lax.axis_index("seq")

    half = round_up(FF, dp * seq * 4)
    peers = dp // 4 * seq
    side = dp_place % 2
    sides = side.astype(jnp.int32).reshape(1)
    tail_half = round_up(4 * D + 16 + 7 * everyone, dp * seq * 4) // 2
    kept_of = []
    for s in range(samples):
        tokens = [image_tokens[s]]
        for step in range(1, seq):
            tokens.append(lax.ppermute(tokens[0], "seq", [(n, (n + step) % seq) for n in range(seq)]))
        number = jnp.arange(STARTS + 2 * seq - 1, dtype=jnp.int32)
        block = number - STARTS
        scalars = jnp.where(block < seq, seq_place - block, seq_place + block - seq + 1) % seq * own
        entries = {
            SIDE: side, PLACE: dp_place * samples + s, SLOT_START: seq_place * slots, SEQ_PLACE: seq_place,
        }
        for at, entry in entries.items():
            scalars = jnp.where(number == at, entry, scalars)
        places = scalars.astype(jnp.int32)
        held_rows = held + padded - slots
        cot_slot = jnp.pad(grad_masked[s], ((0, padded - slots), (0, 0)))
        one = slice(s, s + 1)
        scalars, kept, lines, mod, *owned, mask = own_call(
            [
                (places.shape, jnp.int32), ((held_rows, 1), jnp.int32), ((16, D), F32),
                ((8, D), F32), ((own, D), BF16), ((own, D), BF16), ((HEADS, own, 128), BF16),
                ((HEADS, own, 128), BF16), ((HEADS, own, 128), BF16), ((padded, D), BF16), ((8, total), F32),
            ],
            [places, kept_count[one], sample_valid[one], timestep[one], class_label[one]],
            [
                kept_index[one], rel_bias.transpose(1, 0, 2), ada_bias, qv_bias, out_bias, fc1_bias, fc2_bias,
                class_table, ada_weight, tokens[0], qkv_weight,
            ],
        )
        qaug, kaug, vaug, x, lowered, whole, slot = call(
            functools.partial(prep_kernel, seq),
            [
                ((HEADS, rows, 128), BF16), ((HEADS, total, 128), BF16), ((HEADS, total, 128), BF16),
                ((rows, D), BF16), ((total, D), BF16), ((total, D), BF16), ((padded, D), BF16),
            ],
            [((total, D), BF16), ((total, D), BF16), ((total, D), BF16), ((padded, D), BF16)],
            [scalars, *tokens, *owned, kept, mod, qkv_weight, lines],
            scalars=1, away=3, copies=3, micros=3, limit=16,
        )
        mixed, inverse, spread_far, qaug_far, kaug_far, vaug_far = call(
            functools.partial(attend_kernel, own),
            [
                ((HEADS // 2, rows, 128), F32), ((HEADS // 2, rows, 128), F32),
                ((HEADS, rows, total), BF16), (qaug.shape, BF16), (kaug.shape, BF16), (vaug.shape, BF16),
            ],
            [((HEADS, rows, total), BF16)],
            [qaug, kaug, vaug, mask],
            away=4, copies=3 + 8 * HEADS, micros=10, limit=32,
        )
        attended, hidden, du, biases, keep, send = call(
            functools.partial(feed_kernel, slots),
            [
                ((rows, D), F32), ((rows, FF), BF16), ((rows, FF), BF16), ((8, D), F32), ((half, D), BF16),
                ((half, D), BF16),
            ],
            [((2, half, D), BF16)],
            [
                scalars, mixed, x, grad_full[s], cot_slot, mod, out_weight, fc1_weight, fc2_weight, lines,
            ],
            scalars=1, copies=2, micros=10, limit=24,
        )
        kept_of.append(dict(
            rest=[
                scalars, mixed, inverse, x, grad_full[s], cot_slot, mod, out_weight, fc1_weight, fc2_weight,
                lines, attended, hidden, du, biases,
            ],
            groups=[spread_far, qaug_far, kaug_far, vaug_far], sources=[whole, lowered, slot, qkv_weight],
            small=[scalars, kept, mod], keep=keep, send=send,
        ))

    def added(arrays):
        if len(arrays) == 1:
            return arrays[0]
        return functools.reduce(jnp.add, [a.astype(F32) for a in arrays]).astype(arrays[0].dtype)

    keep, send = added([k["keep"] for k in kept_of]), added([k["send"] for k in kept_of])
    got = swap_cores(send, dp)

    rests = [
        call(
            functools.partial(feed_rest_kernel, slots),
            [
                ((16, D), F32), ((own, D), BF16), ((padded, D), BF16), ((rows, D), F32), ((rows, D), BF16),
                ((HEADS, rows, 128), BF16), ((D, D), BF16),
            ],
            [((rows, D), BF16), ((rows, D), F32), ((HEADS, rows, 128), BF16), ((D, D), BF16)],
            k["rest"],
            scalars=1, away=6, copies=6, micros=6, limit=24,
        )
        for k in kept_of
    ]
    mine = add_call(keep, got, 1)
    mine, rests = lax.optimization_barrier((mine, rests))
    pieces = exchange(mine.reshape(peers, half // peers, D), dp, seq)
    tails = []
    for k, rest in zip(kept_of, rests):
        small, unused_full, unused_slot, dmid, x_far, dout_far, grad_out = rest
        whole, lowered, slot, weights = k["sources"]
        tails.append(
            back_call(
                own, everyone, [*k["groups"], dout_far], [whole, lowered, x_far, slot, weights, dmid, grad_out],
                *k["small"], small, tail_half,
            )
        )

    keep, send = added([t[0] for t in tails]), added([t[1] for t in tails])
    keep, send, pieces = lax.optimization_barrier((keep, send, pieces))
    got = swap_cores(send, dp)
    mine = add_call(keep, got, 1).reshape(peers, tail_half // peers, D)
    pieces, mine = lax.optimization_barrier((pieces, mine))
    near = near_sum(pieces)
    far = far_half(near, dp)
    first_moved = [scatter_rows(t[2][:, : own // 2], seq) for t in tails]
    last_near = near_sum(exchange(mine, dp, seq))
    last_moved = [scatter_rows(after(t[2][:, own // 2 :], last_near), seq) for t in tails]

    def finish(last_near):
        wide = spread_call(last_near, far_half(last_near, dp), peers)
        return wide

    if dp == 16 and seq == 2:
        chunk = (near.astype(F32) + far.astype(F32)).astype(BF16)
        parts, assemble, last_wide, held = gather_chunks(chunk, last_near, first_moved, last_moved, finish, dp, seq)
    else:
        parts = exchange(spread_call(near, far, peers), dp, seq).reshape(half, D)
        assemble = lambda whole: whole
        parts = (parts,)
        held = parts
        last_wide = finish(last_near)
    last_half = exchange(last_wide, dp, seq).reshape(tail_half, D)
    out_full = jnp.stack([rest[1] for rest in rests])
    out_masked = jnp.stack([rest[2][:slots] for rest in rests])
    layer_half = assemble(*parts)
    other = swap_cores(layer_half, dp)
    first = widen_near(sides, layer_half)
    grad_input = []
    for tail, *moved in zip(tails, first_moved, last_moved):
        came = [jnp.concatenate(both).astype(F32) for both in zip(*moved)]
        grad_input.append(functools.reduce(jnp.add, came, tail[3]))
    grad_input = jnp.stack(grad_input)
    last_half = after(last_half, layer_half, grad_input)
    grad_fc1, grad_fc2 = widen_far(sides, other, first)
    found = call(
        functools.partial(last_kernel, everyone),
        [
            ((2, D), F32), ((HEADS, 2, 2 * GRID - 1), F32), ((D,), F32), ((6 * D,), F32), ((FF,), F32), ((D,), F32),
            ((D, 3 * D), F32), ((D, 6 * D), F32), ((classes, D), F32), ((D, D), F32),
        ],
        [((D, 3 * D), F32), ((D, 6 * D), F32), ((classes, D), F32), ((D, D), F32), (ada_weight.shape, BF16)],
        [sides, last_half, swap_cores(last_half, dp), in_hbm(ada_weight)],
        scalars=1, far=1, away=4, copies=12, micros=4, limit=16,
    )
    grad_qv, grad_rel, grad_out_bias, grad_ada_bias, grad_fc1_bias, grad_fc2_bias = found[:6]
    grad_qkv, grad_ada, grad_table, grad_out = found[6:]
    grad_rel = grad_rel.transpose(1, 0, 2)
    return (
        out_full, out_masked, grad_input, grad_table, grad_ada, grad_ada_bias, grad_qkv, grad_qv,
        grad_rel, grad_out, grad_out_bias, grad_fc1, grad_fc1_bias, grad_fc2, grad_fc2_bias,
    )


def solution(mesh):
    split = P("dp", "seq", None)
    placed = (split, P("dp", None)) + (P("dp"),) * 4 + (P(),) * 12 + (split, split)
    return jax.shard_map(
        functools.partial(body, mesh.shape["dp"], mesh.shape["seq"]),
        mesh=mesh,
        in_specs=placed,
        out_specs=(split,) * 3 + (P(),) * 12,
        check_vma=False,
    )
```
